32 devices in a mesh: mode: 4 (over z), rows: 8 (over y, x, core).
Axes of the slice: x: 2, y: 2, z: 4, core: 2. Of those that a mesh axis runs over, the one named last changes fastest.
Arguments:
- object_real: float32 [8, 2048, 2048], P('mode', 'rows'), may hold values from -6 to 6
- object_imag: float32 [8, 2048, 2048], P('mode', 'rows'), may hold values from -6 to 6
- pupil_real: float32 [1024, 1024], P('rows'), may hold values from -0.7 to 0.7
- pupil_imag: float32 [1024, 1024], P('rows'), may hold values from -0.7 to 0.7
- measured: float32 [1, 1024, 1024], P(None, 'rows'), may hold values from 1 to 5
- source_mask: int32 [1, 3], replicated, may hold values from 0 to 1, as said below
- offsets: int32 [3, 2], replicated, may hold values from 0 to 1024
Outputs:
- updated_real: float32 [8, 2048, 2048], P('mode', 'rows')
- updated_imag: float32 [8, 2048, 2048], P('mode', 'rows')
The draws below stay inside these ranges and needn't reach their ends.
Inputs may be any that keep to these rules, and one draw needn't show every extreme that they name: `source_mask`: every frame has at least one LED lit and at least one dark.
All inputs are finite; a program needn't handle non-finite values.
Results may differ from the reference program's by a relative error of at most 0.0003.
Values sent between devices are 32-bit elements; how exact they have to be, the bound alone decides.
No kernel may reach another device: no remote copies, remote signals or barrier semaphores. Data moves between devices by JAX's collectives and lax.ppermute only.
A program may use at most 128 MiB of HBM per device.

```python
import jax
import jax.numpy as jnp
from jax import lax

K = 2048
N = 1024
LEDS = 3
FRAMES = 1
MODES = 8


def draw_source_mask(key, part):
    key_bits = jax.random.fold_in(key, 11)
    key_lit = jax.random.fold_in(key, 12)
    key_dark = jax.random.fold_in(key, 13)
    bits = jax.random.randint(key_bits, (FRAMES, LEDS), 0, 2)
    lit_pick = jax.random.randint(key_lit, (FRAMES,), 0, LEDS)
    dark_step = jax.random.randint(key_dark, (FRAMES,), 1, LEDS)
    dark_pick = (lit_pick + dark_step) % LEDS
    columns = jnp.arange(LEDS, dtype=jnp.int32)[None, :]
    forced_on = (columns == lit_pick[:, None]).astype(jnp.int32)
    forced_off = (columns == dark_pick[:, None]).astype(jnp.int32)
    return (jnp.maximum(bits, forced_on) * (1 - forced_off)).astype(jnp.int32)


def plant(array, own_key, least, top_value):
    dims = array.shape
    index_at = [jax.random.randint(jax.random.fold_in(own_key, axis), (), 0, dims[axis]) for axis in range(len(dims))]
    array = array.at[tuple(index_at)].set(least)
    longest = dims.index(max(dims))
    index_at[longest] = (index_at[longest] + 1) % dims[longest]
    return array.at[tuple(index_at)].set(top_value)


def level_of(key, dims, cuts, smallest, largest):
    def one(position, shards_of):
        draws = jax.random.uniform(jax.random.fold_in(jax.random.fold_in(key, 6), position), (shards_of,), jnp.float32, smallest / len(cuts), largest / len(cuts))
        return jnp.repeat(jnp.exp(draws), dims[position] // shards_of).reshape((-1,) + (1,) * (len(dims) - position - 1))

    loudness = one(*cuts[0])
    for cut in cuts[1:]:
        loudness = loudness * one(*cut)
    return loudness


def scatter_about(key, extent, scale, limit, pieces=(), kind=jnp.bfloat16):
    drawn = jax.random.normal(key, extent, jnp.float32) * scale
    if len(pieces) > 0:
        drawn = level_of(key, extent, pieces, -0.22, 0.18) * drawn
    return jnp.clip(drawn, min=-limit, max=limit).astype(kind)


def setup_inputs(seed: int = 0) -> dict:
    key_list = jax.random.split(jax.random.key(seed), 8)
    object_real = scatter_about(key_list[0], (MODES, K, K), 1.0, 6.0, ((0, 4), (1, 8)), jnp.float32)
    object_imag = scatter_about(key_list[1], (MODES, K, K), 1.0, 6.0, ((0, 4), (1, 8)), jnp.float32)
    pupil_real = jnp.clip(jax.random.uniform(key_list[2], (N, N), jnp.float32, -0.7, 0.7) * level_of(key_list[2], (N, N), ((0, 8),), -0.4, 0.0), -0.7, 0.7)
    pupil_imag = jnp.clip(jax.random.uniform(key_list[3], (N, N), jnp.float32, -0.7, 0.7) * level_of(key_list[3], (N, N), ((0, 8),), -0.4, 0.0), -0.7, 0.7)
    measured = jnp.clip(1.0 + 4.0 * jax.random.uniform(key_list[4], (FRAMES, N, N), jnp.float32) ** level_of(key_list[4], (FRAMES, N, N), ((1, 8),), -0.2, 0.2), 1.0, 5.0)
    source_mask = draw_source_mask(jax.random.fold_in(key_list[7], 71), 0)
    offsets = plant(jax.random.randint(key_list[6], (LEDS, 2), 0, K - N + 1), jax.random.fold_in(key_list[6], 1), 0, K - N).astype(jnp.int32)
    return dict(object_real=object_real, object_imag=object_imag, pupil_real=pupil_real, pupil_imag=pupil_imag, measured=measured, source_mask=source_mask, offsets=offsets)


FLOOR_TERM = 0.5

def reference(object_real, object_imag, pupil_real, pupil_imag, measured, source_mask, offsets):
    spectrum = object_real + 1j * object_imag
    pupil_full = jnp.transpose(pupil_real + 1j * pupil_imag)
    weights = source_mask.astype(object_real.dtype)
    anchor = jnp.zeros((), jnp.int32)
    for frame_index in range(FRAMES):
        fields = []
        intensity = jnp.zeros((N, N), object_real.dtype)
        for source_index in range(LEDS):
            start_row = offsets[source_index, 0].astype(jnp.int32)
            start_col = offsets[source_index, 1].astype(jnp.int32)
            window = lax.dynamic_slice(spectrum, (anchor, start_row, start_col), (MODES, N, N))
            wave_field = jnp.fft.ifft2(pupil_full * window, axes=(1, 2), norm='ortho')
            fields.append(wave_field)
            powers = lax.optimization_barrier(jnp.sum(jnp.real(wave_field) ** 2 + jnp.imag(wave_field) ** 2, axis=0))
            intensity = intensity + weights[frame_index, source_index] * powers
        ratios = measured[frame_index] / jnp.sqrt(intensity + FLOOR_TERM)
        for source_index in range(LEDS):
            start_row = offsets[source_index, 0].astype(jnp.int32)
            start_col = offsets[source_index, 1].astype(jnp.int32)
            change = jnp.fft.fft2(weights[frame_index, source_index] * fields[source_index] * (ratios - 1.0), axes=(1, 2), norm='ortho')
            window = lax.dynamic_slice(spectrum, (anchor, start_row, start_col), (MODES, N, N))
            spectrum = lax.dynamic_update_slice(spectrum, window + jnp.conj(pupil_full) * change, (anchor, start_row, start_col))
    return (jnp.real(spectrum), jnp.imag(spectrum))
```

```python
import functools
import math

import jax
import jax.numpy as jnp
import ml_dtypes
import numpy as np
from jax import lax
from jax.experimental import pallas as pl
from jax.experimental.pallas import tpu as pltpu
from jax.sharding import PartitionSpec as P

FLOOR_TERM = 0.5
HIGHEST_PREC = lax.Precision.HIGHEST


def dft_tables(length):
    indices = jnp.arange(length, dtype=jnp.int32)
    phases = indices[:, None] * indices[None, :] % length
    angles = phases.astype(jnp.float32) * (2.0 * math.pi / length)
    scale_factor = 1.0 / math.sqrt(length)
    cos_table = jnp.cos(angles) * scale_factor
    sin_table = jnp.sin(angles) * scale_factor
    return (
        jnp.concatenate([cos_table, sin_table], axis=1),
        jnp.concatenate([cos_table, sin_table], axis=0),
    )


def transform(form, table, real_part, imag_part, axis, direction_sign):
    result = jnp.einsum(form, jnp.stack([real_part, imag_part]), table, precision=HIGHEST_PREC)
    length = result.shape[axis] // 2
    with_cos = lax.slice_in_dim(result, 0, length, axis=axis)
    with_sin = lax.slice_in_dim(result, length, 2 * length, axis=axis)
    return (with_cos[0] - direction_sign * with_sin[1], with_cos[1] + direction_sign * with_sin[0])


def right_product(real_part, imag_part, wide_cols, direction_sign):
    return transform("smlck,kj->smlcj", wide_cols, real_part, imag_part, 4, direction_sign)


def forward_fields(
    part_real, part_imag, pupil_real, pupil_imag, offsets, wide_cols, wide_rows, length
):
    source_count = offsets.shape[0]
    groups = lax.axis_size("rows")
    crop_real = jnp.stack(
        [
            lax.dynamic_slice_in_dim(part_real, offsets[source_index, 1], length, 2)
            for source_index in range(source_count)
        ],
        axis=1,
    )
    crop_imag = jnp.stack(
        [
            lax.dynamic_slice_in_dim(part_imag, offsets[source_index, 1], length, 2)
            for source_index in range(source_count)
        ],
        axis=1,
    )
    got_real, got_imag = (
        lax.all_to_all(
            jnp.swapaxes(crop_real, 2, 3), "rows", split_axis=2, concat_axis=3, tiled=True
        ),
        lax.all_to_all(
            jnp.swapaxes(crop_imag, 2, 3), "rows", split_axis=2, concat_axis=3, tiled=True
        ),
    )
    win_real = jnp.stack(
        [
            lax.dynamic_slice_in_dim(got_real[:, source_index], offsets[source_index, 0], length, 2)
            for source_index in range(source_count)
        ],
        axis=1,
    )
    win_imag = jnp.stack(
        [
            lax.dynamic_slice_in_dim(got_imag[:, source_index], offsets[source_index, 0], length, 2)
            for source_index in range(source_count)
        ],
        axis=1,
    )
    lifted_real = pupil_real * win_real - pupil_imag * win_imag
    lifted_imag = pupil_real * win_imag + pupil_imag * win_real
    half_real, half_imag = transform("smlcr,yr->smlyc", wide_rows, lifted_real, lifted_imag, 3, 1.0)
    layout = half_real.shape
    blocked = (layout[0], layout[1], groups, layout[2] // groups, layout[3])
    back_real, back_imag = (
        lax.all_to_all(half_real.reshape(blocked), "rows", split_axis=2, concat_axis=4, tiled=True),
        lax.all_to_all(half_imag.reshape(blocked), "rows", split_axis=2, concat_axis=4, tiled=True),
    )
    flat = (layout[0], layout[1], layout[2] // groups, layout[3] * groups)
    return right_product(back_real.reshape(flat), back_imag.reshape(flat), wide_cols, 1.0)


def spectral_updates(diff_real, diff_imag, pupil_real, pupil_imag, offsets, wide_cols, size_k):
    source_count = offsets.shape[0]
    groups = lax.axis_size("rows")
    col_real, col_imag = right_product(diff_real, diff_imag, wide_cols, -1.0)
    layout = col_real.shape
    blocked = (layout[0], layout[1], layout[2], groups, layout[3] // groups)
    got_real, got_imag = (
        lax.all_to_all(col_real.reshape(blocked), "rows", split_axis=3, concat_axis=2, tiled=True),
        lax.all_to_all(col_imag.reshape(blocked), "rows", split_axis=3, concat_axis=2, tiled=True),
    )
    flat = (layout[0], layout[1], layout[2] * groups, layout[3] // groups)
    full_real = got_real.reshape(flat)
    full_imag = got_imag.reshape(flat)
    delta_real, delta_imag = transform("smlyc,yk->smlck", wide_cols, full_real, full_imag, 4, -1.0)
    upd_real = pupil_real * delta_real + pupil_imag * delta_imag
    upd_imag = pupil_real * delta_imag - pupil_imag * delta_real
    blank = jnp.zeros((layout[0], layout[3] // groups, size_k), jnp.float32)
    placed_real = jnp.stack(
        [
            lax.dynamic_update_slice_in_dim(
                blank, upd_real[:, source_index], offsets[source_index, 0], 2
            )
            for source_index in range(source_count)
        ],
        axis=1,
    )
    placed_imag = jnp.stack(
        [
            lax.dynamic_update_slice_in_dim(
                blank, upd_imag[:, source_index], offsets[source_index, 0], 2
            )
            for source_index in range(source_count)
        ],
        axis=1,
    )
    return (
        lax.all_to_all(placed_real, "rows", split_axis=3, concat_axis=2, tiled=True),
        lax.all_to_all(placed_imag, "rows", split_axis=3, concat_axis=2, tiled=True),
    )


def add_window(target, incoming, start_col, length):
    current = lax.dynamic_slice_in_dim(target, start_col, length, 2)
    return lax.dynamic_update_slice_in_dim(
        target, current + jnp.swapaxes(incoming, 1, 2), start_col, 2
    )


def body(object_real, object_imag, pupil_real, pupil_imag, measured, source_mask, offsets):
    length = pupil_real.shape[1]
    size_k = object_real.shape[2]
    source_count = offsets.shape[0]
    wide_cols, wide_rows = dft_tables(length)
    spec_real, spec_imag = (object_real, object_imag)
    weights = source_mask[0].astype(jnp.float32)
    field_real, field_imag = forward_fields(
        spec_real, spec_imag, pupil_real, pupil_imag, offsets, wide_cols, wide_rows, length
    )
    powers = jnp.sum(field_real * field_real + field_imag * field_imag, axis=0)
    partial_sum = jnp.tensordot(weights, powers, axes=1)
    share = lax.psum_scatter(partial_sum, "mode", scatter_dimension=0, tiled=True)
    share_rows = share.shape[0]
    measured_share = lax.dynamic_slice_in_dim(
        measured[0], lax.axis_index("mode") * share_rows, share_rows, 0
    )
    ratio_share = measured_share / jnp.sqrt(share + FLOOR_TERM)
    ratios = lax.all_gather(ratio_share, "mode", axis=0, tiled=True)
    factor = (ratios - 1.0)[None, None] * weights[None, :, None, None]
    diff_real = field_real * factor
    diff_imag = field_imag * factor
    ret_real, ret_imag = spectral_updates(
        diff_real, diff_imag, pupil_real, pupil_imag, offsets, wide_cols, size_k
    )
    for source_index in range(source_count):
        start_col = offsets[source_index, 1]
        spec_real = add_window(spec_real, ret_real[:, source_index], start_col, length)
        spec_imag = add_window(spec_imag, ret_imag[:, source_index], start_col, length)
    return (spec_real, spec_imag)


RADIX = 4
VMEM_LIMIT = 56 * 1024 * 1024


def split_pair(table):
    high = table.astype(ml_dtypes.bfloat16)
    low = (table - high.astype(np.float64)).astype(ml_dtypes.bfloat16)
    return np.stack([high, low])


def radix_tables(length):
    part = length // RADIX
    t = np.arange(RADIX)[:, None, None]
    r = np.arange(part)[None, :, None]
    s = np.arange(part)[None, None, :]
    angles = (r * (t + RADIX * s) % length) * (2.0 * np.pi / length)
    cos_t = np.cos(angles) / np.sqrt(length)
    sin_t = np.sin(angles) / np.sqrt(length)
    swap = lambda x: np.swapaxes(x, 1, 2)
    return (
        split_pair(np.concatenate([cos_t, sin_t], axis=2)),
        split_pair(np.concatenate([swap(cos_t), swap(sin_t)], axis=1)),
        split_pair(np.concatenate([cos_t, sin_t], axis=1)),
        split_pair(np.concatenate([swap(cos_t), swap(sin_t)], axis=2)),
    )


def halves(x):
    high = x.astype(jnp.bfloat16)
    low = (x - high.astype(jnp.float32)).astype(jnp.bfloat16)
    return high, low


def dot(a, b):
    return jnp.dot(a, b, preferred_element_type=jnp.float32)


def dot_right(x, table_ref, t):
    high, low = halves(x)
    return dot(high, table_ref[0, t]) + dot(low, table_ref[0, t]) + dot(high, table_ref[1, t])


def dot_left(table_ref, t, x):
    high, low = halves(x)
    return dot(table_ref[0, t], high) + dot(table_ref[0, t], low) + dot(table_ref[1, t], high)


def butterfly(reals, imags, sign):
    sum_r, sum_i = reals[0] + reals[2], imags[0] + imags[2]
    dif_r, dif_i = reals[0] - reals[2], imags[0] - imags[2]
    odd_r, odd_i = reals[1] + reals[3], imags[1] + imags[3]
    rot_r = sign * (imags[3] - imags[1])
    rot_i = sign * (reals[1] - reals[3])
    return (
        [sum_r + odd_r, dif_r + rot_r, sum_r - odd_r, dif_r - rot_r],
        [sum_i + odd_i, dif_i + rot_i, sum_i - odd_i, dif_i - rot_i],
    )


def lit_offsets(mask_ref, offsets_ref, nth):
    row, col, seen = jnp.int32(0), jnp.int32(0), jnp.int32(0)
    for led in range(offsets_ref.shape[0]):
        lit = mask_ref[0, led] != 0
        take = jnp.logical_and(lit, seen == nth)
        row = jnp.where(take, offsets_ref[led, 0], row)
        col = jnp.where(take, offsets_ref[led, 1], col)
        seen = seen + lit.astype(jnp.int32)
    return row, col


def pupil_send_kernel(nth, mask_ref, offsets_ref, real_ref, imag_ref, out_ref):
    row, _ = lit_offsets(mask_ref, offsets_ref, nth)
    length = real_ref.shape[1]
    part = length // RADIX
    for index, ref in enumerate((real_ref, imag_ref)):
        rolled = pltpu.roll(ref[...], lax.rem(row, length), 1)
        for q in range(RADIX):
            block = rolled[:, q * part : (q + 1) * part].T
            out_ref[q, index] = block
            out_ref[q + RADIX, index] = block


def window_pupil(nth, mask_ref, offsets_ref, place_ref, pupil_ref, row_base):
    row, col = lit_offsets(mask_ref, offsets_ref, nth)
    blocks, _, rows, width = pupil_ref.shape
    length = blocks * width
    upper, first = place_ref[0], place_ref[1]
    position = first + row_base + lax.broadcasted_iota(jnp.int32, (rows, length), 0)
    owned = (position < row).astype(jnp.int32) == upper
    parts = []
    for index in range(2):
        whole = jnp.concatenate([pupil_ref[d, index] for d in range(blocks)], axis=1)
        whole = pltpu.roll(whole, lax.rem(col, length), 1)
        parts.append(jnp.where(owned, whole, 0.0))
    wrapped = lax.broadcasted_iota(jnp.int32, (rows, length), 1) < col
    return parts[0], parts[1], wrapped


def columns_kernel(
    nth, mask_ref, offsets_ref, place_ref, real_ref, imag_ref, pupil_ref, table_ref, out_ref
):
    rows, size_k = real_ref.shape[1:]
    length = size_k // 2
    part = length // RADIX
    base = pl.program_id(0) * rows
    p_r, p_i, wrapped = window_pupil(nth, mask_ref, offsets_ref, place_ref, pupil_ref, base)
    w_r = jnp.where(wrapped, real_ref[0, :, length:], real_ref[0, :, :length])
    w_i = jnp.where(wrapped, imag_ref[0, :, length:], imag_ref[0, :, :length])
    x_r = p_r * w_r - p_i * w_i
    x_i = p_r * w_i + p_i * w_r
    cut = lambda x: [x[:, q * part : (q + 1) * part] for q in range(RADIX)]
    y_r, y_i = butterfly(cut(x_r), cut(x_i), 1.0)
    half = part // 2
    for t in range(RADIX):
        both = dot_right(jnp.concatenate([y_r[t], y_i[t]], axis=0), table_ref, t)
        z_r = both[:rows, :part] - both[rows:, part:]
        z_i = both[:rows, part:] + both[rows:, :part]
        for side in range(2):
            out_ref[2 * t + side, 0] = z_r[:, side * half : (side + 1) * half]
            out_ref[2 * t + side, 1] = z_i[:, side * half : (side + 1) * half]


def rows_kernel(has_total, *refs):
    if has_total:
        got_ref, table_ref, before_ref, field_ref, total_ref = refs
    else:
        got_ref, table_ref, field_ref, total_ref = refs
    width = got_ref.shape[3]
    x_r = [got_ref[q, 0] + got_ref[q + RADIX, 0] for q in range(RADIX)]
    x_i = [got_ref[q, 1] + got_ref[q + RADIX, 1] for q in range(RADIX)]
    y_r, y_i = butterfly(x_r, x_i, 1.0)
    for t in range(RADIX):
        both = dot_left(table_ref, t, jnp.concatenate([y_r[t], y_i[t]], axis=1))
        part = both.shape[0] // 2
        z_r = both[:part, :width] - both[part:, width:]
        z_i = both[:part, width:] + both[part:, :width]
        field_ref[0, t] = z_r
        field_ref[1, t] = z_i
        power = z_r * z_r + z_i * z_i
        total_ref[t] = before_ref[t] + power if has_total else power


def rows_back_kernel(field_ref, factor_ref, table_ref, out_ref):
    width = field_ref.shape[3]
    u_r, u_i = [], []
    for t in range(RADIX):
        factor = factor_ref[t]
        diff = jnp.concatenate([field_ref[0, t] * factor, field_ref[1, t] * factor], axis=1)
        both = dot_left(table_ref, t, diff)
        part = both.shape[0] // 2
        u_r.append(both[:part, :width] + both[part:, width:])
        u_i.append(both[:part, width:] - both[part:, :width])
    x_r, x_i = butterfly(u_r, u_i, -1.0)
    for q in range(RADIX):
        for side in range(2):
            out_ref[q + side * RADIX, 0] = x_r[q]
            out_ref[q + side * RADIX, 1] = x_i[q]


def columns_back_kernel(
    nth, mask_ref, offsets_ref, place_ref, real_ref, imag_ref, pupil_ref, got_ref, table_ref, *outs
):
    out_r, out_i = outs[-2:]
    rows, size_k = real_ref.shape[1:]
    length = size_k // 2
    base = pl.program_id(0) * rows
    p_r, p_i, wrapped = window_pupil(nth, mask_ref, offsets_ref, place_ref, pupil_ref, base)
    u_r, u_i = [], []
    for t in range(RADIX):
        z_r = jnp.concatenate([got_ref[2 * t, 0], got_ref[2 * t + 1, 0]], axis=1)
        z_i = jnp.concatenate([got_ref[2 * t, 1], got_ref[2 * t + 1, 1]], axis=1)
        both = dot_right(jnp.concatenate([z_r, z_i], axis=0), table_ref, t)
        part = both.shape[1] // 2
        u_r.append(both[:rows, :part] + both[rows:, part:])
        u_i.append(both[rows:, :part] - both[:rows, part:])
    x_r, x_i = butterfly(u_r, u_i, -1.0)
    x_r, x_i = jnp.concatenate(x_r, axis=1), jnp.concatenate(x_i, axis=1)
    d_r = p_r * x_r + p_i * x_i
    d_i = p_r * x_i - p_i * x_r
    for ref, out, delta in ((real_ref, out_r, d_r), (imag_ref, out_i, d_i)):
        out[0, :, :length] = ref[0, :, :length] + jnp.where(wrapped, 0.0, delta)
        out[0, :, length:] = ref[0, :, length:] + jnp.where(wrapped, delta, 0.0)


SMEM_SPEC = pl.BlockSpec(memory_space=pltpu.SMEM)
PARAMS = pltpu.CompilerParams(vmem_limit_bytes=VMEM_LIMIT)


def fixed(shape):
    zeros = (0,) * len(shape)
    return pl.BlockSpec(shape, lambda *_: zeros)


def cost(macs, *arrays):
    moved = sum(math.prod(a.shape) * a.dtype.itemsize for a in arrays)
    return pl.CostEstimate(flops=2 * macs, bytes_accessed=moved, transcendentals=0)


def shaped(shape):
    return jax.ShapeDtypeStruct(shape, jnp.float32)


def exchange(blocks):
    return lax.all_to_all(blocks, "rows", split_axis=0, concat_axis=0, tiled=True)


def fast_body(object_real, object_imag, pupil_real, pupil_imag, measured, source_mask, offsets):
    width, length = pupil_real.shape
    modes, local_rows, size_k = object_real.shape
    groups = lax.axis_size("rows")
    part = length // RADIX
    leds = offsets.shape[0]
    tables = [jnp.asarray(table) for table in radix_tables(length)]
    place = lax.axis_index("rows")
    position = jnp.stack([place // RADIX, place % RADIX * local_rows]).astype(jnp.int32)
    tile = local_rows // 2
    block_shape = (groups, 2, local_rows, width)
    dft_macs = 3 * RADIX * 4 * part * part
    scalars = [SMEM_SPEC] * 3
    rows_of_mode = lambda mode: pl.BlockSpec((1, tile, size_k), lambda i: (mode, i, 0))
    tall = pl.BlockSpec((groups, 2, tile, width), lambda i: (0, 0, i, 0))

    def pupil_for(nth):
        out = shaped(block_shape)
        return exchange(
            pl.pallas_call(
                functools.partial(pupil_send_kernel, nth),
                out_shape=out,
                in_specs=[SMEM_SPEC] * 2 + [fixed(pupil_real.shape)] * 2,
                out_specs=fixed(block_shape),
                compiler_params=PARAMS,
                cost_estimate=cost(0, out, pupil_real, pupil_imag),
                name="pupil_send",
            )(source_mask, offsets, pupil_real, pupil_imag)
        )

    def columns(nth, mode, pupil):
        out = shaped(block_shape)
        return exchange(
            pl.pallas_call(
                functools.partial(columns_kernel, nth),
                out_shape=out,
                grid=(local_rows // tile,),
                in_specs=scalars + [rows_of_mode(mode)] * 2 + [tall, fixed(tables[0].shape)],
                out_specs=tall,
                compiler_params=PARAMS,
                cost_estimate=cost(local_rows * dft_macs, out, out, out, out),
                name="columns",
            )(source_mask, offsets, position, object_real, object_imag, pupil, tables[0])
        )

    def rows(got, total):
        field = shaped((2, RADIX, part, width))
        power = shaped((RADIX, part, width))
        before = [] if total is None else [total]
        return pl.pallas_call(
            functools.partial(rows_kernel, bool(before)),
            out_shape=(field, power),
            in_specs=[fixed(got.shape), fixed(tables[1].shape)] + [fixed(b.shape) for b in before],
            out_specs=(fixed(field.shape), fixed(power.shape)),
            compiler_params=PARAMS,
            cost_estimate=cost(width * dft_macs, got, field, power),
            name="rows",
        )(got, tables[1], *before)

    def rows_back(field, factor):
        out = shaped(block_shape)
        return exchange(
            pl.pallas_call(
                rows_back_kernel,
                out_shape=out,
                in_specs=[fixed(field.shape), fixed(factor.shape), fixed(tables[2].shape)],
                out_specs=fixed(block_shape),
                compiler_params=PARAMS,
                cost_estimate=cost(width * dft_macs, out, field, factor),
                name="rows_back",
            )(field, factor, tables[2])
        )

    def columns_back(nth, mode, pupil, got, current, written):
        operands = [source_mask, offsets, position, *current, pupil, got, tables[3]]
        specs = scalars + [rows_of_mode(mode)] * 2 + [tall, tall, fixed(tables[3].shape)]
        if written is None:
            aliases = {}
        elif written is current:
            aliases = {3: 0, 4: 1}
        else:
            aliases = {len(operands): 0, len(operands) + 1: 1}
            operands += written
            specs += [pl.BlockSpec(memory_space=pl.ANY)] * 2
        out = shaped(object_real.shape)
        return pl.pallas_call(
            functools.partial(columns_back_kernel, nth),
            out_shape=(out, out),
            grid=(local_rows // tile,),
            in_specs=specs,
            out_specs=(rows_of_mode(mode), rows_of_mode(mode)),
            input_output_aliases=aliases,
            compiler_params=PARAMS,
            cost_estimate=cost(local_rows * dft_macs, got, got, got, got),
            name="columns_back",
        )(*operands)

    def measured_share():
        level = lax.axis_index("mode")
        mine = lax.dynamic_index_in_dim(
            measured[0].reshape(width // RADIX, RADIX, length), level, 1, keepdims=False
        )
        sent = jnp.transpose(mine.reshape(width // RADIX, part, RADIX), (2, 1, 0))
        sent = jnp.swapaxes(sent.reshape(groups, width, width // RADIX), 1, 2)
        return exchange(sent).reshape(1, part, width)

    def update(count):
        def run(*_):
            pupils = [pupil_for(nth) for nth in range(count)]
            got = {}
            for nth in range(count):
                for mode in range(modes):
                    got[nth, mode] = columns(nth, mode, pupils[nth])
            amplitude = measured_share()
            total, fields = None, {}
            for key, blocks in got.items():
                fields[key], total = rows(blocks, total)
            share = lax.psum_scatter(total, "mode", scatter_dimension=0, tiled=True)
            ratio = amplitude / jnp.sqrt(share + FLOOR_TERM) - 1.0
            factor = lax.all_gather(ratio, "mode", axis=0, tiled=True)
            back = {key: rows_back(field, factor) for key, field in fields.items()}
            current, written = (object_real, object_imag), None
            for nth in range(count):
                for mode in range(modes):
                    written = columns_back(
                        nth, mode, pupils[nth], back[nth, mode], current, written
                    )
                    if nth > 0:
                        current = written
                current = written
            return tuple(written)

        return run

    lit = jnp.sum((source_mask[0] != 0).astype(jnp.int32))
    most = max(leds - 1, 1)
    if most == 1:
        return update(1)()
    return lax.switch(jnp.clip(lit - 1, 0, most - 1), [update(n + 1) for n in range(most)])


def fits_fast(mesh, object_shape, pupil_shape):
    groups, levels = mesh.shape["rows"], mesh.shape["mode"]
    length, size_k = pupil_shape[1], object_shape[2]
    local_rows = size_k // groups
    return (
        size_k == 2 * length
        and groups == 2 * RADIX
        and levels == RADIX
        and local_rows % 256 == 0
        and (length // groups) % 128 == 0
    )


def solution(mesh):
    in_specs = (
        P("mode", "rows", None),
        P("mode", "rows", None),
        P("rows", None),
        P("rows", None),
        P(None, "rows", None),
        P(),
        P(),
    )
    out_specs = (P("mode", "rows", None), P("mode", "rows", None))

    def chosen(object_real, object_imag, pupil_real, *others):
        fast = fits_fast(mesh, object_real.shape, pupil_real.shape)
        mapped = jax.shard_map(
            fast_body if fast else body,
            mesh=mesh,
            in_specs=in_specs,
            out_specs=out_specs,
            check_vma=False,
        )
        return mapped(object_real, object_imag, pupil_real, *others)

    return chosen
```

```python
import functools
import math

import jax
import jax.numpy as jnp
import ml_dtypes
import numpy as np
from jax import lax
from jax.experimental import pallas as pl
from jax.experimental.pallas import tpu as pltpu
from jax.sharding import PartitionSpec as P

FLOOR_TERM = 0.5
HIGHEST_PREC = lax.Precision.HIGHEST


def dft_tables(length):
    indices = jnp.arange(length, dtype=jnp.int32)
    phases = indices[:, None] * indices[None, :] % length
    angles = phases.astype(jnp.float32) * (2.0 * math.pi / length)
    scale_factor = 1.0 / math.sqrt(length)
    cos_table = jnp.cos(angles) * scale_factor
    sin_table = jnp.sin(angles) * scale_factor
    return (
        jnp.concatenate([cos_table, sin_table], axis=1),
        jnp.concatenate([cos_table, sin_table], axis=0),
    )


def transform(form, table, real_part, imag_part, axis, direction_sign):
    result = jnp.einsum(form, jnp.stack([real_part, imag_part]), table, precision=HIGHEST_PREC)
    length = result.shape[axis] // 2
    with_cos = lax.slice_in_dim(result, 0, length, axis=axis)
    with_sin = lax.slice_in_dim(result, length, 2 * length, axis=axis)
    return (with_cos[0] - direction_sign * with_sin[1], with_cos[1] + direction_sign * with_sin[0])


def right_product(real_part, imag_part, wide_cols, direction_sign):
    return transform("smlck,kj->smlcj", wide_cols, real_part, imag_part, 4, direction_sign)


def forward_fields(
    part_real, part_imag, pupil_real, pupil_imag, offsets, wide_cols, wide_rows, length
):
    source_count = offsets.shape[0]
    groups = lax.axis_size("rows")
    crop_real = jnp.stack(
        [
            lax.dynamic_slice_in_dim(part_real, offsets[source_index, 1], length, 2)
            for source_index in range(source_count)
        ],
        axis=1,
    )
    crop_imag = jnp.stack(
        [
            lax.dynamic_slice_in_dim(part_imag, offsets[source_index, 1], length, 2)
            for source_index in range(source_count)
        ],
        axis=1,
    )
    got_real, got_imag = (
        lax.all_to_all(
            jnp.swapaxes(crop_real, 2, 3), "rows", split_axis=2, concat_axis=3, tiled=True
        ),
        lax.all_to_all(
            jnp.swapaxes(crop_imag, 2, 3), "rows", split_axis=2, concat_axis=3, tiled=True
        ),
    )
    win_real = jnp.stack(
        [
            lax.dynamic_slice_in_dim(got_real[:, source_index], offsets[source_index, 0], length, 2)
            for source_index in range(source_count)
        ],
        axis=1,
    )
    win_imag = jnp.stack(
        [
            lax.dynamic_slice_in_dim(got_imag[:, source_index], offsets[source_index, 0], length, 2)
            for source_index in range(source_count)
        ],
        axis=1,
    )
    lifted_real = pupil_real * win_real - pupil_imag * win_imag
    lifted_imag = pupil_real * win_imag + pupil_imag * win_real
    half_real, half_imag = transform("smlcr,yr->smlyc", wide_rows, lifted_real, lifted_imag, 3, 1.0)
    layout = half_real.shape
    blocked = (layout[0], layout[1], groups, layout[2] // groups, layout[3])
    back_real, back_imag = (
        lax.all_to_all(half_real.reshape(blocked), "rows", split_axis=2, concat_axis=4, tiled=True),
        lax.all_to_all(half_imag.reshape(blocked), "rows", split_axis=2, concat_axis=4, tiled=True),
    )
    flat = (layout[0], layout[1], layout[2] // groups, layout[3] * groups)
    return right_product(back_real.reshape(flat), back_imag.reshape(flat), wide_cols, 1.0)


def spectral_updates(diff_real, diff_imag, pupil_real, pupil_imag, offsets, wide_cols, size_k):
    source_count = offsets.shape[0]
    groups = lax.axis_size("rows")
    col_real, col_imag = right_product(diff_real, diff_imag, wide_cols, -1.0)
    layout = col_real.shape
    blocked = (layout[0], layout[1], layout[2], groups, layout[3] // groups)
    got_real, got_imag = (
        lax.all_to_all(col_real.reshape(blocked), "rows", split_axis=3, concat_axis=2, tiled=True),
        lax.all_to_all(col_imag.reshape(blocked), "rows", split_axis=3, concat_axis=2, tiled=True),
    )
    flat = (layout[0], layout[1], layout[2] * groups, layout[3] // groups)
    full_real = got_real.reshape(flat)
    full_imag = got_imag.reshape(flat)
    delta_real, delta_imag = transform("smlyc,yk->smlck", wide_cols, full_real, full_imag, 4, -1.0)
    upd_real = pupil_real * delta_real + pupil_imag * delta_imag
    upd_imag = pupil_real * delta_imag - pupil_imag * delta_real
    blank = jnp.zeros((layout[0], layout[3] // groups, size_k), jnp.float32)
    placed_real = jnp.stack(
        [
            lax.dynamic_update_slice_in_dim(
                blank, upd_real[:, source_index], offsets[source_index, 0], 2
            )
            for source_index in range(source_count)
        ],
        axis=1,
    )
    placed_imag = jnp.stack(
        [
            lax.dynamic_update_slice_in_dim(
                blank, upd_imag[:, source_index], offsets[source_index, 0], 2
            )
            for source_index in range(source_count)
        ],
        axis=1,
    )
    return (
        lax.all_to_all(placed_real, "rows", split_axis=3, concat_axis=2, tiled=True),
        lax.all_to_all(placed_imag, "rows", split_axis=3, concat_axis=2, tiled=True),
    )


def add_window(target, incoming, start_col, length):
    current = lax.dynamic_slice_in_dim(target, start_col, length, 2)
    return lax.dynamic_update_slice_in_dim(
        target, current + jnp.swapaxes(incoming, 1, 2), start_col, 2
    )


def body(object_real, object_imag, pupil_real, pupil_imag, measured, source_mask, offsets):
    length = pupil_real.shape[1]
    size_k = object_real.shape[2]
    source_count = offsets.shape[0]
    wide_cols, wide_rows = dft_tables(length)
    spec_real, spec_imag = (object_real, object_imag)
    weights = source_mask[0].astype(jnp.float32)
    field_real, field_imag = forward_fields(
        spec_real, spec_imag, pupil_real, pupil_imag, offsets, wide_cols, wide_rows, length
    )
    powers = jnp.sum(field_real * field_real + field_imag * field_imag, axis=0)
    partial_sum = jnp.tensordot(weights, powers, axes=1)
    share = lax.psum_scatter(partial_sum, "mode", scatter_dimension=0, tiled=True)
    share_rows = share.shape[0]
    measured_share = lax.dynamic_slice_in_dim(
        measured[0], lax.axis_index("mode") * share_rows, share_rows, 0
    )
    ratio_share = measured_share / jnp.sqrt(share + FLOOR_TERM)
    ratios = lax.all_gather(ratio_share, "mode", axis=0, tiled=True)
    factor = (ratios - 1.0)[None, None] * weights[None, :, None, None]
    diff_real = field_real * factor
    diff_imag = field_imag * factor
    ret_real, ret_imag = spectral_updates(
        diff_real, diff_imag, pupil_real, pupil_imag, offsets, wide_cols, size_k
    )
    for source_index in range(source_count):
        start_col = offsets[source_index, 1]
        spec_real = add_window(spec_real, ret_real[:, source_index], start_col, length)
        spec_imag = add_window(spec_imag, ret_imag[:, source_index], start_col, length)
    return (spec_real, spec_imag)


RADIX = 4
VMEM_LIMIT = 56 * 1024 * 1024


def split_pair(table):
    high = table.astype(ml_dtypes.bfloat16)
    low = (table - high.astype(np.float64)).astype(ml_dtypes.bfloat16)
    return np.stack([high, low])


def radix_tables(length):
    part = length // RADIX
    t = np.arange(RADIX)[:, None, None]
    r = np.arange(part)[None, :, None]
    s = np.arange(part)[None, None, :]
    angles = (r * (t + RADIX * s) % length) * (2.0 * np.pi / length)
    cos_t = np.cos(angles) / np.sqrt(length)
    sin_t = np.sin(angles) / np.sqrt(length)
    swap = lambda x: np.swapaxes(x, 1, 2)
    width = part // RADIX
    pieces = lambda x: x.reshape(RADIX, part, RADIX, width)
    beside = lambda x, y: np.stack([pieces(x), pieces(y)], axis=3).reshape(RADIX, part, 2 * part)
    columns = np.concatenate([beside(cos_t, sin_t), beside(-sin_t, cos_t)], axis=1)
    columns_back = np.swapaxes(columns, 1, 2)
    rows = np.concatenate([swap(cos_t), swap(sin_t)], axis=1)
    rows_back = np.concatenate([cos_t, sin_t], axis=1)
    return tuple(split_pair(table) for table in (columns, rows, rows_back, columns_back))


def halves(x):
    high = x.astype(jnp.bfloat16)
    low = (x - high.astype(jnp.float32)).astype(jnp.bfloat16)
    return high, low


def dot(a, b):
    return jnp.dot(a, b, preferred_element_type=jnp.float32)


def dot_right(x, table_ref, t):
    high, low = halves(x)
    return dot(high, table_ref[0, t]) + dot(low, table_ref[0, t]) + dot(high, table_ref[1, t])


def dot_left(table_ref, t, x):
    high, low = halves(x)
    return dot(table_ref[0, t], high) + dot(table_ref[0, t], low) + dot(table_ref[1, t], high)


def lanes_of(x, slots):
    width = x.shape[1] // slots
    return [x[:, n * width : (n + 1) * width] for n in range(slots)]


def times_i(x):
    half = x.shape[1] // 2
    turned = pltpu.roll(x, half, 1)
    return jnp.where(lax.broadcasted_iota(jnp.int32, x.shape, 1) < half, -turned, turned)


def lit_offsets(params_ref, leds, nth):
    row, col, seen = jnp.int32(0), jnp.int32(0), jnp.int32(0)
    for led in range(leds):
        lit = params_ref[led] != 0
        take = jnp.logical_and(lit, seen == nth)
        row = jnp.where(take, params_ref[leds + 2 * led], row)
        col = jnp.where(take, params_ref[leds + 2 * led + 1], col)
        seen = seen + lit.astype(jnp.int32)
    return row, col


def pupil_send_kernel(leds, params_ref, real_ref, imag_ref, out_ref):
    length = real_ref.shape[1]
    part = length // RADIX
    for nth in range(out_ref.shape[1]):
        row, _ = lit_offsets(params_ref, leds, nth)
        for index, ref in enumerate((real_ref, imag_ref)):
            rolled = pltpu.roll(ref[...], lax.rem(row, length), 1)
            for q in range(RADIX):
                block = rolled[:, q * part : (q + 1) * part].T
                out_ref[q, nth, index] = block
                out_ref[q + RADIX, nth, index] = block


def window_pupil(leds, nth, params_ref, pupil_ref):
    row, col = lit_offsets(params_ref, leds, nth)
    blocks, _, _, rows, width = pupil_ref.shape
    length = blocks * width
    upper, first = params_ref[3 * leds], params_ref[3 * leds + 1]
    position = first + lax.broadcasted_iota(jnp.int32, (rows, length), 0)
    owned = (position < row).astype(jnp.int32) == upper
    parts = []
    for index in range(2):
        whole = jnp.concatenate([pupil_ref[d, nth, index] for d in range(blocks)], axis=1)
        whole = pltpu.roll(whole, lax.rem(col, length), 1)
        parts.append(jnp.where(owned, whole, 0.0))
    wrapped = lax.broadcasted_iota(jnp.int32, (rows, length), 1) < col
    return parts[0], parts[1], wrapped


def columns_kernel(leds, chunk, params_ref, real_ref, imag_ref, pupil_ref, table_ref, *refs):
    out_ref = refs[-1]
    rows, size_k = real_ref.shape[1:]
    length = size_k // 2
    for nth in range(out_ref.shape[1]):
        p_r, p_i, wrapped = window_pupil(leds, nth, params_ref, pupil_ref)
        w_r = jnp.where(wrapped, real_ref[0, :, length:], real_ref[0, :, :length])
        w_i = jnp.where(wrapped, imag_ref[0, :, length:], imag_ref[0, :, :length])
        x_r = lanes_of(p_r * w_r - p_i * w_i, RADIX)
        x_i = lanes_of(p_r * w_i + p_i * w_r, RADIX)
        sum_r, sum_i = x_r[0] + x_r[2], x_i[0] + x_i[2]
        dif_r, dif_i = x_r[0] - x_r[2], x_i[0] - x_i[2]
        odd_r, odd_i = x_r[1] + x_r[3], x_i[1] + x_i[3]
        rot_r, rot_i = x_i[3] - x_i[1], x_r[1] - x_r[3]
        if chunk == 0:
            pairs = ((sum_r + odd_r, sum_i + odd_i), (dif_r + rot_r, dif_i + rot_i))
        else:
            pairs = ((sum_r - odd_r, sum_i - odd_i), (dif_r - rot_r, dif_i - rot_i))
        for t, pair in enumerate(pairs):
            z = dot_right(jnp.concatenate(pair, axis=1), table_ref, t)
            for u, piece in enumerate(lanes_of(z, RADIX)):
                out_ref[RADIX * t + u, nth, 0, :rows] = piece
    if len(refs) > 1:
        out_ref[:, :, 0, rows:] = refs[0][:, :, 0]


def rows_kernel(got_ref, table_ref, field_ref, total_ref):
    groups, count, modes, _, width = got_ref.shape
    part = field_ref.shape[1]
    slots = [(nth, mode) for nth in range(count) for mode in range(modes)]
    y = [[] for _ in range(RADIX)]
    for nth, mode in slots:
        x = [
            got_ref[q, nth, mode, :part] + got_ref[q + RADIX, nth, mode, :part]
            for q in range(RADIX)
        ]
        even, odd = x[0] + x[2], x[1] + x[3]
        dif, rot = x[0] - x[2], times_i(x[1] - x[3])
        for t, value in enumerate((even + odd, dif + rot, even - odd, dif - rot)):
            y[t].append(value)
    powers = []
    for t in range(RADIX):
        both = dot_left(table_ref, t, jnp.concatenate(y[t], axis=1))
        power = None
        for n, (a, b) in enumerate(
            zip(lanes_of(both[:part], len(slots)), lanes_of(both[part:], len(slots)))
        ):
            z = a + times_i(b)
            field_ref[t, :, n * width : (n + 1) * width] = z
            power = z * z if power is None else power + z * z
        powers.append(power + pltpu.roll(power, width // 2, 1))
    levels, _, deep, _ = total_ref.shape
    rows = deep // 2
    low = lax.broadcasted_iota(jnp.int32, (part, width), 1) < width // 2
    for pair in range(2):
        packed = jnp.where(low, powers[2 * pair], powers[2 * pair + 1])
        for d in range(groups):
            for z in range(levels):
                first = (d * levels + z) * rows
                total_ref[z, d, pair * rows : (pair + 1) * rows] = packed[first : first + rows]


def rows_back_kernel(field_ref, factor_ref, table_ref, out_ref):
    groups, count, modes, part, width = out_ref.shape
    slots = [(nth, mode) for nth in range(count) for mode in range(modes)]
    levels, _, deep, _ = factor_ref.shape
    rows = deep // 2
    low = lax.broadcasted_iota(jnp.int32, (part, width), 1) < width // 2
    u = [[] for _ in slots]
    for t in range(RADIX):
        pair = t // 2
        packed = jnp.concatenate(
            [
                factor_ref[z, d, pair * rows : (pair + 1) * rows]
                for d in range(groups)
                for z in range(levels)
            ],
            axis=0,
        )
        turned = pltpu.roll(packed, width // 2, 1)
        factor = jnp.where(low, packed, turned) if t % 2 == 0 else jnp.where(low, turned, packed)
        diff = jnp.concatenate(
            [x * factor for x in lanes_of(field_ref[t], len(slots))], axis=1
        )
        both = dot_left(table_ref, t, diff)
        for n, (a, b) in enumerate(
            zip(lanes_of(both[:part], len(slots)), lanes_of(both[part:], len(slots)))
        ):
            u[n].append(a - times_i(b))
    for (nth, mode), v in zip(slots, u):
        even, odd = v[0] + v[2], v[1] + v[3]
        dif, rot = v[0] - v[2], times_i(v[1] - v[3])
        for q, value in enumerate((even + odd, dif - rot, even - odd, dif + rot)):
            out_ref[q, nth, mode] = value
            out_ref[q + RADIX, nth, mode] = value


def columns_back_kernel(
    leds, chunk, params_ref, real_ref, imag_ref, pupil_ref, got_ref, table_ref, out_r, out_i
):
    rows, size_k = real_ref.shape[1:]
    length = size_k // 2
    totals = [[ref[0, :, :length], ref[0, :, length:]] for ref in (real_ref, imag_ref)]
    for nth in range(got_ref.shape[1]):
        p_r, p_i, wrapped = window_pupil(leds, nth, params_ref, pupil_ref)
        u = []
        for t in range(2):
            z = jnp.concatenate([got_ref[RADIX * t + n, nth, 0] for n in range(RADIX)], axis=1)
            u.append(lanes_of(dot_right(z, table_ref, t), 2))
        (a_r, a_i), (b_r, b_i) = u
        if chunk == 0:
            x_r = [a_r + b_r, a_r + b_i, a_r - b_r, a_r - b_i]
            x_i = [a_i + b_i, a_i - b_r, a_i - b_i, a_i + b_r]
        else:
            x_r = [a_r + b_r, -a_r - b_i, a_r - b_r, b_i - a_r]
            x_i = [a_i + b_i, b_r - a_i, a_i - b_i, -a_i - b_r]
        x_r, x_i = jnp.concatenate(x_r, axis=1), jnp.concatenate(x_i, axis=1)
        for total, delta in zip(totals, (p_r * x_r + p_i * x_i, p_r * x_i - p_i * x_r)):
            total[0] = total[0] + jnp.where(wrapped, 0.0, delta)
            total[1] = total[1] + jnp.where(wrapped, delta, 0.0)
    for out, total in zip((out_r, out_i), totals):
        out[0, :, :length] = total[0]
        out[0, :, length:] = total[1]


SMEM_SPEC = pl.BlockSpec(memory_space=pltpu.SMEM)
PARAMS = pltpu.CompilerParams(vmem_limit_bytes=VMEM_LIMIT)
CHUNKS = 2


def fixed(shape):
    zeros = (0,) * len(shape)
    return pl.BlockSpec(shape, lambda *_: zeros)


def one_mode(shape):
    block = shape[:2] + (1,) + shape[3:]
    return pl.BlockSpec(block, lambda i: (0, 0, i, 0, 0))


def cost(macs, *arrays):
    moved = sum(math.prod(a.shape) * a.dtype.itemsize for a in arrays)
    return pl.CostEstimate(flops=2 * macs, bytes_accessed=moved, transcendentals=0)


def shaped(shape):
    return jax.ShapeDtypeStruct(shape, jnp.float32)


def exchange(blocks):
    return lax.all_to_all(blocks, "rows", split_axis=0, concat_axis=0, tiled=True)


def amplitude_blocks(measured, groups, levels):
    width, length = measured.shape[1:]
    rows = width // levels
    mine = lax.dynamic_slice_in_dim(measured[0], lax.axis_index("mode") * rows, rows, 0)
    depth = rows // RADIX
    columns = length // groups // CHUNKS
    dims = (depth, 2, 2, groups // 2, columns, CHUNKS, 2)
    order = (6, 3, 5, 1, 0, 2, 4)
    return jnp.transpose(mine.reshape(dims), order).reshape(groups, rows, 2 * columns)


def fast_body(object_real, object_imag, pupil_real, pupil_imag, measured, source_mask, offsets):
    width, length = pupil_real.shape
    modes, local_rows, size_k = object_real.shape
    groups, levels = lax.axis_size("rows"), lax.axis_size("mode")
    part = length // RADIX
    leds = offsets.shape[0]
    tables = [jnp.asarray(table) for table in radix_tables(length)]
    place = lax.axis_index("rows")
    position = jnp.stack([place // RADIX, place % RADIX * local_rows]).astype(jnp.int32)
    params = jnp.concatenate([source_mask.reshape(-1), offsets.reshape(-1), position])
    spectrum = pl.BlockSpec((1, local_rows, size_k), lambda i: (i, 0, 0))

    def update(count):
        slots = count * modes
        dft_macs = 3 * slots * 2 * 4 * part * part * local_rows
        pupil_shape = (groups, count, 2, local_rows, width)
        block_shape = (groups, count, modes, local_rows, width)
        half_table = (2, RADIX // CHUNKS) + tables[0].shape[2:]

        def columns(chunk, pupil, amplitude):
            extra = 0 if amplitude is None else amplitude.shape[1] // slots
            out = shaped(block_shape[:3] + (local_rows + extra, width))
            operands = [params, object_real, object_imag, pupil, tables[0]]
            specs = [
                SMEM_SPEC,
                spectrum,
                spectrum,
                fixed(pupil_shape),
                pl.BlockSpec(half_table, lambda i: (0, chunk, 0, 0)),
            ]
            if amplitude is not None:
                amplitude = amplitude.reshape(groups, count, modes, extra, width)
                operands.append(amplitude)
                specs.append(one_mode(amplitude.shape))
            sent = pl.pallas_call(
                functools.partial(columns_kernel, leds, chunk),
                out_shape=out,
                grid=(modes,),
                in_specs=specs,
                out_specs=one_mode(out.shape),
                compiler_params=PARAMS,
                cost_estimate=cost(dft_macs, out, pupil, object_real, object_imag),
                name="columns",
            )(*operands)
            return exchange(sent)

        def rows(got):
            field = shaped((RADIX, part, slots * width))
            total = shaped((levels, groups, 2 * part // groups // levels, width))
            return pl.pallas_call(
                rows_kernel,
                out_shape=(field, total),
                grid=(1,),
                in_specs=[fixed(got.shape), fixed(tables[1].shape)],
                out_specs=(fixed(field.shape), fixed(total.shape)),
                compiler_params=PARAMS,
                cost_estimate=cost(dft_macs, got, field, total),
                name="rows",
            )(got, tables[1])

        def rows_back(field, factor):
            out = shaped(block_shape)
            sent = pl.pallas_call(
                rows_back_kernel,
                out_shape=out,
                grid=(1,),
                in_specs=[fixed(field.shape), fixed(factor.shape), fixed(tables[2].shape)],
                out_specs=fixed(block_shape),
                compiler_params=PARAMS,
                cost_estimate=cost(dft_macs, out, field, factor),
                name="rows_back",
            )(field, factor, tables[2])
            return exchange(sent)

        def columns_back(chunk, pupil, got, current):
            out = shaped(object_real.shape)
            return pl.pallas_call(
                functools.partial(columns_back_kernel, leds, chunk),
                out_shape=(out, out),
                grid=(modes,),
                in_specs=[
                    SMEM_SPEC,
                    spectrum,
                    spectrum,
                    fixed(pupil_shape),
                    one_mode(block_shape),
                    pl.BlockSpec(half_table, lambda i: (0, chunk, 0, 0)),
                ],
                out_specs=(spectrum, spectrum),
                input_output_aliases={1: 0, 2: 1} if chunk > 0 else {},
                compiler_params=PARAMS,
                cost_estimate=cost(dft_macs, got, pupil, out, out, out, out),
                name="columns_back",
            )(params, *current, pupil, got, tables[3])

        def run(*_):
            amplitude = amplitude_blocks(measured, groups, levels)
            out = shaped(pupil_shape)
            sent = pl.pallas_call(
                functools.partial(pupil_send_kernel, leds),
                out_shape=out,
                grid=(1,),
                in_specs=[SMEM_SPEC] + [fixed(pupil_real.shape)] * 2,
                out_specs=fixed(pupil_shape),
                compiler_params=PARAMS,
                cost_estimate=cost(0, out, pupil_real, pupil_imag),
                name="pupil_send",
            )(params, pupil_real, pupil_imag)
            pupil = exchange(sent)
            got = [columns(0, pupil, amplitude), columns(1, pupil, None)]
            amplitude = got[0][:, :, :, local_rows:].reshape(amplitude.shape)
            back = []
            for chunk in range(CHUNKS):
                field, total = rows(got[chunk])
                share = lax.psum_scatter(total, "mode", scatter_dimension=0, tiled=True)
                deep = share.shape[2]
                mine = amplitude[None, :, chunk * deep : (chunk + 1) * deep]
                ratio = mine / jnp.sqrt(share + FLOOR_TERM) - 1.0
                factor = lax.all_gather(ratio, "mode", axis=0, tiled=True)
                back.append(rows_back(field, factor))
            current = (object_real, object_imag)
            for chunk in range(CHUNKS):
                current = columns_back(chunk, pupil, back[chunk], current)
            return tuple(current)

        return run

    lit = jnp.sum((source_mask[0] != 0).astype(jnp.int32))
    most = max(leds - 1, 1)
    if most == 1:
        return update(1)()
    return lax.switch(jnp.clip(lit - 1, 0, most - 1), [update(n + 1) for n in range(most)])


def fits_fast(mesh, object_shape, pupil_shape, leds):
    groups, levels = mesh.shape["rows"], mesh.shape["mode"]
    length, size_k = pupil_shape[1], object_shape[2]
    modes, local_rows, width = object_shape[0] // levels, size_k // groups, length // groups
    amplitude_rows = width // levels
    return (
        size_k == 2 * length
        and groups == 2 * RADIX
        and levels == RADIX
        and local_rows % 256 == 0
        and width % 128 == 0
        and all(amplitude_rows % (8 * modes * n) == 0 for n in range(1, max(leds, 2)))
    )


def solution(mesh):
    in_specs = (
        P("mode", "rows", None),
        P("mode", "rows", None),
        P("rows", None),
        P("rows", None),
        P(None, "rows", None),
        P(),
        P(),
    )
    out_specs = (P("mode", "rows", None), P("mode", "rows", None))

    def chosen(object_real, object_imag, pupil_real, *others):
        fast = fits_fast(mesh, object_real.shape, pupil_real.shape, others[-1].shape[0])
        mapped = jax.shard_map(
            fast_body if fast else body,
            mesh=mesh,
            in_specs=in_specs,
            out_specs=out_specs,
            check_vma=False,
        )
        return mapped(object_real, object_imag, pupil_real, *others)

    return chosen
```

```python
import functools
import math

import jax
import jax.numpy as jnp
import ml_dtypes
import numpy as np
from jax import lax
from jax.experimental import pallas as pl
from jax.experimental.pallas import tpu as pltpu
from jax.sharding import PartitionSpec as P

FLOOR_TERM = 0.5
HIGHEST_PREC = lax.Precision.HIGHEST


def dft_tables(length):
    indices = jnp.arange(length, dtype=jnp.int32)
    phases = indices[:, None] * indices[None, :] % length
    angles = phases.astype(jnp.float32) * (2.0 * math.pi / length)
    scale_factor = 1.0 / math.sqrt(length)
    cos_table = jnp.cos(angles) * scale_factor
    sin_table = jnp.sin(angles) * scale_factor
    return (
        jnp.concatenate([cos_table, sin_table], axis=1),
        jnp.concatenate([cos_table, sin_table], axis=0),
    )


def transform(form, table, real_part, imag_part, axis, direction_sign):
    result = jnp.einsum(form, jnp.stack([real_part, imag_part]), table, precision=HIGHEST_PREC)
    length = result.shape[axis] // 2
    with_cos = lax.slice_in_dim(result, 0, length, axis=axis)
    with_sin = lax.slice_in_dim(result, length, 2 * length, axis=axis)
    return (with_cos[0] - direction_sign * with_sin[1], with_cos[1] + direction_sign * with_sin[0])


def right_product(real_part, imag_part, wide_cols, direction_sign):
    return transform("smlck,kj->smlcj", wide_cols, real_part, imag_part, 4, direction_sign)


def forward_fields(
    part_real, part_imag, pupil_real, pupil_imag, offsets, wide_cols, wide_rows, length
):
    source_count = offsets.shape[0]
    groups = lax.axis_size("rows")
    crop_real = jnp.stack(
        [
            lax.dynamic_slice_in_dim(part_real, offsets[source_index, 1], length, 2)
            for source_index in range(source_count)
        ],
        axis=1,
    )
    crop_imag = jnp.stack(
        [
            lax.dynamic_slice_in_dim(part_imag, offsets[source_index, 1], length, 2)
            for source_index in range(source_count)
        ],
        axis=1,
    )
    got_real, got_imag = (
        lax.all_to_all(
            jnp.swapaxes(crop_real, 2, 3), "rows", split_axis=2, concat_axis=3, tiled=True
        ),
        lax.all_to_all(
            jnp.swapaxes(crop_imag, 2, 3), "rows", split_axis=2, concat_axis=3, tiled=True
        ),
    )
    win_real = jnp.stack(
        [
            lax.dynamic_slice_in_dim(got_real[:, source_index], offsets[source_index, 0], length, 2)
            for source_index in range(source_count)
        ],
        axis=1,
    )
    win_imag = jnp.stack(
        [
            lax.dynamic_slice_in_dim(got_imag[:, source_index], offsets[source_index, 0], length, 2)
            for source_index in range(source_count)
        ],
        axis=1,
    )
    lifted_real = pupil_real * win_real - pupil_imag * win_imag
    lifted_imag = pupil_real * win_imag + pupil_imag * win_real
    half_real, half_imag = transform("smlcr,yr->smlyc", wide_rows, lifted_real, lifted_imag, 3, 1.0)
    layout = half_real.shape
    blocked = (layout[0], layout[1], groups, layout[2] // groups, layout[3])
    back_real, back_imag = (
        lax.all_to_all(half_real.reshape(blocked), "rows", split_axis=2, concat_axis=4, tiled=True),
        lax.all_to_all(half_imag.reshape(blocked), "rows", split_axis=2, concat_axis=4, tiled=True),
    )
    flat = (layout[0], layout[1], layout[2] // groups, layout[3] * groups)
    return right_product(back_real.reshape(flat), back_imag.reshape(flat), wide_cols, 1.0)


def spectral_updates(diff_real, diff_imag, pupil_real, pupil_imag, offsets, wide_cols, size_k):
    source_count = offsets.shape[0]
    groups = lax.axis_size("rows")
    col_real, col_imag = right_product(diff_real, diff_imag, wide_cols, -1.0)
    layout = col_real.shape
    blocked = (layout[0], layout[1], layout[2], groups, layout[3] // groups)
    got_real, got_imag = (
        lax.all_to_all(col_real.reshape(blocked), "rows", split_axis=3, concat_axis=2, tiled=True),
        lax.all_to_all(col_imag.reshape(blocked), "rows", split_axis=3, concat_axis=2, tiled=True),
    )
    flat = (layout[0], layout[1], layout[2] * groups, layout[3] // groups)
    full_real = got_real.reshape(flat)
    full_imag = got_imag.reshape(flat)
    delta_real, delta_imag = transform("smlyc,yk->smlck", wide_cols, full_real, full_imag, 4, -1.0)
    upd_real = pupil_real * delta_real + pupil_imag * delta_imag
    upd_imag = pupil_real * delta_imag - pupil_imag * delta_real
    blank = jnp.zeros((layout[0], layout[3] // groups, size_k), jnp.float32)
    placed_real = jnp.stack(
        [
            lax.dynamic_update_slice_in_dim(
                blank, upd_real[:, source_index], offsets[source_index, 0], 2
            )
            for source_index in range(source_count)
        ],
        axis=1,
    )
    placed_imag = jnp.stack(
        [
            lax.dynamic_update_slice_in_dim(
                blank, upd_imag[:, source_index], offsets[source_index, 0], 2
            )
            for source_index in range(source_count)
        ],
        axis=1,
    )
    return (
        lax.all_to_all(placed_real, "rows", split_axis=3, concat_axis=2, tiled=True),
        lax.all_to_all(placed_imag, "rows", split_axis=3, concat_axis=2, tiled=True),
    )


def add_window(target, incoming, start_col, length):
    current = lax.dynamic_slice_in_dim(target, start_col, length, 2)
    return lax.dynamic_update_slice_in_dim(
        target, current + jnp.swapaxes(incoming, 1, 2), start_col, 2
    )


def body(object_real, object_imag, pupil_real, pupil_imag, measured, source_mask, offsets):
    length = pupil_real.shape[1]
    size_k = object_real.shape[2]
    source_count = offsets.shape[0]
    wide_cols, wide_rows = dft_tables(length)
    spec_real, spec_imag = (object_real, object_imag)
    weights = source_mask[0].astype(jnp.float32)
    field_real, field_imag = forward_fields(
        spec_real, spec_imag, pupil_real, pupil_imag, offsets, wide_cols, wide_rows, length
    )
    powers = jnp.sum(field_real * field_real + field_imag * field_imag, axis=0)
    partial_sum = jnp.tensordot(weights, powers, axes=1)
    share = lax.psum_scatter(partial_sum, "mode", scatter_dimension=0, tiled=True)
    share_rows = share.shape[0]
    measured_share = lax.dynamic_slice_in_dim(
        measured[0], lax.axis_index("mode") * share_rows, share_rows, 0
    )
    ratio_share = measured_share / jnp.sqrt(share + FLOOR_TERM)
    ratios = lax.all_gather(ratio_share, "mode", axis=0, tiled=True)
    factor = (ratios - 1.0)[None, None] * weights[None, :, None, None]
    diff_real = field_real * factor
    diff_imag = field_imag * factor
    ret_real, ret_imag = spectral_updates(
        diff_real, diff_imag, pupil_real, pupil_imag, offsets, wide_cols, size_k
    )
    for source_index in range(source_count):
        start_col = offsets[source_index, 1]
        spec_real = add_window(spec_real, ret_real[:, source_index], start_col, length)
        spec_imag = add_window(spec_imag, ret_imag[:, source_index], start_col, length)
    return (spec_real, spec_imag)


RADIX = 4
VMEM_LIMIT = 56 * 1024 * 1024


def split_pair(table):
    high = table.astype(ml_dtypes.bfloat16)
    low = (table - high.astype(np.float64)).astype(ml_dtypes.bfloat16)
    return np.stack([high, low])


def radix_tables(length):
    part = length // RADIX
    t = np.arange(RADIX)[:, None, None]
    r = np.arange(part)[None, :, None]
    s = np.arange(part)[None, None, :]
    angles = (r * (t + RADIX * s) % length) * (2.0 * np.pi / length)
    cos_t = np.cos(angles) / np.sqrt(length)
    sin_t = np.sin(angles) / np.sqrt(length)
    swap = lambda x: np.swapaxes(x, 1, 2)
    width = part // RADIX
    pieces = lambda x: x.reshape(RADIX, part, RADIX, width)
    beside = lambda x, y: np.stack([pieces(x), pieces(y)], axis=3).reshape(RADIX, part, 2 * part)
    columns = np.concatenate([beside(cos_t, sin_t), beside(-sin_t, cos_t)], axis=1)
    columns_back = np.swapaxes(columns, 1, 2)
    rows = np.concatenate([swap(cos_t), swap(sin_t)], axis=1)
    rows_back = np.concatenate([cos_t, sin_t], axis=1)
    return tuple(split_pair(table) for table in (columns, rows, rows_back, columns_back))


def halves(x):
    high = x.astype(jnp.bfloat16)
    low = (x - high.astype(jnp.float32)).astype(jnp.bfloat16)
    return high, low


def dot(a, b):
    return jnp.dot(a, b, preferred_element_type=jnp.float32)


def dot_right(x, table_ref, t):
    high, low = halves(x)
    return dot(high, table_ref[0, t]) + dot(low, table_ref[0, t]) + dot(high, table_ref[1, t])


def dot_left(table_ref, t, x):
    high, low = halves(x)
    return dot(table_ref[0, t], high) + dot(table_ref[0, t], low) + dot(table_ref[1, t], high)


def lanes_of(x, slots):
    width = x.shape[1] // slots
    return [x[:, n * width : (n + 1) * width] for n in range(slots)]


def times_i(x):
    half = x.shape[1] // 2
    turned = pltpu.roll(x, half, 1)
    return jnp.where(lax.broadcasted_iota(jnp.int32, x.shape, 1) < half, -turned, turned)


def lit_offsets(params_ref, leds, nth):
    row, col, seen = jnp.int32(0), jnp.int32(0), jnp.int32(0)
    for led in range(leds):
        lit = params_ref[led] != 0
        take = jnp.logical_and(lit, seen == nth)
        row = jnp.where(take, params_ref[leds + 2 * led], row)
        col = jnp.where(take, params_ref[leds + 2 * led + 1], col)
        seen = seen + lit.astype(jnp.int32)
    return row, col


def place_of(params_ref, leds, levels=False):
    return params_ref[3 * leds + (1 if levels else 0)]


def hand_out(stage_ref, out_refs, here):
    for k, out_ref in enumerate(out_refs):
        out_ref[...] = stage_ref[jnp.bitwise_xor(here, k)]


def take_in(got_refs, stage_ref, here):
    for k, got_ref in enumerate(got_refs):
        stage_ref[jnp.bitwise_xor(here, k)] = got_ref[...]


def pupil_send_kernel(leds, params_ref, real_ref, imag_ref, *refs):
    out_refs, out_ref = refs[:-1], refs[-1]
    length = real_ref.shape[1]
    part = length // RADIX
    for nth in range(out_ref.shape[1]):
        row, _ = lit_offsets(params_ref, leds, nth)
        for index, ref in enumerate((real_ref, imag_ref)):
            rolled = pltpu.roll(ref[...], lax.rem(row, length), 1)
            for q in range(RADIX):
                block = rolled[:, q * part : (q + 1) * part].T
                out_ref[q, nth, index] = block
                out_ref[q + RADIX, nth, index] = block
    hand_out(out_ref, out_refs, place_of(params_ref, leds))


def window_pupil(leds, nth, params_ref, pupil_ref):
    row, col = lit_offsets(params_ref, leds, nth)
    blocks, _, _, rows, width = pupil_ref.shape
    length = blocks * width
    here = place_of(params_ref, leds)
    upper, first = here // RADIX, lax.rem(here, RADIX) * rows
    position = first + lax.broadcasted_iota(jnp.int32, (rows, length), 0)
    owned = (position < row).astype(jnp.int32) == upper
    parts = []
    for index in range(2):
        whole = jnp.concatenate([pupil_ref[d, nth, index] for d in range(blocks)], axis=1)
        whole = pltpu.roll(whole, lax.rem(col, length), 1)
        parts.append(jnp.where(owned, whole, 0.0))
    wrapped = lax.broadcasted_iota(jnp.int32, (rows, length), 1) < col
    return parts[0], parts[1], wrapped


def columns_kernel(leds, chunk, groups, params_ref, real_ref, imag_ref, table_ref, *refs):
    got_refs, refs = refs[:groups], refs[groups:]
    pupil_ref, out_ref = refs[-2:]
    out_refs, refs = refs[-2 - groups : -2], refs[: -2 - groups]
    here = place_of(params_ref, leds)
    take_in(got_refs, pupil_ref, here)
    rows, size_k = real_ref.shape[1:]
    length = size_k // 2
    for nth in range(out_ref.shape[1]):
        p_r, p_i, wrapped = window_pupil(leds, nth, params_ref, pupil_ref)
        w_r = jnp.where(wrapped, real_ref[0, :, length:], real_ref[0, :, :length])
        w_i = jnp.where(wrapped, imag_ref[0, :, length:], imag_ref[0, :, :length])
        x_r = lanes_of(p_r * w_r - p_i * w_i, RADIX)
        x_i = lanes_of(p_r * w_i + p_i * w_r, RADIX)
        sum_r, sum_i = x_r[0] + x_r[2], x_i[0] + x_i[2]
        dif_r, dif_i = x_r[0] - x_r[2], x_i[0] - x_i[2]
        odd_r, odd_i = x_r[1] + x_r[3], x_i[1] + x_i[3]
        rot_r, rot_i = x_i[3] - x_i[1], x_r[1] - x_r[3]
        if chunk == 0:
            pairs = ((sum_r + odd_r, sum_i + odd_i), (dif_r + rot_r, dif_i + rot_i))
        else:
            pairs = ((sum_r - odd_r, sum_i - odd_i), (dif_r - rot_r, dif_i - rot_i))
        for t, pair in enumerate(pairs):
            z = dot_right(jnp.concatenate(pair, axis=1), table_ref, t)
            for u, piece in enumerate(lanes_of(z, RADIX)):
                out_ref[RADIX * t + u, nth, 0, :rows] = piece
    if len(refs) > 0:
        out_ref[:, :, 0, rows:] = refs[0][:, :, 0]
    hand_out(out_ref, out_refs, here)


def rows_kernel(leds, params_ref, table_ref, *refs):
    got_ref, total_ref = refs[-2:]
    groups, count, modes, _, width = got_ref.shape
    levels = total_ref.shape[0]
    field_ref, total_refs = refs[groups], refs[groups + 1 : groups + 1 + levels]
    take_in(refs[:groups], got_ref, place_of(params_ref, leds))
    for amplitude_ref in refs[groups + 1 + levels : -2]:
        amplitude_ref[...] = got_ref[:, :, :, field_ref.shape[1] :]
    part = field_ref.shape[1]
    slots = [(nth, mode) for nth in range(count) for mode in range(modes)]
    y = [[] for _ in range(RADIX)]
    for nth, mode in slots:
        x = [
            got_ref[q, nth, mode, :part] + got_ref[q + RADIX, nth, mode, :part]
            for q in range(RADIX)
        ]
        even, odd = x[0] + x[2], x[1] + x[3]
        dif, rot = x[0] - x[2], times_i(x[1] - x[3])
        for t, value in enumerate((even + odd, dif + rot, even - odd, dif - rot)):
            y[t].append(value)
    powers = []
    for t in range(RADIX):
        both = dot_left(table_ref, t, jnp.concatenate(y[t], axis=1))
        power = None
        for n, (a, b) in enumerate(
            zip(lanes_of(both[:part], len(slots)), lanes_of(both[part:], len(slots)))
        ):
            z = a + times_i(b)
            field_ref[t, :, n * width : (n + 1) * width] = z
            power = z * z if power is None else power + z * z
        powers.append(power + pltpu.roll(power, width // 2, 1))
    rows = total_ref.shape[2] // 2
    low = lax.broadcasted_iota(jnp.int32, (part, width), 1) < width // 2
    for pair in range(2):
        packed = jnp.where(low, powers[2 * pair], powers[2 * pair + 1])
        for d in range(groups):
            for z in range(levels):
                first = (d * levels + z) * rows
                total_ref[z, d, pair * rows : (pair + 1) * rows] = packed[first : first + rows]
    level = place_of(params_ref, leds, True)
    for k, ref in enumerate(total_refs):
        ref[...] = total_ref[lax.rem(level + k, levels)]


def rows_back_kernel(leds, params_ref, table_ref, field_ref, *refs):
    factor_ref, out_ref = refs[-2:]
    groups, count, modes, part, width = out_ref.shape
    levels = factor_ref.shape[0]
    level = place_of(params_ref, leds, True)
    for k, ref in enumerate(refs[:levels]):
        factor_ref[lax.rem(level + levels - k, levels)] = ref[...]
    out_refs = refs[levels:-2]
    slots = [(nth, mode) for nth in range(count) for mode in range(modes)]
    rows = factor_ref.shape[2] // 2
    low = lax.broadcasted_iota(jnp.int32, (part, width), 1) < width // 2
    u = [[] for _ in slots]
    for t in range(RADIX):
        pair = t // 2
        packed = jnp.concatenate(
            [
                factor_ref[z, d, pair * rows : (pair + 1) * rows]
                for d in range(groups)
                for z in range(levels)
            ],
            axis=0,
        )
        turned = pltpu.roll(packed, width // 2, 1)
        factor = jnp.where(low, packed, turned) if t % 2 == 0 else jnp.where(low, turned, packed)
        diff = jnp.concatenate(
            [x * factor for x in lanes_of(field_ref[t], len(slots))], axis=1
        )
        both = dot_left(table_ref, t, diff)
        for n, (a, b) in enumerate(
            zip(lanes_of(both[:part], len(slots)), lanes_of(both[part:], len(slots)))
        ):
            u[n].append(a - times_i(b))
    for (nth, mode), v in zip(slots, u):
        even, odd = v[0] + v[2], v[1] + v[3]
        dif, rot = v[0] - v[2], times_i(v[1] - v[3])
        for q, value in enumerate((even + odd, dif - rot, even - odd, dif + rot)):
            out_ref[q, nth, mode] = value
            out_ref[q + RADIX, nth, mode] = value
    hand_out(out_ref, out_refs, place_of(params_ref, leds))


def columns_back_kernel(leds, chunk, groups, params_ref, real_ref, imag_ref, table_ref, *refs):
    out_r, out_i, pupil_ref, got_ref = refs[-4:]
    here = place_of(params_ref, leds)
    take_in(refs[:groups], pupil_ref, here)
    take_in(refs[groups : 2 * groups], got_ref, here)
    rows, size_k = real_ref.shape[1:]
    length = size_k // 2
    totals = [[ref[0, :, :length], ref[0, :, length:]] for ref in (real_ref, imag_ref)]
    for nth in range(got_ref.shape[1]):
        p_r, p_i, wrapped = window_pupil(leds, nth, params_ref, pupil_ref)
        u = []
        for t in range(2):
            z = jnp.concatenate([got_ref[RADIX * t + n, nth, 0] for n in range(RADIX)], axis=1)
            u.append(lanes_of(dot_right(z, table_ref, t), 2))
        (a_r, a_i), (b_r, b_i) = u
        if chunk == 0:
            x_r = [a_r + b_r, a_r + b_i, a_r - b_r, a_r - b_i]
            x_i = [a_i + b_i, a_i - b_r, a_i - b_i, a_i + b_r]
        else:
            x_r = [a_r + b_r, -a_r - b_i, a_r - b_r, b_i - a_r]
            x_i = [a_i + b_i, b_r - a_i, a_i - b_i, -a_i - b_r]
        x_r, x_i = jnp.concatenate(x_r, axis=1), jnp.concatenate(x_i, axis=1)
        for total, delta in zip(totals, (p_r * x_r + p_i * x_i, p_r * x_i - p_i * x_r)):
            total[0] = total[0] + jnp.where(wrapped, 0.0, delta)
            total[1] = total[1] + jnp.where(wrapped, delta, 0.0)
    for out, total in zip((out_r, out_i), totals):
        out[0, :, :length] = total[0]
        out[0, :, length:] = total[1]


SMEM_SPEC = pl.BlockSpec(memory_space=pltpu.SMEM)
PARAMS = pltpu.CompilerParams(vmem_limit_bytes=VMEM_LIMIT)
CHUNKS = 2


def fixed(shape):
    zeros = (0,) * len(shape)
    return pl.BlockSpec(shape, lambda *_: zeros)


def one_mode(shape):
    before = len(shape) - 3
    block = shape[:before] + (1,) + shape[before + 1 :]
    return pl.BlockSpec(block, lambda i: (0,) * before + (i, 0, 0))


def cost(macs, *arrays):
    moved = sum(math.prod(a.shape) * a.dtype.itemsize for a in arrays)
    return pl.CostEstimate(flops=2 * macs, bytes_accessed=moved, transcendentals=0)


def shaped(shape):
    return jax.ShapeDtypeStruct(shape, jnp.float32)


def exchange(blocks):
    places = range(len(blocks))
    return [blocks[0]] + [
        lax.ppermute(blocks[k], "rows", [(d, d ^ k) for d in places]) for k in places[1:]
    ]


def around(levels, value_of):
    ring = range(levels)
    return [value_of(0)] + [
        lax.ppermute(value_of(k), "mode", [(z, (z + k) % levels) for z in ring]) for k in ring[1:]
    ]


def amplitude_kernel(leds, params_ref, measured_ref, out_ref):
    groups, rows, lanes = out_ref.shape
    width, length = measured_ref.shape[1:]
    columns = lanes // 2
    depth = rows // RADIX
    first = place_of(params_ref, leds, True) * rows

    def pick(x, y, turned):
        total = None
        for _ in range(3):
            x_part = x.astype(jnp.bfloat16)
            x = x - x_part.astype(jnp.float32)
            piece = dot(y, x_part) if turned else dot(x_part, y)
            total = piece if total is None else total + piece
        return total

    def ones_where(condition):
        return jnp.where(condition, 1.0, 0.0).astype(jnp.bfloat16)

    order = lax.broadcasted_iota(jnp.int32, (rows, width), 0)
    source = RADIX * (order % depth) + 2 * ((order // depth) % 2) + order // (2 * depth)
    taken = lax.broadcasted_iota(jnp.int32, (rows, width), 1) == source + first
    mine = pick(measured_ref[0], ones_where(taken), True)
    part = length // RADIX
    from_col = lax.broadcasted_iota(jnp.int32, (length, part), 0)
    to_col = lax.broadcasted_iota(jnp.int32, (length, part), 1)
    half = rows // 2
    for t in range(RADIX):
        chunk, side = t // 2, t % 2
        found = pick(mine, ones_where(from_col == RADIX * to_col + t), False)
        for u, piece in enumerate(lanes_of(found, RADIX)):
            out_ref[RADIX * side + u, chunk * half : (chunk + 1) * half] = jnp.concatenate(
                [piece[:half], piece[half:]], axis=1
            )


def fast_body(object_real, object_imag, pupil_real, pupil_imag, measured, source_mask, offsets):
    width, length = pupil_real.shape
    modes, local_rows, size_k = object_real.shape
    groups, levels = lax.axis_size("rows"), lax.axis_size("mode")
    part = length // RADIX
    leds = offsets.shape[0]
    tables = [jnp.asarray(table) for table in radix_tables(length)]
    position = jnp.stack([lax.axis_index("rows"), lax.axis_index("mode")]).astype(jnp.int32)
    params = jnp.concatenate([source_mask.reshape(-1), offsets.reshape(-1), position])
    spectrum = pl.BlockSpec((1, local_rows, size_k), lambda i: (i, 0, 0))

    def update(count):
        slots = count * modes
        dft_macs = 3 * slots * 2 * 4 * part * part * local_rows
        pupil_shape = (count, 2, local_rows, width)
        block_shape = (count, modes, local_rows, width)
        half_table = (2, RADIX // CHUNKS) + tables[0].shape[2:]
        by_mode = (count, 1) + block_shape[2:]
        pupil_stage = pltpu.VMEM((groups,) + pupil_shape, jnp.float32)

        def columns(chunk, pupil, amplitude):
            extra = 0 if amplitude is None else amplitude.shape[1] // slots
            out = shaped(block_shape[:2] + (local_rows + extra, width))
            operands = [params, object_real, object_imag, tables[0], *pupil]
            specs = [
                SMEM_SPEC,
                spectrum,
                spectrum,
                pl.BlockSpec(half_table, lambda i: (0, chunk, 0, 0)),
            ] + [fixed(pupil_shape)] * groups
            if amplitude is not None:
                amplitude = amplitude.reshape(groups, count, modes, extra, width)
                operands.append(amplitude)
                specs.append(one_mode(amplitude.shape))
            stage = (groups, count, 1) + out.shape[2:]
            sent = pl.pallas_call(
                functools.partial(columns_kernel, leds, chunk, groups),
                out_shape=(out,) * groups,
                grid=(modes,),
                in_specs=specs,
                out_specs=(one_mode(out.shape),) * groups,
                scratch_shapes=[pupil_stage, pltpu.VMEM(stage, jnp.float32)],
                compiler_params=PARAMS,
                cost_estimate=cost(dft_macs, *[out] * 16, object_real, object_imag),
                name="columns",
            )(*operands)
            return exchange(sent)

        def rows(got):
            field = shaped((RADIX, part, slots * width))
            total = shaped((groups, 2 * part // groups // levels, width))
            extra = got[0].shape[2] - local_rows
            outs = (field,) + (total,) * levels
            if extra > 0:
                outs += (shaped((groups, count, modes, extra, width)),)
            return pl.pallas_call(
                functools.partial(rows_kernel, leds),
                out_shape=outs,
                grid=(1,),
                in_specs=[SMEM_SPEC, fixed(tables[1].shape)] + [fixed(got[0].shape)] * groups,
                out_specs=tuple(fixed(out.shape) for out in outs),
                scratch_shapes=[
                    pltpu.VMEM((groups,) + got[0].shape, jnp.float32),
                    pltpu.VMEM((levels,) + total.shape, jnp.float32),
                ],
                compiler_params=PARAMS,
                cost_estimate=cost(dft_macs, *got, field),
                name="rows",
            )(params, tables[1], *got)

        def rows_back(field, factor):
            out = shaped(block_shape)
            sent = pl.pallas_call(
                functools.partial(rows_back_kernel, leds),
                out_shape=(out,) * groups,
                grid=(1,),
                in_specs=[SMEM_SPEC, fixed(tables[2].shape), fixed(field.shape)]
                + [fixed(factor[0].shape)] * levels,
                out_specs=(fixed(block_shape),) * groups,
                scratch_shapes=[
                    pltpu.VMEM((levels,) + factor[0].shape, jnp.float32),
                    pltpu.VMEM((groups,) + block_shape, jnp.float32),
                ],
                compiler_params=PARAMS,
                cost_estimate=cost(dft_macs, *[out] * groups, field),
                name="rows_back",
            )(params, tables[2], field, *factor)
            return exchange(sent)

        def columns_back(chunk, pupil, got, current):
            out = shaped(object_real.shape)
            return pl.pallas_call(
                functools.partial(columns_back_kernel, leds, chunk, groups),
                out_shape=(out, out),
                grid=(modes,),
                in_specs=[
                    SMEM_SPEC,
                    spectrum,
                    spectrum,
                    pl.BlockSpec(half_table, lambda i: (0, chunk, 0, 0)),
                ]
                + [fixed(pupil_shape)] * groups
                + [one_mode(block_shape)] * groups,
                out_specs=(spectrum, spectrum),
                scratch_shapes=[pupil_stage, pltpu.VMEM((groups,) + by_mode, jnp.float32)],
                input_output_aliases={1: 0, 2: 1} if chunk > 0 else {},
                compiler_params=PARAMS,
                cost_estimate=cost(dft_macs, *got, *pupil, out, out, out, out),
                name="columns_back",
            )(params, *current, tables[3], *pupil, *got)

        def run(*_):
            amplitude = shaped((groups, width // levels, width))
            amplitude = pl.pallas_call(
                functools.partial(amplitude_kernel, leds),
                out_shape=amplitude,
                grid=(1,),
                in_specs=[SMEM_SPEC, fixed(measured.shape)],
                out_specs=fixed(amplitude.shape),
                compiler_params=PARAMS,
                cost_estimate=cost(3 * length * length * RADIX * 8, amplitude, measured),
                name="amplitude",
            )(params, measured)
            out = shaped(pupil_shape)
            sent = pl.pallas_call(
                functools.partial(pupil_send_kernel, leds),
                out_shape=(out,) * groups,
                grid=(1,),
                in_specs=[SMEM_SPEC] + [fixed(pupil_real.shape)] * 2,
                out_specs=(fixed(pupil_shape),) * groups,
                scratch_shapes=[pupil_stage],
                compiler_params=PARAMS,
                cost_estimate=cost(0, *[out] * groups, pupil_real, pupil_imag),
                name="pupil_send",
            )(params, pupil_real, pupil_imag)
            pupil = exchange(sent)
            got = [columns(0, pupil, amplitude), columns(1, pupil, None)]
            back = []
            for chunk in range(CHUNKS):
                field, *totals = rows(got[chunk])
                if chunk == 0:
                    mine = totals.pop().reshape(groups, width // levels, width)
                share = sum(around(levels, lambda k: totals[k]))
                deep = share.shape[1]
                ratio = mine[:, chunk * deep : (chunk + 1) * deep] / jnp.sqrt(share + FLOOR_TERM)
                factor = around(levels, lambda k: ratio - 1.0)
                back.append(rows_back(field, factor))
            current = (object_real, object_imag)
            for chunk in range(CHUNKS):
                current = columns_back(chunk, pupil, back[chunk], current)
            return tuple(current)

        return run

    lit = jnp.sum((source_mask[0] != 0).astype(jnp.int32))
    most = max(leds - 1, 1)
    if most == 1:
        return update(1)()
    return lax.switch(jnp.clip(lit - 1, 0, most - 1), [update(n + 1) for n in range(most)])


def fits_fast(mesh, object_shape, pupil_shape, leds):
    groups, levels = mesh.shape["rows"], mesh.shape["mode"]
    length, size_k = pupil_shape[1], object_shape[2]
    modes, local_rows, width = object_shape[0] // levels, size_k // groups, length // groups
    amplitude_rows = width // levels
    return (
        size_k == 2 * length
        and groups == 2 * RADIX
        and levels == RADIX
        and local_rows % 256 == 0
        and width % 128 == 0
        and all(amplitude_rows % (8 * modes * n) == 0 for n in range(1, max(leds, 2)))
    )


def solution(mesh):
    in_specs = (
        P("mode", "rows", None),
        P("mode", "rows", None),
        P("rows", None),
        P("rows", None),
        P(None, "rows", None),
        P(),
        P(),
    )
    out_specs = (P("mode", "rows", None), P("mode", "rows", None))

    def chosen(object_real, object_imag, pupil_real, *others):
        fast = fits_fast(mesh, object_real.shape, pupil_real.shape, others[-1].shape[0])
        mapped = jax.shard_map(
            fast_body if fast else body,
            mesh=mesh,
            in_specs=in_specs,
            out_specs=out_specs,
            check_vma=False,
        )
        return mapped(object_real, object_imag, pupil_real, *others)

    return chosen
```

```python
import functools
import math

import jax
import jax.numpy as jnp
import ml_dtypes
import numpy as np
from jax import lax
from jax.experimental import pallas as pl
from jax.experimental.pallas import tpu as pltpu
from jax.sharding import PartitionSpec as P

FLOOR_TERM = 0.5
HIGHEST_PREC = lax.Precision.HIGHEST


def dft_tables(length):
    indices = jnp.arange(length, dtype=jnp.int32)
    phases = indices[:, None] * indices[None, :] % length
    angles = phases.astype(jnp.float32) * (2.0 * math.pi / length)
    scale_factor = 1.0 / math.sqrt(length)
    cos_table = jnp.cos(angles) * scale_factor
    sin_table = jnp.sin(angles) * scale_factor
    return (
        jnp.concatenate([cos_table, sin_table], axis=1),
        jnp.concatenate([cos_table, sin_table], axis=0),
    )


def transform(form, table, real_part, imag_part, axis, direction_sign):
    result = jnp.einsum(form, jnp.stack([real_part, imag_part]), table, precision=HIGHEST_PREC)
    length = result.shape[axis] // 2
    with_cos = lax.slice_in_dim(result, 0, length, axis=axis)
    with_sin = lax.slice_in_dim(result, length, 2 * length, axis=axis)
    return (with_cos[0] - direction_sign * with_sin[1], with_cos[1] + direction_sign * with_sin[0])


def right_product(real_part, imag_part, wide_cols, direction_sign):
    return transform("smlck,kj->smlcj", wide_cols, real_part, imag_part, 4, direction_sign)


def forward_fields(
    part_real, part_imag, pupil_real, pupil_imag, offsets, wide_cols, wide_rows, length
):
    source_count = offsets.shape[0]
    groups = lax.axis_size("rows")
    crop_real = jnp.stack(
        [
            lax.dynamic_slice_in_dim(part_real, offsets[source_index, 1], length, 2)
            for source_index in range(source_count)
        ],
        axis=1,
    )
    crop_imag = jnp.stack(
        [
            lax.dynamic_slice_in_dim(part_imag, offsets[source_index, 1], length, 2)
            for source_index in range(source_count)
        ],
        axis=1,
    )
    got_real, got_imag = (
        lax.all_to_all(
            jnp.swapaxes(crop_real, 2, 3), "rows", split_axis=2, concat_axis=3, tiled=True
        ),
        lax.all_to_all(
            jnp.swapaxes(crop_imag, 2, 3), "rows", split_axis=2, concat_axis=3, tiled=True
        ),
    )
    win_real = jnp.stack(
        [
            lax.dynamic_slice_in_dim(got_real[:, source_index], offsets[source_index, 0], length, 2)
            for source_index in range(source_count)
        ],
        axis=1,
    )
    win_imag = jnp.stack(
        [
            lax.dynamic_slice_in_dim(got_imag[:, source_index], offsets[source_index, 0], length, 2)
            for source_index in range(source_count)
        ],
        axis=1,
    )
    lifted_real = pupil_real * win_real - pupil_imag * win_imag
    lifted_imag = pupil_real * win_imag + pupil_imag * win_real
    half_real, half_imag = transform("smlcr,yr->smlyc", wide_rows, lifted_real, lifted_imag, 3, 1.0)
    layout = half_real.shape
    blocked = (layout[0], layout[1], groups, layout[2] // groups, layout[3])
    back_real, back_imag = (
        lax.all_to_all(half_real.reshape(blocked), "rows", split_axis=2, concat_axis=4, tiled=True),
        lax.all_to_all(half_imag.reshape(blocked), "rows", split_axis=2, concat_axis=4, tiled=True),
    )
    flat = (layout[0], layout[1], layout[2] // groups, layout[3] * groups)
    return right_product(back_real.reshape(flat), back_imag.reshape(flat), wide_cols, 1.0)


def spectral_updates(diff_real, diff_imag, pupil_real, pupil_imag, offsets, wide_cols, size_k):
    source_count = offsets.shape[0]
    groups = lax.axis_size("rows")
    col_real, col_imag = right_product(diff_real, diff_imag, wide_cols, -1.0)
    layout = col_real.shape
    blocked = (layout[0], layout[1], layout[2], groups, layout[3] // groups)
    got_real, got_imag = (
        lax.all_to_all(col_real.reshape(blocked), "rows", split_axis=3, concat_axis=2, tiled=True),
        lax.all_to_all(col_imag.reshape(blocked), "rows", split_axis=3, concat_axis=2, tiled=True),
    )
    flat = (layout[0], layout[1], layout[2] * groups, layout[3] // groups)
    full_real = got_real.reshape(flat)
    full_imag = got_imag.reshape(flat)
    delta_real, delta_imag = transform("smlyc,yk->smlck", wide_cols, full_real, full_imag, 4, -1.0)
    upd_real = pupil_real * delta_real + pupil_imag * delta_imag
    upd_imag = pupil_real * delta_imag - pupil_imag * delta_real
    blank = jnp.zeros((layout[0], layout[3] // groups, size_k), jnp.float32)
    placed_real = jnp.stack(
        [
            lax.dynamic_update_slice_in_dim(
                blank, upd_real[:, source_index], offsets[source_index, 0], 2
            )
            for source_index in range(source_count)
        ],
        axis=1,
    )
    placed_imag = jnp.stack(
        [
            lax.dynamic_update_slice_in_dim(
                blank, upd_imag[:, source_index], offsets[source_index, 0], 2
            )
            for source_index in range(source_count)
        ],
        axis=1,
    )
    return (
        lax.all_to_all(placed_real, "rows", split_axis=3, concat_axis=2, tiled=True),
        lax.all_to_all(placed_imag, "rows", split_axis=3, concat_axis=2, tiled=True),
    )


def add_window(target, incoming, start_col, length):
    current = lax.dynamic_slice_in_dim(target, start_col, length, 2)
    return lax.dynamic_update_slice_in_dim(
        target, current + jnp.swapaxes(incoming, 1, 2), start_col, 2
    )


def body(object_real, object_imag, pupil_real, pupil_imag, measured, source_mask, offsets):
    length = pupil_real.shape[1]
    size_k = object_real.shape[2]
    source_count = offsets.shape[0]
    wide_cols, wide_rows = dft_tables(length)
    spec_real, spec_imag = (object_real, object_imag)
    weights = source_mask[0].astype(jnp.float32)
    field_real, field_imag = forward_fields(
        spec_real, spec_imag, pupil_real, pupil_imag, offsets, wide_cols, wide_rows, length
    )
    powers = jnp.sum(field_real * field_real + field_imag * field_imag, axis=0)
    partial_sum = jnp.tensordot(weights, powers, axes=1)
    share = lax.psum_scatter(partial_sum, "mode", scatter_dimension=0, tiled=True)
    share_rows = share.shape[0]
    measured_share = lax.dynamic_slice_in_dim(
        measured[0], lax.axis_index("mode") * share_rows, share_rows, 0
    )
    ratio_share = measured_share / jnp.sqrt(share + FLOOR_TERM)
    ratios = lax.all_gather(ratio_share, "mode", axis=0, tiled=True)
    factor = (ratios - 1.0)[None, None] * weights[None, :, None, None]
    diff_real = field_real * factor
    diff_imag = field_imag * factor
    ret_real, ret_imag = spectral_updates(
        diff_real, diff_imag, pupil_real, pupil_imag, offsets, wide_cols, size_k
    )
    for source_index in range(source_count):
        start_col = offsets[source_index, 1]
        spec_real = add_window(spec_real, ret_real[:, source_index], start_col, length)
        spec_imag = add_window(spec_imag, ret_imag[:, source_index], start_col, length)
    return (spec_real, spec_imag)


RADIX = 4
ROW_TILE = 64


def split_pair(table):
    high = table.astype(ml_dtypes.bfloat16)
    low = (table - high.astype(np.float64)).astype(ml_dtypes.bfloat16)
    return np.stack([high, low])


def radix_tables(length):
    part = length // RADIX
    t = np.arange(RADIX)[:, None, None]
    r = np.arange(part)[None, :, None]
    s = np.arange(part)[None, None, :]
    angles = (r * (t + RADIX * s) % length) * (2.0 * np.pi / length)
    cos_t = np.cos(angles) / np.sqrt(length)
    sin_t = np.sin(angles) / np.sqrt(length)
    swap = lambda x: np.swapaxes(x, 1, 2)
    width = part // RADIX
    pieces = lambda x: x.reshape(RADIX, part, RADIX, width)
    beside = lambda x, y: np.stack([pieces(x), pieces(y)], axis=3).reshape(RADIX, part, 2 * part)
    columns = np.concatenate([beside(cos_t, sin_t), beside(-sin_t, cos_t)], axis=1)
    columns_back = np.swapaxes(columns, 1, 2)
    rows = np.concatenate([swap(cos_t), swap(sin_t)], axis=1)
    rows_back = np.concatenate([cos_t, sin_t], axis=1)
    return tuple(split_pair(table) for table in (columns, rows, rows_back, columns_back))


def halves(x):
    high = x.astype(jnp.bfloat16)
    low = (x - high.astype(jnp.float32)).astype(jnp.bfloat16)
    return high, low


def dot(a, b):
    return jnp.dot(a, b, preferred_element_type=jnp.float32)


def dot_right(pair_ref, table_ref, t):
    high, low = pair_ref[0], pair_ref[1]
    return dot(high, table_ref[0, t]) + dot(low, table_ref[0, t]) + dot(high, table_ref[1, t])


def dot_left(table_ref, t, high, low):
    return dot(table_ref[0, t], high) + dot(table_ref[0, t], low) + dot(table_ref[1, t], high)


def over_rows(rows, step):
    def one(i, _):
        step(pl.ds(pl.multiple_of(i * ROW_TILE, ROW_TILE), ROW_TILE))
        return 0

    lax.fori_loop(0, rows // ROW_TILE, one, 0)


def lanes_of(x, slots):
    width = x.shape[1] // slots
    return [x[:, n * width : (n + 1) * width] for n in range(slots)]


def times_i(x):
    half = x.shape[1] // 2
    turned = pltpu.roll(x, half, 1)
    return jnp.where(lax.broadcasted_iota(jnp.int32, x.shape, 1) < half, -turned, turned)


def lit_offsets(params_ref, leds, nth):
    row, col, seen = jnp.int32(0), jnp.int32(0), jnp.int32(0)
    for led in range(leds):
        lit = params_ref[led] != 0
        take = jnp.logical_and(lit, seen == nth)
        row = jnp.where(take, params_ref[leds + 2 * led], row)
        col = jnp.where(take, params_ref[leds + 2 * led + 1], col)
        seen = seen + lit.astype(jnp.int32)
    return row, col


def place_of(params_ref, leds, levels=False):
    return params_ref[3 * leds + (1 if levels else 0)]


def hand_out(stage_ref, out_refs, here):
    for k, out_ref in enumerate(out_refs):
        out_ref[...] = stage_ref[jnp.bitwise_xor(here, k)]


def take_in(got_refs, stage_ref, here):
    for k, got_ref in enumerate(got_refs):
        stage_ref[jnp.bitwise_xor(here, k)] = got_ref[...]


def pupil_send_kernel(leds, params_ref, real_ref, imag_ref, *refs):
    out_refs, out_ref = refs[:-1], refs[-1]
    length = real_ref.shape[1]
    part = length // RADIX
    for nth in range(out_ref.shape[1]):
        row, _ = lit_offsets(params_ref, leds, nth)
        for index, ref in enumerate((real_ref, imag_ref)):
            rolled = pltpu.roll(ref[...], lax.rem(row, length), 1)
            for q in range(RADIX):
                block = rolled[:, q * part : (q + 1) * part].T
                out_ref[q, nth, index] = block
                out_ref[q + RADIX, nth, index] = block
    hand_out(out_ref, out_refs, place_of(params_ref, leds))


def window_pupil(leds, params_ref, stage_ref, pupil_ref):
    here = place_of(params_ref, leds)
    blocks, count, _, rows, width = stage_ref.shape
    length = blocks * width
    upper, first = here // RADIX, lax.rem(here, RADIX) * rows
    for nth in range(count):
        row, col = lit_offsets(params_ref, leds, nth)

        def tile(at):
            position = first + at.start + lax.broadcasted_iota(jnp.int32, (ROW_TILE, length), 0)
            owned = (position < row).astype(jnp.int32) == upper
            for index in range(2):
                whole = [stage_ref[d, nth, index, at] for d in range(blocks)]
                whole = pltpu.roll(jnp.concatenate(whole, axis=1), lax.rem(col, length), 1)
                pupil_ref[nth, index, at] = jnp.where(owned, whole, 0.0)

        over_rows(rows, tile)


def columns_kernel(leds, chunk, groups, params_ref, real_ref, imag_ref, table_ref, *refs):
    here = place_of(params_ref, leds)
    out_ref, pair_ref = refs[-2:]
    if chunk == 0:
        got_refs, amplitude_ref = refs[:groups], refs[groups]
        out_refs, (pupil_ref, stage_ref) = refs[groups + 1 : -4], refs[-4:-2]

        @pl.when(pl.program_id(0) == 0)
        def _():
            take_in(got_refs, stage_ref, here)
            window_pupil(leds, params_ref, stage_ref, pupil_ref)
    else:
        pupil_ref, out_refs = refs[0], refs[-2 - groups : -2]
    rows, size_k = real_ref.shape[1:]
    length = size_k // 2
    for nth in range(out_ref.shape[1]):
        _, col = lit_offsets(params_ref, leds, nth)

        def tile(at):
            wrapped = lax.broadcasted_iota(jnp.int32, (ROW_TILE, length), 1) < col
            p_r, p_i = pupil_ref[nth, 0, at], pupil_ref[nth, 1, at]
            w_r = jnp.where(wrapped, real_ref[0, at, length:], real_ref[0, at, :length])
            w_i = jnp.where(wrapped, imag_ref[0, at, length:], imag_ref[0, at, :length])
            x_r = lanes_of(p_r * w_r - p_i * w_i, RADIX)
            x_i = lanes_of(p_r * w_i + p_i * w_r, RADIX)
            sum_r, sum_i = x_r[0] + x_r[2], x_i[0] + x_i[2]
            dif_r, dif_i = x_r[0] - x_r[2], x_i[0] - x_i[2]
            odd_r, odd_i = x_r[1] + x_r[3], x_i[1] + x_i[3]
            rot_r, rot_i = x_i[3] - x_i[1], x_r[1] - x_r[3]
            if chunk == 0:
                pairs = ((sum_r + odd_r, sum_i + odd_i), (dif_r + rot_r, dif_i + rot_i))
            else:
                pairs = ((sum_r - odd_r, sum_i - odd_i), (dif_r - rot_r, dif_i - rot_i))
            for t, pair in enumerate(pairs):
                pair_ref[t, 0, at], pair_ref[t, 1, at] = halves(jnp.concatenate(pair, axis=1))

        over_rows(rows, tile)
        for t in range(2):
            z = dot_right(pair_ref[t], table_ref, t)
            for u, piece in enumerate(lanes_of(z, RADIX)):
                out_ref[RADIX * t + u, nth, 0, :rows] = piece
    if chunk == 0:
        out_ref[:, :, 0, rows:] = amplitude_ref[:, :, 0]
    hand_out(out_ref, out_refs, here)


def rows_kernel(leds, waits, params_ref, table_ref, *refs):
    got_ref, total_ref, pair_ref = refs[-3:]
    groups, count, modes, _, width = got_ref.shape
    levels = total_ref.shape[0]
    take_in(refs[:groups], got_ref, place_of(params_ref, leds))
    refs = refs[groups + waits : -3]
    field_ref, total_refs = refs[0], refs[1 : 1 + levels]
    part = field_ref.shape[1]
    for amplitude_ref in refs[1 + levels :]:
        amplitude_ref[...] = got_ref[:, :, :, part:]
    slots = [(nth, mode) for nth in range(count) for mode in range(modes)]

    def tile(at):
        for n, (nth, mode) in enumerate(slots):
            x = [got_ref[q, nth, mode, at] + got_ref[q + RADIX, nth, mode, at] for q in range(RADIX)]
            even, odd = x[0] + x[2], x[1] + x[3]
            dif, rot = x[0] - x[2], times_i(x[1] - x[3])
            for t, value in enumerate((even + odd, dif + rot, even - odd, dif - rot)):
                lanes = slice(n * width, (n + 1) * width)
                pair_ref[t, 0, at, lanes], pair_ref[t, 1, at, lanes] = halves(value)

    over_rows(part, tile)
    powers = []
    for t in range(RADIX):
        both = dot_left(table_ref, t, pair_ref[t, 0], pair_ref[t, 1])
        power = None
        for n, (a, b) in enumerate(
            zip(lanes_of(both[:part], len(slots)), lanes_of(both[part:], len(slots)))
        ):
            z = a + times_i(b)
            field_ref[t, :, n * width : (n + 1) * width] = z
            power = z * z if power is None else power + z * z
        powers.append(power + pltpu.roll(power, width // 2, 1))
    rows = total_ref.shape[2] // 2
    low = lax.broadcasted_iota(jnp.int32, (part, width), 1) < width // 2
    for pair in range(2):
        packed = jnp.where(low, powers[2 * pair], powers[2 * pair + 1])
        for d in range(groups):
            for z in range(levels):
                first = (d * levels + z) * rows
                total_ref[z, d, pair * rows : (pair + 1) * rows] = packed[first : first + rows]
    level = place_of(params_ref, leds, True)
    for k, ref in enumerate(total_refs):
        ref[...] = total_ref[lax.rem(level + k, levels)]


def rows_back_kernel(leds, params_ref, table_ref, field_ref, *refs):
    factor_ref, out_ref, turn_ref = refs[-3:]
    groups, count, modes, part, width = out_ref.shape
    levels = factor_ref.shape[0]
    level = place_of(params_ref, leds, True)
    for k, ref in enumerate(refs[:levels]):
        factor_ref[lax.rem(level + levels - k, levels)] = ref[...]
    out_refs = refs[levels:-3]
    slots = [(nth, mode) for nth in range(count) for mode in range(modes)]
    rows = factor_ref.shape[2] // 2
    low = lax.broadcasted_iota(jnp.int32, (part, width), 1) < width // 2
    for t in range(RADIX):
        pair = t // 2
        packed = jnp.concatenate(
            [
                factor_ref[z, d, pair * rows : (pair + 1) * rows]
                for d in range(groups)
                for z in range(levels)
            ],
            axis=0,
        )
        turned = pltpu.roll(packed, width // 2, 1)
        factor = jnp.where(low, packed, turned) if t % 2 == 0 else jnp.where(low, turned, packed)
        diff = jnp.concatenate([x * factor for x in lanes_of(field_ref[t], len(slots))], axis=1)
        both = dot_left(table_ref, t, *halves(diff))
        for n, (a, b) in enumerate(
            zip(lanes_of(both[:part], len(slots)), lanes_of(both[part:], len(slots)))
        ):
            turn_ref[t, :, n * width : (n + 1) * width] = a - times_i(b)

    def tile(at):
        for n, (nth, mode) in enumerate(slots):
            v = [turn_ref[t, at, n * width : (n + 1) * width] for t in range(RADIX)]
            even, odd = v[0] + v[2], v[1] + v[3]
            dif, rot = v[0] - v[2], times_i(v[1] - v[3])
            for q, value in enumerate((even + odd, dif - rot, even - odd, dif + rot)):
                out_ref[q, nth, mode, at] = value
                out_ref[q + RADIX, nth, mode, at] = value

    over_rows(part, tile)
    hand_out(out_ref, out_refs, place_of(params_ref, leds))


def columns_back_kernel(leds, chunk, groups, params_ref, real_ref, imag_ref, table_ref, *refs):
    out_r, out_i, got_ref, pair_ref, turn_ref = refs[-5:]
    take_in(refs[:groups], got_ref, place_of(params_ref, leds))
    pupil_ref = refs[groups]
    count = got_ref.shape[1]
    rows, size_k = real_ref.shape[1:]
    length = size_k // 2
    for nth in range(count):
        for t in range(2):

            def split(at):
                z = [got_ref[RADIX * t + n, nth, 0, at] for n in range(RADIX)]
                pair_ref[t, 0, at], pair_ref[t, 1, at] = halves(jnp.concatenate(z, axis=1))

            over_rows(rows, split)
            turn_ref[nth, t] = dot_right(pair_ref[t], table_ref, t)

    def tile(at):
        totals = [[ref[0, at, :length], ref[0, at, length:]] for ref in (real_ref, imag_ref)]
        for nth in range(count):
            _, col = lit_offsets(params_ref, leds, nth)
            wrapped = lax.broadcasted_iota(jnp.int32, (ROW_TILE, length), 1) < col
            p_r, p_i = pupil_ref[nth, 0, at], pupil_ref[nth, 1, at]
            (a_r, a_i), (b_r, b_i) = [lanes_of(turn_ref[nth, t, at], 2) for t in range(2)]
            if chunk == 0:
                x_r = [a_r + b_r, a_r + b_i, a_r - b_r, a_r - b_i]
                x_i = [a_i + b_i, a_i - b_r, a_i - b_i, a_i + b_r]
            else:
                x_r = [a_r + b_r, -a_r - b_i, a_r - b_r, b_i - a_r]
                x_i = [a_i + b_i, b_r - a_i, a_i - b_i, -a_i - b_r]
            x_r, x_i = jnp.concatenate(x_r, axis=1), jnp.concatenate(x_i, axis=1)
            for total, delta in zip(totals, (p_r * x_r + p_i * x_i, p_r * x_i - p_i * x_r)):
                total[0] = total[0] + jnp.where(wrapped, 0.0, delta)
                total[1] = total[1] + jnp.where(wrapped, delta, 0.0)
        for out, total in zip((out_r, out_i), totals):
            out[0, at, :length] = total[0]
            out[0, at, length:] = total[1]

    over_rows(rows, tile)


SMEM_SPEC = pl.BlockSpec(memory_space=pltpu.SMEM)
ANY_SPEC = pl.BlockSpec(memory_space=pl.ANY)


def room(count):
    return pltpu.CompilerParams(vmem_limit_bytes=(16 + 16 * count) * 1024 * 1024)


CHUNKS = 2


def fixed(shape):
    zeros = (0,) * len(shape)
    return pl.BlockSpec(shape, lambda *_: zeros)


def one_mode(shape):
    before = len(shape) - 3
    block = shape[:before] + (1,) + shape[before + 1 :]
    return pl.BlockSpec(block, lambda i: (0,) * before + (i, 0, 0))


def cost(macs, *arrays):
    moved = sum(math.prod(a.shape) * a.dtype.itemsize for a in arrays)
    return pl.CostEstimate(flops=2 * macs, bytes_accessed=moved, transcendentals=0)


def shaped(shape):
    return jax.ShapeDtypeStruct(shape, jnp.float32)


def exchange(blocks):
    places = range(len(blocks))
    return [blocks[0]] + [
        lax.ppermute(blocks[k], "rows", [(d, d ^ k) for d in places]) for k in places[1:]
    ]


def around(levels, value_of):
    ring = range(levels)
    return [value_of(0)] + [
        lax.ppermute(value_of(k), "mode", [(z, (z + k) % levels) for z in ring]) for k in ring[1:]
    ]


def amplitude_kernel(leds, params_ref, measured_ref, out_ref):
    groups, rows, lanes = out_ref.shape
    width, length = measured_ref.shape[1:]
    columns = lanes // 2
    depth = rows // RADIX
    first = place_of(params_ref, leds, True) * rows

    def pick(x, y, turned):
        total = None
        for _ in range(3):
            x_part = x.astype(jnp.bfloat16)
            x = x - x_part.astype(jnp.float32)
            piece = dot(y, x_part) if turned else dot(x_part, y)
            total = piece if total is None else total + piece
        return total

    def ones_where(condition):
        return jnp.where(condition, 1.0, 0.0).astype(jnp.bfloat16)

    order = lax.broadcasted_iota(jnp.int32, (rows, width), 0)
    source = RADIX * (order % depth) + 2 * ((order // depth) % 2) + order // (2 * depth)
    taken = lax.broadcasted_iota(jnp.int32, (rows, width), 1) == source + first
    mine = pick(measured_ref[0], ones_where(taken), True)
    part = length // RADIX
    from_col = lax.broadcasted_iota(jnp.int32, (length, part), 0)
    to_col = lax.broadcasted_iota(jnp.int32, (length, part), 1)
    half = rows // 2
    for t in range(RADIX):
        chunk, side = t // 2, t % 2
        found = pick(mine, ones_where(from_col == RADIX * to_col + t), False)
        for u, piece in enumerate(lanes_of(found, RADIX)):
            out_ref[RADIX * side + u, chunk * half : (chunk + 1) * half] = jnp.concatenate(
                [piece[:half], piece[half:]], axis=1
            )


def fast_body(object_real, object_imag, pupil_real, pupil_imag, measured, source_mask, offsets):
    width, length = pupil_real.shape
    modes, local_rows, size_k = object_real.shape
    groups, levels = lax.axis_size("rows"), lax.axis_size("mode")
    part = length // RADIX
    leds = offsets.shape[0]
    tables = [jnp.asarray(table) for table in radix_tables(length)]
    position = jnp.stack([lax.axis_index("rows"), lax.axis_index("mode")]).astype(jnp.int32)
    params = jnp.concatenate([source_mask.reshape(-1), offsets.reshape(-1), position])
    spectrum = pl.BlockSpec((1, local_rows, size_k), lambda i: (i, 0, 0))

    def update(count):
        slots = count * modes
        dft_macs = 3 * slots * 2 * 4 * part * part * local_rows
        pupil_shape = (count, 2, local_rows, width)
        block_shape = (count, modes, local_rows, width)
        half_table = (2, RADIX // CHUNKS) + tables[0].shape[2:]
        by_mode = (count, 1) + block_shape[2:]
        pupil_stage = pltpu.VMEM((groups,) + pupil_shape, jnp.float32)

        def columns(chunk, pupil, others):
            extra = others.shape[1] // slots if chunk == 0 else 0
            out = shaped(block_shape[:2] + (local_rows + extra, width))
            whole = shaped((count, 2, local_rows, length))
            operands = [params, object_real, object_imag, tables[0], *pupil]
            specs = [
                SMEM_SPEC,
                spectrum,
                spectrum,
                pl.BlockSpec(half_table, lambda i: (0, chunk, 0, 0)),
            ]
            outs, out_specs = (out,) * groups, (one_mode(out.shape),) * groups
            scratch = [
                pltpu.VMEM((groups, count, 1) + out.shape[2:], jnp.float32),
                pltpu.VMEM((2, 2, local_rows, 2 * part), jnp.bfloat16),
            ]
            if chunk == 0:
                others = others.reshape(groups, count, modes, extra, width)
                specs += [fixed(pupil_shape)] * groups + [one_mode(others.shape)]
                outs, out_specs = outs + (whole,), out_specs + (fixed(whole.shape),)
                scratch = [pupil_stage] + scratch
            else:
                specs += [fixed(whole.shape), ANY_SPEC]
            sent = pl.pallas_call(
                functools.partial(columns_kernel, leds, chunk, groups),
                out_shape=outs,
                grid=(modes,),
                in_specs=specs,
                out_specs=out_specs,
                scratch_shapes=scratch,
                compiler_params=room(count),
                cost_estimate=cost(dft_macs, *[out] * 16, object_real, object_imag),
                name="columns",
            )(*operands, others)
            return exchange(sent[:groups]), sent[groups:]

        def rows(got, waits):
            field = shaped((RADIX, part, slots * width))
            total = shaped((groups, 2 * part // groups // levels, width))
            extra = got[0].shape[2] - local_rows
            outs = (field,) + (total,) * levels
            if extra > 0:
                outs += (shaped((groups, count, modes, extra, width)),)
            return pl.pallas_call(
                functools.partial(rows_kernel, leds, len(waits)),
                out_shape=outs,
                grid=(1,),
                in_specs=[SMEM_SPEC, fixed(tables[1].shape)]
                + [fixed(got[0].shape)] * groups
                + [ANY_SPEC] * len(waits),
                out_specs=tuple(fixed(out.shape) for out in outs),
                scratch_shapes=[
                    pltpu.VMEM((groups,) + got[0].shape, jnp.float32),
                    pltpu.VMEM((levels,) + total.shape, jnp.float32),
                    pltpu.VMEM((RADIX, 2, part, slots * width), jnp.bfloat16),
                ],
                compiler_params=room(count),
                cost_estimate=cost(dft_macs, *got, field),
                name="rows",
            )(params, tables[1], *got, *waits)

        def rows_back(field, factor):
            out = shaped(block_shape)
            sent = pl.pallas_call(
                functools.partial(rows_back_kernel, leds),
                out_shape=(out,) * groups,
                grid=(1,),
                in_specs=[SMEM_SPEC, fixed(tables[2].shape), fixed(field.shape)]
                + [fixed(factor[0].shape)] * levels,
                out_specs=(fixed(block_shape),) * groups,
                scratch_shapes=[
                    pltpu.VMEM((levels,) + factor[0].shape, jnp.float32),
                    pltpu.VMEM((groups,) + block_shape, jnp.float32),
                    pltpu.VMEM(field.shape, jnp.float32),
                ],
                compiler_params=room(count),
                cost_estimate=cost(dft_macs, *[out] * groups, field),
                name="rows_back",
            )(params, tables[2], field, *factor)
            return exchange(sent), sent[0]

        def columns_back(chunk, pupil, got, current, wait):
            out = shaped(object_real.shape)
            return pl.pallas_call(
                functools.partial(columns_back_kernel, leds, chunk, groups),
                out_shape=(out, out),
                grid=(modes,),
                in_specs=[
                    SMEM_SPEC,
                    spectrum,
                    spectrum,
                    pl.BlockSpec(half_table, lambda i: (0, chunk, 0, 0)),
                ]
                + [one_mode(block_shape)] * groups
                + [fixed(pupil.shape), ANY_SPEC],
                out_specs=(spectrum, spectrum),
                scratch_shapes=[
                    pltpu.VMEM((groups,) + by_mode, jnp.float32),
                    pltpu.VMEM((2, 2, local_rows, 2 * part), jnp.bfloat16),
                    pltpu.VMEM((count, 2, local_rows, 2 * part), jnp.float32),
                ],
                input_output_aliases={1: 0, 2: 1} if chunk > 0 else {},
                compiler_params=room(count),
                cost_estimate=cost(dft_macs, *got, pupil, out, out, out, out),
                name="columns_back",
            )(params, *current, tables[3], *got, pupil, wait)

        def run(*_):
            amplitude = shaped((groups, width // levels, width))
            amplitude = pl.pallas_call(
                functools.partial(amplitude_kernel, leds),
                out_shape=amplitude,
                grid=(1,),
                in_specs=[SMEM_SPEC, fixed(measured.shape)],
                out_specs=fixed(amplitude.shape),
                compiler_params=room(count),
                cost_estimate=cost(3 * length * length * RADIX * 8, amplitude, measured),
                name="amplitude",
            )(params, measured)
            out = shaped(pupil_shape)
            sent = pl.pallas_call(
                functools.partial(pupil_send_kernel, leds),
                out_shape=(out,) * groups,
                grid=(1,),
                in_specs=[SMEM_SPEC] + [fixed(pupil_real.shape)] * 2,
                out_specs=(fixed(pupil_shape),) * groups,
                scratch_shapes=[pupil_stage],
                compiler_params=room(count),
                cost_estimate=cost(0, *[out] * groups, pupil_real, pupil_imag),
                name="pupil_send",
            )(params, pupil_real, pupil_imag)
            got, (pupil,) = columns(0, exchange(sent), amplitude)
            got = [got, columns(1, [pupil], got[min(2, groups - 1)])[0]]
            back, waits = [], []
            for chunk in range(CHUNKS):
                field, *totals = rows(got[chunk], waits)
                if chunk == 0:
                    mine = totals.pop().reshape(groups, width // levels, width)
                share = sum(around(levels, lambda k: totals[k]))
                deep = share.shape[1]
                ratio = mine[:, chunk * deep : (chunk + 1) * deep] / jnp.sqrt(share + FLOOR_TERM)
                factor = around(levels, lambda k: ratio - 1.0)
                blocks, wait = rows_back(field, factor)
                back.append(blocks)
                waits = [wait]
            current = (object_real, object_imag)
            for chunk in range(CHUNKS):
                current = columns_back(chunk, pupil, back[chunk], current, wait)
            return tuple(current)

        return run

    lit = jnp.sum((source_mask[0] != 0).astype(jnp.int32))
    most = max(leds - 1, 1)
    if most == 1:
        return update(1)()
    return lax.switch(jnp.clip(lit - 1, 0, most - 1), [update(n + 1) for n in range(most)])


def fits_fast(mesh, object_shape, pupil_shape, leds):
    groups, levels = mesh.shape["rows"], mesh.shape["mode"]
    length, size_k = pupil_shape[1], object_shape[2]
    modes, local_rows, width = object_shape[0] // levels, size_k // groups, length // groups
    amplitude_rows = width // levels
    return (
        size_k == 2 * length
        and groups == 2 * RADIX
        and levels == RADIX
        and local_rows % 256 == 0
        and width % 128 == 0
        and all(amplitude_rows % (8 * modes * n) == 0 for n in range(1, max(leds, 2)))
    )


def solution(mesh):
    in_specs = (
        P("mode", "rows", None),
        P("mode", "rows", None),
        P("rows", None),
        P("rows", None),
        P(None, "rows", None),
        P(),
        P(),
    )
    out_specs = (P("mode", "rows", None), P("mode", "rows", None))

    def chosen(object_real, object_imag, pupil_real, *others):
        fast = fits_fast(mesh, object_real.shape, pupil_real.shape, others[-1].shape[0])
        mapped = jax.shard_map(
            fast_body if fast else body,
            mesh=mesh,
            in_specs=in_specs,
            out_specs=out_specs,
            check_vma=False,
        )
        return mapped(object_real, object_imag, pupil_real, *others)

    return chosen
```

```python
import functools
import math

import jax
import jax.numpy as jnp
import ml_dtypes
import numpy as np
from jax import lax
from jax.experimental import pallas as pl
from jax.experimental.pallas import tpu as pltpu
from jax.sharding import PartitionSpec as P

FLOOR_TERM = 0.5
HIGHEST_PREC = lax.Precision.HIGHEST


def dft_tables(length):
    indices = jnp.arange(length, dtype=jnp.int32)
    phases = indices[:, None] * indices[None, :] % length
    angles = phases.astype(jnp.float32) * (2.0 * math.pi / length)
    scale_factor = 1.0 / math.sqrt(length)
    cos_table = jnp.cos(angles) * scale_factor
    sin_table = jnp.sin(angles) * scale_factor
    return (
        jnp.concatenate([cos_table, sin_table], axis=1),
        jnp.concatenate([cos_table, sin_table], axis=0),
    )


def transform(form, table, real_part, imag_part, axis, direction_sign):
    result = jnp.einsum(form, jnp.stack([real_part, imag_part]), table, precision=HIGHEST_PREC)
    length = result.shape[axis] // 2
    with_cos = lax.slice_in_dim(result, 0, length, axis=axis)
    with_sin = lax.slice_in_dim(result, length, 2 * length, axis=axis)
    return (with_cos[0] - direction_sign * with_sin[1], with_cos[1] + direction_sign * with_sin[0])


def right_product(real_part, imag_part, wide_cols, direction_sign):
    return transform("smlck,kj->smlcj", wide_cols, real_part, imag_part, 4, direction_sign)


def forward_fields(
    part_real, part_imag, pupil_real, pupil_imag, offsets, wide_cols, wide_rows, length
):
    source_count = offsets.shape[0]
    groups = lax.axis_size("rows")
    crop_real = jnp.stack(
        [
            lax.dynamic_slice_in_dim(part_real, offsets[source_index, 1], length, 2)
            for source_index in range(source_count)
        ],
        axis=1,
    )
    crop_imag = jnp.stack(
        [
            lax.dynamic_slice_in_dim(part_imag, offsets[source_index, 1], length, 2)
            for source_index in range(source_count)
        ],
        axis=1,
    )
    got_real, got_imag = (
        lax.all_to_all(
            jnp.swapaxes(crop_real, 2, 3), "rows", split_axis=2, concat_axis=3, tiled=True
        ),
        lax.all_to_all(
            jnp.swapaxes(crop_imag, 2, 3), "rows", split_axis=2, concat_axis=3, tiled=True
        ),
    )
    win_real = jnp.stack(
        [
            lax.dynamic_slice_in_dim(got_real[:, source_index], offsets[source_index, 0], length, 2)
            for source_index in range(source_count)
        ],
        axis=1,
    )
    win_imag = jnp.stack(
        [
            lax.dynamic_slice_in_dim(got_imag[:, source_index], offsets[source_index, 0], length, 2)
            for source_index in range(source_count)
        ],
        axis=1,
    )
    lifted_real = pupil_real * win_real - pupil_imag * win_imag
    lifted_imag = pupil_real * win_imag + pupil_imag * win_real
    half_real, half_imag = transform("smlcr,yr->smlyc", wide_rows, lifted_real, lifted_imag, 3, 1.0)
    layout = half_real.shape
    blocked = (layout[0], layout[1], groups, layout[2] // groups, layout[3])
    back_real, back_imag = (
        lax.all_to_all(half_real.reshape(blocked), "rows", split_axis=2, concat_axis=4, tiled=True),
        lax.all_to_all(half_imag.reshape(blocked), "rows", split_axis=2, concat_axis=4, tiled=True),
    )
    flat = (layout[0], layout[1], layout[2] // groups, layout[3] * groups)
    return right_product(back_real.reshape(flat), back_imag.reshape(flat), wide_cols, 1.0)


def spectral_updates(diff_real, diff_imag, pupil_real, pupil_imag, offsets, wide_cols, size_k):
    source_count = offsets.shape[0]
    groups = lax.axis_size("rows")
    col_real, col_imag = right_product(diff_real, diff_imag, wide_cols, -1.0)
    layout = col_real.shape
    blocked = (layout[0], layout[1], layout[2], groups, layout[3] // groups)
    got_real, got_imag = (
        lax.all_to_all(col_real.reshape(blocked), "rows", split_axis=3, concat_axis=2, tiled=True),
        lax.all_to_all(col_imag.reshape(blocked), "rows", split_axis=3, concat_axis=2, tiled=True),
    )
    flat = (layout[0], layout[1], layout[2] * groups, layout[3] // groups)
    full_real = got_real.reshape(flat)
    full_imag = got_imag.reshape(flat)
    delta_real, delta_imag = transform("smlyc,yk->smlck", wide_cols, full_real, full_imag, 4, -1.0)
    upd_real = pupil_real * delta_real + pupil_imag * delta_imag
    upd_imag = pupil_real * delta_imag - pupil_imag * delta_real
    blank = jnp.zeros((layout[0], layout[3] // groups, size_k), jnp.float32)
    placed_real = jnp.stack(
        [
            lax.dynamic_update_slice_in_dim(
                blank, upd_real[:, source_index], offsets[source_index, 0], 2
            )
            for source_index in range(source_count)
        ],
        axis=1,
    )
    placed_imag = jnp.stack(
        [
            lax.dynamic_update_slice_in_dim(
                blank, upd_imag[:, source_index], offsets[source_index, 0], 2
            )
            for source_index in range(source_count)
        ],
        axis=1,
    )
    return (
        lax.all_to_all(placed_real, "rows", split_axis=3, concat_axis=2, tiled=True),
        lax.all_to_all(placed_imag, "rows", split_axis=3, concat_axis=2, tiled=True),
    )


def add_window(target, incoming, start_col, length):
    current = lax.dynamic_slice_in_dim(target, start_col, length, 2)
    return lax.dynamic_update_slice_in_dim(
        target, current + jnp.swapaxes(incoming, 1, 2), start_col, 2
    )


def body(object_real, object_imag, pupil_real, pupil_imag, measured, source_mask, offsets):
    length = pupil_real.shape[1]
    size_k = object_real.shape[2]
    source_count = offsets.shape[0]
    wide_cols, wide_rows = dft_tables(length)
    spec_real, spec_imag = (object_real, object_imag)
    weights = source_mask[0].astype(jnp.float32)
    field_real, field_imag = forward_fields(
        spec_real, spec_imag, pupil_real, pupil_imag, offsets, wide_cols, wide_rows, length
    )
    powers = jnp.sum(field_real * field_real + field_imag * field_imag, axis=0)
    partial_sum = jnp.tensordot(weights, powers, axes=1)
    share = lax.psum_scatter(partial_sum, "mode", scatter_dimension=0, tiled=True)
    share_rows = share.shape[0]
    measured_share = lax.dynamic_slice_in_dim(
        measured[0], lax.axis_index("mode") * share_rows, share_rows, 0
    )
    ratio_share = measured_share / jnp.sqrt(share + FLOOR_TERM)
    ratios = lax.all_gather(ratio_share, "mode", axis=0, tiled=True)
    factor = (ratios - 1.0)[None, None] * weights[None, :, None, None]
    diff_real = field_real * factor
    diff_imag = field_imag * factor
    ret_real, ret_imag = spectral_updates(
        diff_real, diff_imag, pupil_real, pupil_imag, offsets, wide_cols, size_k
    )
    for source_index in range(source_count):
        start_col = offsets[source_index, 1]
        spec_real = add_window(spec_real, ret_real[:, source_index], start_col, length)
        spec_imag = add_window(spec_imag, ret_imag[:, source_index], start_col, length)
    return (spec_real, spec_imag)


RADIX = 4
ROW_TILE = 64


def split_pair(table):
    high = table.astype(ml_dtypes.bfloat16)
    low = (table - high.astype(np.float64)).astype(ml_dtypes.bfloat16)
    return np.stack([high, low])


def radix_tables(length):
    part = length // RADIX
    t = np.arange(RADIX)[:, None, None]
    r = np.arange(part)[None, :, None]
    s = np.arange(part)[None, None, :]
    angles = (r * (t + RADIX * s) % length) * (2.0 * np.pi / length)
    cos_t = np.cos(angles) / np.sqrt(length)
    sin_t = np.sin(angles) / np.sqrt(length)
    swap = lambda x: np.swapaxes(x, 1, 2)
    width = part // RADIX
    pieces = lambda x: x.reshape(RADIX, part, RADIX, width)
    beside = lambda x, y: np.stack([pieces(x), pieces(y)], axis=3).reshape(RADIX, part, 2 * part)
    columns = np.concatenate([beside(cos_t, sin_t), beside(-sin_t, cos_t)], axis=1)
    columns_back = np.swapaxes(columns, 1, 2)
    rows = np.concatenate([swap(cos_t), swap(sin_t)], axis=1)
    rows_back = np.concatenate([cos_t, sin_t], axis=1)
    return tuple(split_pair(table) for table in (columns, rows, rows_back, columns_back))


def halves(x):
    high = x.astype(jnp.bfloat16)
    low = (x - high.astype(jnp.float32)).astype(jnp.bfloat16)
    return high, low


def dot(a, b):
    return jnp.dot(a, b, preferred_element_type=jnp.float32)


def dot_right(pair_ref, table_ref, t):
    high, low = pair_ref[0], pair_ref[1]
    return dot(high, table_ref[0, t]) + dot(low, table_ref[0, t]) + dot(high, table_ref[1, t])


def dot_left(table_ref, t, high, low):
    return dot(table_ref[0, t], high) + dot(table_ref[0, t], low) + dot(table_ref[1, t], high)


def over_rows(rows, step):
    def one(i, _):
        step(pl.ds(pl.multiple_of(i * ROW_TILE, ROW_TILE), ROW_TILE))
        return 0

    lax.fori_loop(0, rows // ROW_TILE, one, 0)


def lanes_of(x, slots):
    width = x.shape[1] // slots
    return [x[:, n * width : (n + 1) * width] for n in range(slots)]


def times_i(x):
    half = x.shape[1] // 2
    turned = pltpu.roll(x, half, 1)
    return jnp.where(lax.broadcasted_iota(jnp.int32, x.shape, 1) < half, -turned, turned)


def lit_offsets(params_ref, leds, nth):
    row, col, seen = jnp.int32(0), jnp.int32(0), jnp.int32(0)
    for led in range(leds):
        lit = params_ref[led] != 0
        take = jnp.logical_and(lit, seen == nth)
        row = jnp.where(take, params_ref[leds + 2 * led], row)
        col = jnp.where(take, params_ref[leds + 2 * led + 1], col)
        seen = seen + lit.astype(jnp.int32)
    return row, col


def place_of(params_ref, leds, levels=False):
    return params_ref[3 * leds + (1 if levels else 0)]


def hand_out(stage_ref, out_refs, here):
    for k, out_ref in enumerate(out_refs):
        out_ref[...] = stage_ref[jnp.bitwise_xor(here, k)]


def take_in(got_refs, stage_ref, here):
    for k, got_ref in enumerate(got_refs):
        stage_ref[jnp.bitwise_xor(here, k)] = got_ref[...]


def pupil_send_kernel(leds, params_ref, real_ref, imag_ref, *refs):
    out_refs, out_ref = refs[:-1], refs[-1]
    length = real_ref.shape[1]
    part = length // RADIX
    for nth in range(out_ref.shape[1]):
        row, _ = lit_offsets(params_ref, leds, nth)
        for index, ref in enumerate((real_ref, imag_ref)):
            rolled = pltpu.roll(ref[...], lax.rem(row, length), 1)
            for q in range(RADIX):
                block = rolled[:, q * part : (q + 1) * part].T
                out_ref[q, nth, index] = block
                out_ref[q + RADIX, nth, index] = block
    hand_out(out_ref, out_refs, place_of(params_ref, leds))


def window_pupil(leds, params_ref, stage_ref, pupil_ref):
    here = place_of(params_ref, leds)
    blocks, count, _, rows, width = stage_ref.shape
    length = blocks * width
    upper, first = here // RADIX, lax.rem(here, RADIX) * rows
    for nth in range(count):
        row, col = lit_offsets(params_ref, leds, nth)

        def tile(at):
            position = first + at.start + lax.broadcasted_iota(jnp.int32, (ROW_TILE, length), 0)
            owned = (position < row).astype(jnp.int32) == upper
            for index in range(2):
                whole = [stage_ref[d, nth, index, at] for d in range(blocks)]
                whole = pltpu.roll(jnp.concatenate(whole, axis=1), lax.rem(col, length), 1)
                pupil_ref[nth, index, at] = jnp.where(owned, whole, 0.0)

        over_rows(rows, tile)


def columns_kernel(leds, chunk, groups, params_ref, real_ref, imag_ref, table_ref, *refs):
    here = place_of(params_ref, leds)
    out_ref, pair_ref = refs[-2:]
    if chunk == 0:
        got_refs, amplitude_ref = refs[:groups], refs[groups]
        out_refs, (pupil_ref, stage_ref) = refs[groups + 1 : -4], refs[-4:-2]

        @pl.when(pl.program_id(0) == 0)
        def _():
            take_in(got_refs, stage_ref, here)
            window_pupil(leds, params_ref, stage_ref, pupil_ref)
    else:
        pupil_ref, out_refs = refs[0], refs[-2 - groups : -2]
    rows, size_k = real_ref.shape[1:]
    length = size_k // 2
    for nth in range(out_ref.shape[1]):
        _, col = lit_offsets(params_ref, leds, nth)

        def tile(at):
            wrapped = lax.broadcasted_iota(jnp.int32, (ROW_TILE, length), 1) < col
            p_r, p_i = pupil_ref[nth, 0, at], pupil_ref[nth, 1, at]
            w_r = jnp.where(wrapped, real_ref[0, at, length:], real_ref[0, at, :length])
            w_i = jnp.where(wrapped, imag_ref[0, at, length:], imag_ref[0, at, :length])
            x_r = lanes_of(p_r * w_r - p_i * w_i, RADIX)
            x_i = lanes_of(p_r * w_i + p_i * w_r, RADIX)
            sum_r, sum_i = x_r[0] + x_r[2], x_i[0] + x_i[2]
            dif_r, dif_i = x_r[0] - x_r[2], x_i[0] - x_i[2]
            odd_r, odd_i = x_r[1] + x_r[3], x_i[1] + x_i[3]
            rot_r, rot_i = x_i[3] - x_i[1], x_r[1] - x_r[3]
            if chunk == 0:
                pairs = ((sum_r + odd_r, sum_i + odd_i), (dif_r + rot_r, dif_i + rot_i))
            else:
                pairs = ((sum_r - odd_r, sum_i - odd_i), (dif_r - rot_r, dif_i - rot_i))
            for t, pair in enumerate(pairs):
                pair_ref[t, 0, at], pair_ref[t, 1, at] = halves(jnp.concatenate(pair, axis=1))

        over_rows(rows, tile)
        for t in range(2):
            z = dot_right(pair_ref[t], table_ref, t)
            for u, piece in enumerate(lanes_of(z, RADIX)):
                out_ref[RADIX * t + u, nth, 0, :rows] = piece
    if chunk == 0:
        out_ref[:, :, 0, rows:] = amplitude_ref[:, :, 0]
    hand_out(out_ref, out_refs, here)


def rows_kernel(leds, waits, params_ref, table_ref, *refs):
    got_ref, pair_ref = refs[-2:]
    groups, count, modes, _, width = got_ref.shape
    take_in(refs[:groups], got_ref, place_of(params_ref, leds))
    refs = refs[groups + waits : -2]
    field_ref, total_ref = refs[:2]
    levels, part = total_ref.shape[0], field_ref.shape[1]
    for amplitude_ref in refs[2:]:
        amplitude_ref[...] = got_ref[:, :, :, part:]
    slots = [(nth, mode) for nth in range(count) for mode in range(modes)]

    def tile(at):
        for n, (nth, mode) in enumerate(slots):
            x = [got_ref[q, nth, mode, at] + got_ref[q + RADIX, nth, mode, at] for q in range(RADIX)]
            even, odd = x[0] + x[2], x[1] + x[3]
            dif, rot = x[0] - x[2], times_i(x[1] - x[3])
            for t, value in enumerate((even + odd, dif + rot, even - odd, dif - rot)):
                lanes = slice(n * width, (n + 1) * width)
                pair_ref[t, 0, at, lanes], pair_ref[t, 1, at, lanes] = halves(value)

    over_rows(part, tile)
    powers = []
    for t in range(RADIX):
        both = dot_left(table_ref, t, pair_ref[t, 0], pair_ref[t, 1])
        power = None
        for n, (a, b) in enumerate(
            zip(lanes_of(both[:part], len(slots)), lanes_of(both[part:], len(slots)))
        ):
            z = a + times_i(b)
            field_ref[t, :, n * width : (n + 1) * width] = z
            power = z * z if power is None else power + z * z
        powers.append(power + pltpu.roll(power, width // 2, 1))
    rows = total_ref.shape[2] // 2
    low = lax.broadcasted_iota(jnp.int32, (part, width), 1) < width // 2
    for pair in range(2):
        packed = jnp.where(low, powers[2 * pair], powers[2 * pair + 1])
        for d in range(groups):
            for z in range(levels):
                first = (d * levels + z) * rows
                total_ref[z, d, pair * rows : (pair + 1) * rows] = packed[first : first + rows]


def rows_back_kernel(leds, params_ref, table_ref, field_ref, factor_ref, *refs):
    out_refs, (out_ref, turn_ref) = refs[:-2], refs[-2:]
    groups, count, modes, part, width = out_ref.shape
    levels = factor_ref.shape[0]
    slots = [(nth, mode) for nth in range(count) for mode in range(modes)]
    rows = factor_ref.shape[2] // 2
    low = lax.broadcasted_iota(jnp.int32, (part, width), 1) < width // 2
    for t in range(RADIX):
        pair = t // 2
        packed = jnp.concatenate(
            [
                factor_ref[z, d, pair * rows : (pair + 1) * rows]
                for d in range(groups)
                for z in range(levels)
            ],
            axis=0,
        )
        turned = pltpu.roll(packed, width // 2, 1)
        factor = jnp.where(low, packed, turned) if t % 2 == 0 else jnp.where(low, turned, packed)
        diff = jnp.concatenate([x * factor for x in lanes_of(field_ref[t], len(slots))], axis=1)
        both = dot_left(table_ref, t, *halves(diff))
        for n, (a, b) in enumerate(
            zip(lanes_of(both[:part], len(slots)), lanes_of(both[part:], len(slots)))
        ):
            turn_ref[t, :, n * width : (n + 1) * width] = a - times_i(b)

    def tile(at):
        for n, (nth, mode) in enumerate(slots):
            v = [turn_ref[t, at, n * width : (n + 1) * width] for t in range(RADIX)]
            even, odd = v[0] + v[2], v[1] + v[3]
            dif, rot = v[0] - v[2], times_i(v[1] - v[3])
            for q, value in enumerate((even + odd, dif - rot, even - odd, dif + rot)):
                out_ref[q, nth, mode, at] = value
                out_ref[q + RADIX, nth, mode, at] = value

    over_rows(part, tile)
    hand_out(out_ref, out_refs, place_of(params_ref, leds))


def columns_back_kernel(leds, chunk, groups, params_ref, real_ref, imag_ref, table_ref, *refs):
    out_r, out_i, got_ref, pair_ref, turn_ref = refs[-5:]
    take_in(refs[:groups], got_ref, place_of(params_ref, leds))
    pupil_ref = refs[groups]
    count = got_ref.shape[1]
    rows, size_k = real_ref.shape[1:]
    length = size_k // 2
    for nth in range(count):
        for t in range(2):

            def split(at):
                z = [got_ref[RADIX * t + n, nth, 0, at] for n in range(RADIX)]
                pair_ref[t, 0, at], pair_ref[t, 1, at] = halves(jnp.concatenate(z, axis=1))

            over_rows(rows, split)
            turn_ref[nth, t] = dot_right(pair_ref[t], table_ref, t)

    def tile(at):
        totals = [[ref[0, at, :length], ref[0, at, length:]] for ref in (real_ref, imag_ref)]
        for nth in range(count):
            _, col = lit_offsets(params_ref, leds, nth)
            wrapped = lax.broadcasted_iota(jnp.int32, (ROW_TILE, length), 1) < col
            p_r, p_i = pupil_ref[nth, 0, at], pupil_ref[nth, 1, at]
            (a_r, a_i), (b_r, b_i) = [lanes_of(turn_ref[nth, t, at], 2) for t in range(2)]
            if chunk == 0:
                x_r = [a_r + b_r, a_r + b_i, a_r - b_r, a_r - b_i]
                x_i = [a_i + b_i, a_i - b_r, a_i - b_i, a_i + b_r]
            else:
                x_r = [a_r + b_r, -a_r - b_i, a_r - b_r, b_i - a_r]
                x_i = [a_i + b_i, b_r - a_i, a_i - b_i, -a_i - b_r]
            x_r, x_i = jnp.concatenate(x_r, axis=1), jnp.concatenate(x_i, axis=1)
            for total, delta in zip(totals, (p_r * x_r + p_i * x_i, p_r * x_i - p_i * x_r)):
                total[0] = total[0] + jnp.where(wrapped, 0.0, delta)
                total[1] = total[1] + jnp.where(wrapped, delta, 0.0)
        for out, total in zip((out_r, out_i), totals):
            out[0, at, :length] = total[0]
            out[0, at, length:] = total[1]

    over_rows(rows, tile)


SMEM_SPEC = pl.BlockSpec(memory_space=pltpu.SMEM)
ANY_SPEC = pl.BlockSpec(memory_space=pl.ANY)


def room(count):
    return pltpu.CompilerParams(vmem_limit_bytes=(16 + 16 * count) * 1024 * 1024)


CHUNKS = 2
WAIT_BLOCK = 2


def fixed(shape):
    zeros = (0,) * len(shape)
    return pl.BlockSpec(shape, lambda *_: zeros)


def one_mode(shape):
    before = len(shape) - 3
    block = shape[:before] + (1,) + shape[before + 1 :]
    return pl.BlockSpec(block, lambda i: (0,) * before + (i, 0, 0))


def cost(macs, *arrays):
    moved = sum(math.prod(a.shape) * a.dtype.itemsize for a in arrays)
    return pl.CostEstimate(flops=2 * macs, bytes_accessed=moved, transcendentals=0)


def shaped(shape):
    return jax.ShapeDtypeStruct(shape, jnp.float32)


def exchange(blocks):
    places = range(len(blocks))
    return [blocks[0]] + [
        lax.ppermute(blocks[k], "rows", [(d, d ^ k) for d in places]) for k in places[1:]
    ]


def across(shares):
    return lax.all_to_all(shares, "mode", split_axis=0, concat_axis=0, tiled=True)


def amplitude_kernel(leds, params_ref, measured_ref, out_ref):
    groups, rows, lanes = out_ref.shape
    width, length = measured_ref.shape[1:]
    columns = lanes // 2
    depth = rows // RADIX
    first = place_of(params_ref, leds, True) * rows

    def pick(x, y, turned):
        total = None
        for _ in range(3):
            x_part = x.astype(jnp.bfloat16)
            x = x - x_part.astype(jnp.float32)
            piece = dot(y, x_part) if turned else dot(x_part, y)
            total = piece if total is None else total + piece
        return total

    def ones_where(condition):
        return jnp.where(condition, 1.0, 0.0).astype(jnp.bfloat16)

    order = lax.broadcasted_iota(jnp.int32, (rows, width), 0)
    source = RADIX * (order % depth) + 2 * ((order // depth) % 2) + order // (2 * depth)
    taken = lax.broadcasted_iota(jnp.int32, (rows, width), 1) == source + first
    mine = pick(measured_ref[0], ones_where(taken), True)
    part = length // RADIX
    from_col = lax.broadcasted_iota(jnp.int32, (length, part), 0)
    to_col = lax.broadcasted_iota(jnp.int32, (length, part), 1)
    half = rows // 2
    for t in range(RADIX):
        chunk, side = t // 2, t % 2
        found = pick(mine, ones_where(from_col == RADIX * to_col + t), False)
        for u, piece in enumerate(lanes_of(found, RADIX)):
            out_ref[RADIX * side + u, chunk * half : (chunk + 1) * half] = jnp.concatenate(
                [piece[:half], piece[half:]], axis=1
            )


def fast_body(object_real, object_imag, pupil_real, pupil_imag, measured, source_mask, offsets):
    width, length = pupil_real.shape
    modes, local_rows, size_k = object_real.shape
    groups, levels = lax.axis_size("rows"), lax.axis_size("mode")
    part = length // RADIX
    leds = offsets.shape[0]
    tables = [jnp.asarray(table) for table in radix_tables(length)]
    position = jnp.stack([lax.axis_index("rows"), lax.axis_index("mode")]).astype(jnp.int32)
    params = jnp.concatenate([source_mask.reshape(-1), offsets.reshape(-1), position])
    spectrum = pl.BlockSpec((1, local_rows, size_k), lambda i: (i, 0, 0))

    def update(count):
        slots = count * modes
        dft_macs = 3 * slots * 2 * 4 * part * part * local_rows
        pupil_shape = (count, 2, local_rows, width)
        block_shape = (count, modes, local_rows, width)
        half_table = (2, RADIX // CHUNKS) + tables[0].shape[2:]
        by_mode = (count, 1) + block_shape[2:]
        pupil_stage = pltpu.VMEM((groups,) + pupil_shape, jnp.float32)

        def columns(chunk, pupil, others):
            extra = others.shape[1] // slots if chunk == 0 else 0
            out = shaped(block_shape[:2] + (local_rows + extra, width))
            whole = shaped((count, 2, local_rows, length))
            operands = [params, object_real, object_imag, tables[0], *pupil]
            specs = [
                SMEM_SPEC,
                spectrum,
                spectrum,
                pl.BlockSpec(half_table, lambda i: (0, chunk, 0, 0)),
            ]
            outs, out_specs = (out,) * groups, (one_mode(out.shape),) * groups
            scratch = [
                pltpu.VMEM((groups, count, 1) + out.shape[2:], jnp.float32),
                pltpu.VMEM((2, 2, local_rows, 2 * part), jnp.bfloat16),
            ]
            if chunk == 0:
                others = others.reshape(groups, count, modes, extra, width)
                specs += [fixed(pupil_shape)] * groups + [one_mode(others.shape)]
                outs, out_specs = outs + (whole,), out_specs + (fixed(whole.shape),)
                scratch = [pupil_stage] + scratch
            else:
                specs += [fixed(whole.shape), ANY_SPEC]
            sent = pl.pallas_call(
                functools.partial(columns_kernel, leds, chunk, groups),
                out_shape=outs,
                grid=(modes,),
                in_specs=specs,
                out_specs=out_specs,
                scratch_shapes=scratch,
                compiler_params=room(count),
                cost_estimate=cost(dft_macs, *[out] * 16, object_real, object_imag),
                name="columns",
            )(*operands, others)
            return exchange(sent[:groups]), sent[groups:], sent[0]

        def rows(got, waits):
            field = shaped((RADIX, part, slots * width))
            total = shaped((levels, groups, 2 * part // groups // levels, width))
            extra = got[0].shape[2] - local_rows
            outs = (field, total)
            if extra > 0:
                outs += (shaped((groups, count, modes, extra, width)),)
            return pl.pallas_call(
                functools.partial(rows_kernel, leds, len(waits)),
                out_shape=outs,
                grid=(1,),
                in_specs=[SMEM_SPEC, fixed(tables[1].shape)]
                + [fixed(got[0].shape)] * groups
                + [ANY_SPEC] * len(waits),
                out_specs=tuple(fixed(out.shape) for out in outs),
                scratch_shapes=[
                    pltpu.VMEM((groups,) + got[0].shape, jnp.float32),
                    pltpu.VMEM((RADIX, 2, part, slots * width), jnp.bfloat16),
                ],
                compiler_params=room(count),
                cost_estimate=cost(dft_macs, *got, field),
                name="rows",
            )(params, tables[1], *got, *waits)

        def rows_back(field, factor):
            out = shaped(block_shape)
            sent = pl.pallas_call(
                functools.partial(rows_back_kernel, leds),
                out_shape=(out,) * groups,
                grid=(1,),
                in_specs=[SMEM_SPEC, fixed(tables[2].shape), fixed(field.shape)]
                + [fixed(factor.shape)],
                out_specs=(fixed(block_shape),) * groups,
                scratch_shapes=[
                    pltpu.VMEM((groups,) + block_shape, jnp.float32),
                    pltpu.VMEM(field.shape, jnp.float32),
                ],
                compiler_params=room(count),
                cost_estimate=cost(dft_macs, *[out] * groups, field),
                name="rows_back",
            )(params, tables[2], field, factor)
            return exchange(sent), sent[0]

        def columns_back(chunk, pupil, got, current, wait):
            out = shaped(object_real.shape)
            return pl.pallas_call(
                functools.partial(columns_back_kernel, leds, chunk, groups),
                out_shape=(out, out),
                grid=(modes,),
                in_specs=[
                    SMEM_SPEC,
                    spectrum,
                    spectrum,
                    pl.BlockSpec(half_table, lambda i: (0, chunk, 0, 0)),
                ]
                + [one_mode(block_shape)] * groups
                + [fixed(pupil.shape), ANY_SPEC],
                out_specs=(spectrum, spectrum),
                scratch_shapes=[
                    pltpu.VMEM((groups,) + by_mode, jnp.float32),
                    pltpu.VMEM((2, 2, local_rows, 2 * part), jnp.bfloat16),
                    pltpu.VMEM((count, 2, local_rows, 2 * part), jnp.float32),
                ],
                input_output_aliases={1: 0, 2: 1} if chunk > 0 else {},
                compiler_params=room(count),
                cost_estimate=cost(dft_macs, *got, pupil, out, out, out, out),
                name="columns_back",
            )(params, *current, tables[3], *got, pupil, wait)

        def run(*_):
            amplitude = shaped((groups, width // levels, width))
            amplitude = pl.pallas_call(
                functools.partial(amplitude_kernel, leds),
                out_shape=amplitude,
                grid=(1,),
                in_specs=[SMEM_SPEC, fixed(measured.shape)],
                out_specs=fixed(amplitude.shape),
                compiler_params=room(count),
                cost_estimate=cost(3 * length * length * RADIX * 8, amplitude, measured),
                name="amplitude",
            )(params, measured)
            out = shaped(pupil_shape)
            sent = pl.pallas_call(
                functools.partial(pupil_send_kernel, leds),
                out_shape=(out,) * groups,
                grid=(1,),
                in_specs=[SMEM_SPEC] + [fixed(pupil_real.shape)] * 2,
                out_specs=(fixed(pupil_shape),) * groups,
                scratch_shapes=[pupil_stage],
                compiler_params=room(count),
                cost_estimate=cost(0, *[out] * groups, pupil_real, pupil_imag),
                name="pupil_send",
            )(params, pupil_real, pupil_imag)
            got, (pupil,), _ = columns(0, exchange(sent), amplitude)
            more, _, wait = columns(1, [pupil], got[WAIT_BLOCK])
            got = [got, more]
            back, waits = [], [wait]
            for chunk in range(CHUNKS):
                field, total, *amplitudes = rows(got[chunk], waits)
                if chunk == 0:
                    mine = amplitudes[0].reshape(groups, width // levels, width)
                share = jnp.sum(across(total), axis=0)
                deep = share.shape[1]
                ratio = mine[:, chunk * deep : (chunk + 1) * deep] / jnp.sqrt(share + FLOOR_TERM)
                factor = across(jnp.broadcast_to(ratio - 1.0, total.shape))
                blocks, wait = rows_back(field, factor)
                back.append(blocks)
                waits = [wait]
            current = (object_real, object_imag)
            for chunk in range(CHUNKS):
                current = columns_back(chunk, pupil, back[chunk], current, wait)
            return tuple(current)

        return run

    lit = jnp.sum((source_mask[0] != 0).astype(jnp.int32))
    most = max(leds - 1, 1)
    if most == 1:
        return update(1)()
    return lax.switch(jnp.clip(lit - 1, 0, most - 1), [update(n + 1) for n in range(most)])


def fits_fast(mesh, object_shape, pupil_shape, leds):
    groups, levels = mesh.shape["rows"], mesh.shape["mode"]
    length, size_k = pupil_shape[1], object_shape[2]
    modes, local_rows, width = object_shape[0] // levels, size_k // groups, length // groups
    amplitude_rows = width // levels
    return (
        size_k == 2 * length
        and groups == 2 * RADIX
        and levels == RADIX
        and local_rows % 256 == 0
        and width % 128 == 0
        and all(amplitude_rows % (8 * modes * n) == 0 for n in range(1, max(leds, 2)))
    )


def solution(mesh):
    in_specs = (
        P("mode", "rows", None),
        P("mode", "rows", None),
        P("rows", None),
        P("rows", None),
        P(None, "rows", None),
        P(),
        P(),
    )
    out_specs = (P("mode", "rows", None), P("mode", "rows", None))

    def chosen(object_real, object_imag, pupil_real, *others):
        fast = fits_fast(mesh, object_real.shape, pupil_real.shape, others[-1].shape[0])
        mapped = jax.shard_map(
            fast_body if fast else body,
            mesh=mesh,
            in_specs=in_specs,
            out_specs=out_specs,
            check_vma=False,
        )
        return mapped(object_real, object_imag, pupil_real, *others)

    return chosen
```

```python
import functools
import math

import jax
import jax.numpy as jnp
import ml_dtypes
import numpy as np
from jax import lax
from jax.experimental import pallas as pl
from jax.experimental.pallas import tpu as pltpu
from jax.sharding import PartitionSpec as P

FLOOR_TERM = 0.5
HIGHEST_PREC = lax.Precision.HIGHEST


def dft_tables(length):
    indices = jnp.arange(length, dtype=jnp.int32)
    phases = indices[:, None] * indices[None, :] % length
    angles = phases.astype(jnp.float32) * (2.0 * math.pi / length)
    scale_factor = 1.0 / math.sqrt(length)
    cos_table = jnp.cos(angles) * scale_factor
    sin_table = jnp.sin(angles) * scale_factor
    return (
        jnp.concatenate([cos_table, sin_table], axis=1),
        jnp.concatenate([cos_table, sin_table], axis=0),
    )


def transform(form, table, real_part, imag_part, axis, direction_sign):
    result = jnp.einsum(form, jnp.stack([real_part, imag_part]), table, precision=HIGHEST_PREC)
    length = result.shape[axis] // 2
    with_cos = lax.slice_in_dim(result, 0, length, axis=axis)
    with_sin = lax.slice_in_dim(result, length, 2 * length, axis=axis)
    return (with_cos[0] - direction_sign * with_sin[1], with_cos[1] + direction_sign * with_sin[0])


def right_product(real_part, imag_part, wide_cols, direction_sign):
    return transform("smlck,kj->smlcj", wide_cols, real_part, imag_part, 4, direction_sign)


def forward_fields(
    part_real, part_imag, pupil_real, pupil_imag, offsets, wide_cols, wide_rows, length
):
    source_count = offsets.shape[0]
    groups = lax.axis_size("rows")
    crop_real = jnp.stack(
        [
            lax.dynamic_slice_in_dim(part_real, offsets[source_index, 1], length, 2)
            for source_index in range(source_count)
        ],
        axis=1,
    )
    crop_imag = jnp.stack(
        [
            lax.dynamic_slice_in_dim(part_imag, offsets[source_index, 1], length, 2)
            for source_index in range(source_count)
        ],
        axis=1,
    )
    got_real, got_imag = (
        lax.all_to_all(
            jnp.swapaxes(crop_real, 2, 3), "rows", split_axis=2, concat_axis=3, tiled=True
        ),
        lax.all_to_all(
            jnp.swapaxes(crop_imag, 2, 3), "rows", split_axis=2, concat_axis=3, tiled=True
        ),
    )
    win_real = jnp.stack(
        [
            lax.dynamic_slice_in_dim(got_real[:, source_index], offsets[source_index, 0], length, 2)
            for source_index in range(source_count)
        ],
        axis=1,
    )
    win_imag = jnp.stack(
        [
            lax.dynamic_slice_in_dim(got_imag[:, source_index], offsets[source_index, 0], length, 2)
            for source_index in range(source_count)
        ],
        axis=1,
    )
    lifted_real = pupil_real * win_real - pupil_imag * win_imag
    lifted_imag = pupil_real * win_imag + pupil_imag * win_real
    half_real, half_imag = transform("smlcr,yr->smlyc", wide_rows, lifted_real, lifted_imag, 3, 1.0)
    layout = half_real.shape
    blocked = (layout[0], layout[1], groups, layout[2] // groups, layout[3])
    back_real, back_imag = (
        lax.all_to_all(half_real.reshape(blocked), "rows", split_axis=2, concat_axis=4, tiled=True),
        lax.all_to_all(half_imag.reshape(blocked), "rows", split_axis=2, concat_axis=4, tiled=True),
    )
    flat = (layout[0], layout[1], layout[2] // groups, layout[3] * groups)
    return right_product(back_real.reshape(flat), back_imag.reshape(flat), wide_cols, 1.0)


def spectral_updates(diff_real, diff_imag, pupil_real, pupil_imag, offsets, wide_cols, size_k):
    source_count = offsets.shape[0]
    groups = lax.axis_size("rows")
    col_real, col_imag = right_product(diff_real, diff_imag, wide_cols, -1.0)
    layout = col_real.shape
    blocked = (layout[0], layout[1], layout[2], groups, layout[3] // groups)
    got_real, got_imag = (
        lax.all_to_all(col_real.reshape(blocked), "rows", split_axis=3, concat_axis=2, tiled=True),
        lax.all_to_all(col_imag.reshape(blocked), "rows", split_axis=3, concat_axis=2, tiled=True),
    )
    flat = (layout[0], layout[1], layout[2] * groups, layout[3] // groups)
    full_real = got_real.reshape(flat)
    full_imag = got_imag.reshape(flat)
    delta_real, delta_imag = transform("smlyc,yk->smlck", wide_cols, full_real, full_imag, 4, -1.0)
    upd_real = pupil_real * delta_real + pupil_imag * delta_imag
    upd_imag = pupil_real * delta_imag - pupil_imag * delta_real
    blank = jnp.zeros((layout[0], layout[3] // groups, size_k), jnp.float32)
    placed_real = jnp.stack(
        [
            lax.dynamic_update_slice_in_dim(
                blank, upd_real[:, source_index], offsets[source_index, 0], 2
            )
            for source_index in range(source_count)
        ],
        axis=1,
    )
    placed_imag = jnp.stack(
        [
            lax.dynamic_update_slice_in_dim(
                blank, upd_imag[:, source_index], offsets[source_index, 0], 2
            )
            for source_index in range(source_count)
        ],
        axis=1,
    )
    return (
        lax.all_to_all(placed_real, "rows", split_axis=3, concat_axis=2, tiled=True),
        lax.all_to_all(placed_imag, "rows", split_axis=3, concat_axis=2, tiled=True),
    )


def add_window(target, incoming, start_col, length):
    current = lax.dynamic_slice_in_dim(target, start_col, length, 2)
    return lax.dynamic_update_slice_in_dim(
        target, current + jnp.swapaxes(incoming, 1, 2), start_col, 2
    )


def body(object_real, object_imag, pupil_real, pupil_imag, measured, source_mask, offsets):
    length = pupil_real.shape[1]
    size_k = object_real.shape[2]
    source_count = offsets.shape[0]
    wide_cols, wide_rows = dft_tables(length)
    spec_real, spec_imag = (object_real, object_imag)
    weights = source_mask[0].astype(jnp.float32)
    field_real, field_imag = forward_fields(
        spec_real, spec_imag, pupil_real, pupil_imag, offsets, wide_cols, wide_rows, length
    )
    powers = jnp.sum(field_real * field_real + field_imag * field_imag, axis=0)
    partial_sum = jnp.tensordot(weights, powers, axes=1)
    share = lax.psum_scatter(partial_sum, "mode", scatter_dimension=0, tiled=True)
    share_rows = share.shape[0]
    measured_share = lax.dynamic_slice_in_dim(
        measured[0], lax.axis_index("mode") * share_rows, share_rows, 0
    )
    ratio_share = measured_share / jnp.sqrt(share + FLOOR_TERM)
    ratios = lax.all_gather(ratio_share, "mode", axis=0, tiled=True)
    factor = (ratios - 1.0)[None, None] * weights[None, :, None, None]
    diff_real = field_real * factor
    diff_imag = field_imag * factor
    ret_real, ret_imag = spectral_updates(
        diff_real, diff_imag, pupil_real, pupil_imag, offsets, wide_cols, size_k
    )
    for source_index in range(source_count):
        start_col = offsets[source_index, 1]
        spec_real = add_window(spec_real, ret_real[:, source_index], start_col, length)
        spec_imag = add_window(spec_imag, ret_imag[:, source_index], start_col, length)
    return (spec_real, spec_imag)


RADIX = 4
ROW_TILE = 64


def split_pair(table):
    high = table.astype(ml_dtypes.bfloat16)
    low = (table - high.astype(np.float64)).astype(ml_dtypes.bfloat16)
    return np.stack([high, low])


def radix_tables(length):
    part = length // RADIX
    t = np.arange(RADIX)[:, None, None]
    r = np.arange(part)[None, :, None]
    s = np.arange(part)[None, None, :]
    angles = (r * (t + RADIX * s) % length) * (2.0 * np.pi / length)
    cos_t = np.cos(angles) / np.sqrt(length)
    sin_t = np.sin(angles) / np.sqrt(length)
    swap = lambda x: np.swapaxes(x, 1, 2)
    width = part // RADIX
    pieces = lambda x: x.reshape(RADIX, part, RADIX, width)
    beside = lambda x, y: np.stack([pieces(x), pieces(y)], axis=3).reshape(RADIX, part, 2 * part)
    columns = np.concatenate([beside(cos_t, sin_t), beside(-sin_t, cos_t)], axis=1)
    rows = np.concatenate([swap(cos_t), swap(sin_t)], axis=1)
    rows_back = np.concatenate([cos_t, sin_t], axis=1)
    return tuple(split_pair(table) for table in (columns, rows, rows_back))


def halves(x):
    high = x.astype(jnp.bfloat16)
    low = (x - high.astype(jnp.float32)).astype(jnp.bfloat16)
    return high, low


def dot(a, b):
    return jnp.dot(a, b, preferred_element_type=jnp.float32)


def dot_right(pair_ref, table_ref, t, turned=False):
    def product(a, b):
        dims = (((1,), (1 if turned else 0,)), ((), ()))
        return lax.dot_general(a, b, dims, preferred_element_type=jnp.float32)

    high, low = pair_ref[0], pair_ref[1]
    return (
        product(high, table_ref[0, t])
        + product(low, table_ref[0, t])
        + product(high, table_ref[1, t])
    )


def dot_left(table_ref, t, high, low):
    return dot(table_ref[0, t], high) + dot(table_ref[0, t], low) + dot(table_ref[1, t], high)


def over_rows(rows, step):
    def one(i, _):
        step(pl.ds(pl.multiple_of(i * ROW_TILE, ROW_TILE), ROW_TILE))
        return 0

    lax.fori_loop(0, rows // ROW_TILE, one, 0)


def lanes_of(x, slots):
    width = x.shape[1] // slots
    return [x[:, n * width : (n + 1) * width] for n in range(slots)]


def times_i(x):
    half = x.shape[1] // 2
    turned = pltpu.roll(x, half, 1)
    return jnp.where(lax.broadcasted_iota(jnp.int32, x.shape, 1) < half, -turned, turned)


def lit_offsets(params_ref, leds, nth):
    row, col, seen = jnp.int32(0), jnp.int32(0), jnp.int32(0)
    for led in range(leds):
        lit = params_ref[led] != 0
        take = jnp.logical_and(lit, seen == nth)
        row = jnp.where(take, params_ref[leds + 2 * led], row)
        col = jnp.where(take, params_ref[leds + 2 * led + 1], col)
        seen = seen + lit.astype(jnp.int32)
    return row, col


def place_of(params_ref, leds, levels=False):
    return params_ref[3 * leds + (1 if levels else 0)]


def pupil_send_kernel(leds, params_ref, real_ref, imag_ref, out_ref):
    length = real_ref.shape[1]
    part = length // RADIX
    for nth in range(out_ref.shape[1]):
        row, _ = lit_offsets(params_ref, leds, nth)
        for index, ref in enumerate((real_ref, imag_ref)):
            rolled = pltpu.roll(ref[...], lax.rem(row, length), 1)
            for q in range(RADIX):
                block = rolled[:, q * part : (q + 1) * part].T
                out_ref[q, nth, index] = block
                out_ref[q + RADIX, nth, index] = block


def window_pupil(leds, params_ref, stage_ref, pupil_ref):
    here = place_of(params_ref, leds)
    blocks, count, _, rows, width = stage_ref.shape
    length = blocks * width
    upper, first = here // RADIX, lax.rem(here, RADIX) * rows
    for nth in range(count):
        row, col = lit_offsets(params_ref, leds, nth)

        def tile(at):
            position = first + at.start + lax.broadcasted_iota(jnp.int32, (ROW_TILE, length), 0)
            owned = (position < row).astype(jnp.int32) == upper
            for index in range(2):
                whole = [stage_ref[d, nth, index, at] for d in range(blocks)]
                whole = pltpu.roll(jnp.concatenate(whole, axis=1), lax.rem(col, length), 1)
                pupil_ref[nth, index, at] = jnp.where(owned, whole, 0.0)

        over_rows(rows, tile)


def columns_kernel(leds, chunk, params_ref, real_ref, imag_ref, table_ref, *refs):
    pair_ref = refs[-1]
    if chunk == 0:
        stage_ref, amplitude_ref, out_ref, pupil_ref = refs[:-1]

        @pl.when(pl.program_id(0) == 0)
        def _():
            window_pupil(leds, params_ref, stage_ref, pupil_ref)
    else:
        pupil_ref, out_ref = refs[0], refs[-2]
    rows, size_k = real_ref.shape[1:]
    length = size_k // 2
    for nth in range(out_ref.shape[1]):
        _, col = lit_offsets(params_ref, leds, nth)

        def tile(at):
            wrapped = lax.broadcasted_iota(jnp.int32, (ROW_TILE, length), 1) < col
            p_r, p_i = pupil_ref[nth, 0, at], pupil_ref[nth, 1, at]
            w_r = jnp.where(wrapped, real_ref[0, at, length:], real_ref[0, at, :length])
            w_i = jnp.where(wrapped, imag_ref[0, at, length:], imag_ref[0, at, :length])
            x_r = lanes_of(p_r * w_r - p_i * w_i, RADIX)
            x_i = lanes_of(p_r * w_i + p_i * w_r, RADIX)
            sum_r, sum_i = x_r[0] + x_r[2], x_i[0] + x_i[2]
            dif_r, dif_i = x_r[0] - x_r[2], x_i[0] - x_i[2]
            odd_r, odd_i = x_r[1] + x_r[3], x_i[1] + x_i[3]
            rot_r, rot_i = x_i[3] - x_i[1], x_r[1] - x_r[3]
            if chunk == 0:
                pairs = ((sum_r + odd_r, sum_i + odd_i), (dif_r + rot_r, dif_i + rot_i))
            else:
                pairs = ((sum_r - odd_r, sum_i - odd_i), (dif_r - rot_r, dif_i - rot_i))
            for t, pair in enumerate(pairs):
                pair_ref[t, 0, at], pair_ref[t, 1, at] = halves(jnp.concatenate(pair, axis=1))

        over_rows(rows, tile)
        for t in range(2):
            z = dot_right(pair_ref[t], table_ref, t)
            for u, piece in enumerate(lanes_of(z, RADIX)):
                out_ref[RADIX * t + u, nth, 0, :rows] = piece
    if chunk == 0:
        out_ref[:, :, 0, rows:] = amplitude_ref[:, :, 0]


def rows_kernel(leds, waits, params_ref, table_ref, got_ref, *refs):
    total_ref, pair_ref = refs[-2:]
    groups, count, modes, _, width = got_ref.shape
    levels = total_ref.shape[0]
    refs = refs[waits:-2]
    field_ref, total_refs = refs[0], refs[1 : 1 + levels]
    part = field_ref.shape[1]
    for amplitude_ref in refs[1 + levels :]:
        amplitude_ref[...] = got_ref[:, :, :, part:]
    slots = [(nth, mode) for nth in range(count) for mode in range(modes)]

    def tile(at):
        for n, (nth, mode) in enumerate(slots):
            x = [got_ref[q, nth, mode, at] + got_ref[q + RADIX, nth, mode, at] for q in range(RADIX)]
            even, odd = x[0] + x[2], x[1] + x[3]
            dif, rot = x[0] - x[2], times_i(x[1] - x[3])
            for t, value in enumerate((even + odd, dif + rot, even - odd, dif - rot)):
                lanes = slice(n * width, (n + 1) * width)
                pair_ref[t, 0, at, lanes], pair_ref[t, 1, at, lanes] = halves(value)

    over_rows(part, tile)
    powers = []
    for t in range(RADIX):
        both = dot_left(table_ref, t, pair_ref[t, 0], pair_ref[t, 1])
        power = None
        for n, (a, b) in enumerate(
            zip(lanes_of(both[:part], len(slots)), lanes_of(both[part:], len(slots)))
        ):
            z = a + times_i(b)
            field_ref[t, :, n * width : (n + 1) * width] = z
            power = z * z if power is None else power + z * z
        powers.append(power + pltpu.roll(power, width // 2, 1))
    rows = total_ref.shape[2] // 2
    low = lax.broadcasted_iota(jnp.int32, (part, width), 1) < width // 2
    for pair in range(2):
        packed = jnp.where(low, powers[2 * pair], powers[2 * pair + 1])
        for d in range(groups):
            for z in range(levels):
                first = (d * levels + z) * rows
                total_ref[z, d, pair * rows : (pair + 1) * rows] = packed[first : first + rows]
    level = place_of(params_ref, leds, True)
    for k, ref in enumerate(total_refs):
        ref[...] = total_ref[lax.rem(level + k, levels)]


def rows_back_kernel(leds, params_ref, table_ref, field_ref, *refs):
    out_ref, factor_ref, turn_ref = refs[-3:]
    groups, count, modes, part, width = out_ref.shape
    levels = factor_ref.shape[0]
    level = place_of(params_ref, leds, True)
    for k, ref in enumerate(refs[:levels]):
        factor_ref[lax.rem(level + levels - k, levels)] = ref[...]
    slots = [(nth, mode) for nth in range(count) for mode in range(modes)]
    rows = factor_ref.shape[2] // 2
    low = lax.broadcasted_iota(jnp.int32, (part, width), 1) < width // 2
    for t in range(RADIX):
        pair = t // 2
        packed = jnp.concatenate(
            [
                factor_ref[z, d, pair * rows : (pair + 1) * rows]
                for d in range(groups)
                for z in range(levels)
            ],
            axis=0,
        )
        turned = pltpu.roll(packed, width // 2, 1)
        factor = jnp.where(low, packed, turned) if t % 2 == 0 else jnp.where(low, turned, packed)
        diff = jnp.concatenate([x * factor for x in lanes_of(field_ref[t], len(slots))], axis=1)
        both = dot_left(table_ref, t, *halves(diff))
        for n, (a, b) in enumerate(
            zip(lanes_of(both[:part], len(slots)), lanes_of(both[part:], len(slots)))
        ):
            turn_ref[t, :, n * width : (n + 1) * width] = a - times_i(b)

    def tile(at):
        for n, (nth, mode) in enumerate(slots):
            v = [turn_ref[t, at, n * width : (n + 1) * width] for t in range(RADIX)]
            even, odd = v[0] + v[2], v[1] + v[3]
            dif, rot = v[0] - v[2], times_i(v[1] - v[3])
            for q, value in enumerate((even + odd, dif - rot, even - odd, dif + rot)):
                out_ref[q, nth, mode, at] = value
                out_ref[q + RADIX, nth, mode, at] = value

    over_rows(part, tile)


def columns_back_kernel(leds, chunk, params_ref, real_ref, imag_ref, table_ref, *refs):
    got_ref, pupil_ref, _, out_r, out_i, pair_ref, turn_ref = refs
    count = got_ref.shape[1]
    rows, size_k = real_ref.shape[1:]
    length = size_k // 2
    for nth in range(count):
        for t in range(2):

            def split(at):
                z = [got_ref[RADIX * t + n, nth, 0, at] for n in range(RADIX)]
                pair_ref[t, 0, at], pair_ref[t, 1, at] = halves(jnp.concatenate(z, axis=1))

            over_rows(rows, split)
            turn_ref[nth, t] = dot_right(pair_ref[t], table_ref, t, True)

    def tile(at):
        totals = [[ref[0, at, :length], ref[0, at, length:]] for ref in (real_ref, imag_ref)]
        for nth in range(count):
            _, col = lit_offsets(params_ref, leds, nth)
            wrapped = lax.broadcasted_iota(jnp.int32, (ROW_TILE, length), 1) < col
            p_r, p_i = pupil_ref[nth, 0, at], pupil_ref[nth, 1, at]
            (a_r, a_i), (b_r, b_i) = [lanes_of(turn_ref[nth, t, at], 2) for t in range(2)]
            if chunk == 0:
                x_r = [a_r + b_r, a_r + b_i, a_r - b_r, a_r - b_i]
                x_i = [a_i + b_i, a_i - b_r, a_i - b_i, a_i + b_r]
            else:
                x_r = [a_r + b_r, -a_r - b_i, a_r - b_r, b_i - a_r]
                x_i = [a_i + b_i, b_r - a_i, a_i - b_i, -a_i - b_r]
            x_r, x_i = jnp.concatenate(x_r, axis=1), jnp.concatenate(x_i, axis=1)
            for total, delta in zip(totals, (p_r * x_r + p_i * x_i, p_r * x_i - p_i * x_r)):
                total[0] = total[0] + jnp.where(wrapped, 0.0, delta)
                total[1] = total[1] + jnp.where(wrapped, delta, 0.0)
        for out, total in zip((out_r, out_i), totals):
            out[0, at, :length] = total[0]
            out[0, at, length:] = total[1]

    over_rows(rows, tile)


SMEM_SPEC = pl.BlockSpec(memory_space=pltpu.SMEM)
ANY_SPEC = pl.BlockSpec(memory_space=pl.ANY)


def room(count):
    return pltpu.CompilerParams(vmem_limit_bytes=(16 + 16 * count) * 1024 * 1024)


CHUNKS = 2


def fixed(shape):
    zeros = (0,) * len(shape)
    return pl.BlockSpec(shape, lambda *_: zeros)


def one_mode(shape):
    before = len(shape) - 3
    block = shape[:before] + (1,) + shape[before + 1 :]
    return pl.BlockSpec(block, lambda i: (0,) * before + (i, 0, 0))


def kept(shape):
    zeros = (0,) * len(shape)
    return pl.BlockSpec(shape, lambda *_: zeros, pipeline_mode=pl.Buffered(1))


def cost(macs, *arrays):
    moved = sum(math.prod(a.shape) * a.dtype.itemsize for a in arrays)
    return pl.CostEstimate(flops=2 * macs, bytes_accessed=moved, transcendentals=0)


def shaped(shape):
    return jax.ShapeDtypeStruct(shape, jnp.float32)


def exchange(blocks):
    return lax.all_to_all(blocks, "rows", split_axis=0, concat_axis=0, tiled=True)


def around(levels, value_of):
    ring = range(levels)
    return [value_of(0)] + [
        lax.ppermute(value_of(k), "mode", [(z, (z + k) % levels) for z in ring]) for k in ring[1:]
    ]


def amplitude_kernel(leds, params_ref, measured_ref, out_ref):
    groups, rows, lanes = out_ref.shape
    width, length = measured_ref.shape[1:]
    columns = lanes // 2
    depth = rows // RADIX
    first = place_of(params_ref, leds, True) * rows

    def pick(x, y, turned):
        total = None
        for _ in range(3):
            x_part = x.astype(jnp.bfloat16)
            x = x - x_part.astype(jnp.float32)
            piece = dot(y, x_part) if turned else dot(x_part, y)
            total = piece if total is None else total + piece
        return total

    def ones_where(condition):
        return jnp.where(condition, 1.0, 0.0).astype(jnp.bfloat16)

    order = lax.broadcasted_iota(jnp.int32, (rows, width), 0)
    source = RADIX * (order % depth) + 2 * ((order // depth) % 2) + order // (2 * depth)
    taken = lax.broadcasted_iota(jnp.int32, (rows, width), 1) == source + first
    mine = pick(measured_ref[0], ones_where(taken), True)
    part = length // RADIX
    from_col = lax.broadcasted_iota(jnp.int32, (length, part), 0)
    to_col = lax.broadcasted_iota(jnp.int32, (length, part), 1)
    half = rows // 2
    for t in range(RADIX):
        chunk, side = t // 2, t % 2
        found = pick(mine, ones_where(from_col == RADIX * to_col + t), False)
        for u, piece in enumerate(lanes_of(found, RADIX)):
            out_ref[RADIX * side + u, chunk * half : (chunk + 1) * half] = jnp.concatenate(
                [piece[:half], piece[half:]], axis=1
            )


def fast_body(object_real, object_imag, pupil_real, pupil_imag, measured, source_mask, offsets):
    width, length = pupil_real.shape
    modes, local_rows, size_k = object_real.shape
    groups, levels = lax.axis_size("rows"), lax.axis_size("mode")
    part = length // RADIX
    leds = offsets.shape[0]
    tables = [jnp.asarray(table) for table in radix_tables(length)]
    position = jnp.stack([lax.axis_index("rows"), lax.axis_index("mode")]).astype(jnp.int32)
    params = jnp.concatenate([source_mask.reshape(-1), offsets.reshape(-1), position])
    spectrum = pl.BlockSpec((1, local_rows, size_k), lambda i: (i, 0, 0))

    def update(count):
        slots = count * modes
        dft_macs = 3 * slots * 2 * 4 * part * part * local_rows
        pupil_shape = (groups, count, 2, local_rows, width)
        block_shape = (groups, count, modes, local_rows, width)
        half_table = (2, RADIX // CHUNKS) + tables[0].shape[2:]

        def columns(chunk, pupil, others):
            extra = others.shape[1] // slots if chunk == 0 else 0
            out = shaped(block_shape[:3] + (local_rows + extra, width))
            whole = shaped((count, 2, local_rows, length))
            specs = [
                SMEM_SPEC,
                spectrum,
                spectrum,
                pl.BlockSpec(half_table, lambda i: (0, chunk, 0, 0), pipeline_mode=pl.Buffered(1)),
            ]
            outs, out_specs = (out,), (one_mode(out.shape),)
            if chunk == 0:
                others = others.reshape(groups, count, modes, extra, width)
                specs += [kept(pupil_shape), one_mode(others.shape)]
                outs, out_specs = outs + (whole,), out_specs + (fixed(whole.shape),)
            else:
                specs += [kept(whole.shape), ANY_SPEC]
            sent, *kept_pupil = pl.pallas_call(
                functools.partial(columns_kernel, leds, chunk),
                out_shape=outs,
                grid=(modes,),
                in_specs=specs,
                out_specs=out_specs,
                scratch_shapes=[pltpu.VMEM((2, 2, local_rows, 2 * part), jnp.bfloat16)],
                compiler_params=room(count),
                cost_estimate=cost(dft_macs, out, out, object_real, object_imag),
                name="columns",
            )(params, object_real, object_imag, tables[0], pupil, others)
            return exchange(sent), kept_pupil, sent

        def rows(got, waits):
            field = shaped((RADIX, part, slots * width))
            total = shaped((groups, 2 * part // groups // levels, width))
            extra = got.shape[3] - local_rows
            outs = (field,) + (total,) * levels
            if extra > 0:
                outs += (shaped((groups, count, modes, extra, width)),)
            return pl.pallas_call(
                functools.partial(rows_kernel, leds, len(waits)),
                out_shape=outs,
                grid=(1,),
                in_specs=[SMEM_SPEC, fixed(tables[1].shape)]
                + [fixed(got.shape)]
                + [ANY_SPEC] * len(waits),
                out_specs=tuple(fixed(out.shape) for out in outs),
                scratch_shapes=[
                    pltpu.VMEM((levels,) + total.shape, jnp.float32),
                    pltpu.VMEM((RADIX, 2, part, slots * width), jnp.bfloat16),
                ],
                compiler_params=room(count),
                cost_estimate=cost(dft_macs, got, field),
                name="rows",
            )(params, tables[1], got, *waits)

        def rows_back(field, factor):
            out = shaped(block_shape)
            sent = pl.pallas_call(
                functools.partial(rows_back_kernel, leds),
                out_shape=out,
                grid=(1,),
                in_specs=[SMEM_SPEC, fixed(tables[2].shape), fixed(field.shape)]
                + [fixed(factor[0].shape)] * levels,
                out_specs=fixed(block_shape),
                scratch_shapes=[
                    pltpu.VMEM((levels,) + factor[0].shape, jnp.float32),
                    pltpu.VMEM(field.shape, jnp.float32),
                ],
                compiler_params=room(count),
                cost_estimate=cost(dft_macs, out, field),
                name="rows_back",
            )(params, tables[2], field, *factor)
            return exchange(sent), sent

        def columns_back(chunk, pupil, got, current, wait):
            out = shaped(object_real.shape)
            return pl.pallas_call(
                functools.partial(columns_back_kernel, leds, chunk),
                out_shape=(out, out),
                grid=(modes,),
                in_specs=[
                    SMEM_SPEC,
                    spectrum,
                    spectrum,
                    pl.BlockSpec(
                        half_table, lambda i: (0, chunk, 0, 0), pipeline_mode=pl.Buffered(1)
                    ),
                    one_mode(block_shape),
                    kept(pupil.shape),
                    ANY_SPEC,
                ],
                out_specs=(spectrum, spectrum),
                scratch_shapes=[
                    pltpu.VMEM((2, 2, local_rows, 2 * part), jnp.bfloat16),
                    pltpu.VMEM((count, 2, local_rows, 2 * part), jnp.float32),
                ],
                input_output_aliases={1: 0, 2: 1} if chunk > 0 else {},
                compiler_params=room(count),
                cost_estimate=cost(dft_macs, got, pupil, out, out, out, out),
                name="columns_back",
            )(params, *current, tables[0], got, pupil, wait)

        def run(*_):
            amplitude = shaped((groups, width // levels, width))
            amplitude = pl.pallas_call(
                functools.partial(amplitude_kernel, leds),
                out_shape=amplitude,
                grid=(1,),
                in_specs=[SMEM_SPEC, fixed(measured.shape)],
                out_specs=fixed(amplitude.shape),
                compiler_params=room(count),
                cost_estimate=cost(3 * length * length * RADIX * 8, amplitude, measured),
                name="amplitude",
            )(params, measured)
            out = shaped(pupil_shape)
            sent = pl.pallas_call(
                functools.partial(pupil_send_kernel, leds),
                out_shape=out,
                grid=(1,),
                in_specs=[SMEM_SPEC] + [fixed(pupil_real.shape)] * 2,
                out_specs=fixed(pupil_shape),
                compiler_params=room(count),
                cost_estimate=cost(0, out, pupil_real, pupil_imag),
                name="pupil_send",
            )(params, pupil_real, pupil_imag)
            got, (pupil,), wait = columns(0, exchange(sent), amplitude)
            more, _, wait = columns(1, pupil, wait)
            got = [got, more]
            back, waits = [], [wait]
            for chunk in range(CHUNKS):
                field, *totals = rows(got[chunk], waits)
                if chunk == 0:
                    mine = totals.pop().reshape(groups, width // levels, width)
                share = sum(around(levels, lambda k: totals[k]))
                deep = share.shape[1]
                ratio = mine[:, chunk * deep : (chunk + 1) * deep] / jnp.sqrt(share + FLOOR_TERM)
                factor = around(levels, lambda k: ratio - 1.0)
                blocks, wait = rows_back(field, factor)
                back.append(blocks)
                waits = [wait]
            current = (object_real, object_imag)
            for chunk in range(CHUNKS):
                current = columns_back(chunk, pupil, back[chunk], current, wait)
            return tuple(current)

        return run

    lit = jnp.sum((source_mask[0] != 0).astype(jnp.int32))
    most = max(leds - 1, 1)
    if most == 1:
        return update(1)()
    return lax.switch(jnp.clip(lit - 1, 0, most - 1), [update(n + 1) for n in range(most)])


def fits_fast(mesh, object_shape, pupil_shape, leds):
    groups, levels = mesh.shape["rows"], mesh.shape["mode"]
    length, size_k = pupil_shape[1], object_shape[2]
    modes, local_rows, width = object_shape[0] // levels, size_k // groups, length // groups
    amplitude_rows = width // levels
    return (
        size_k == 2 * length
        and groups == 2 * RADIX
        and levels == RADIX
        and local_rows % 256 == 0
        and width % 128 == 0
        and all(amplitude_rows % (8 * modes * n) == 0 for n in range(1, max(leds, 2)))
    )


def solution(mesh):
    in_specs = (
        P("mode", "rows", None),
        P("mode", "rows", None),
        P("rows", None),
        P("rows", None),
        P(None, "rows", None),
        P(),
        P(),
    )
    out_specs = (P("mode", "rows", None), P("mode", "rows", None))

    def chosen(object_real, object_imag, pupil_real, *others):
        fast = fits_fast(mesh, object_real.shape, pupil_real.shape, others[-1].shape[0])
        mapped = jax.shard_map(
            fast_body if fast else body,
            mesh=mesh,
            in_specs=in_specs,
            out_specs=out_specs,
            check_vma=False,
        )
        return mapped(object_real, object_imag, pupil_real, *others)

    return chosen
```

```python
import functools
import math

import jax
import jax.numpy as jnp
import ml_dtypes
import numpy as np
from jax import lax
from jax.experimental import pallas as pl
from jax.experimental.pallas import tpu as pltpu
from jax.sharding import PartitionSpec as P

FLOOR_TERM = 0.5
HIGHEST_PREC = lax.Precision.HIGHEST


def dft_tables(length):
    indices = jnp.arange(length, dtype=jnp.int32)
    phases = indices[:, None] * indices[None, :] % length
    angles = phases.astype(jnp.float32) * (2.0 * math.pi / length)
    scale_factor = 1.0 / math.sqrt(length)
    cos_table = jnp.cos(angles) * scale_factor
    sin_table = jnp.sin(angles) * scale_factor
    return (
        jnp.concatenate([cos_table, sin_table], axis=1),
        jnp.concatenate([cos_table, sin_table], axis=0),
    )


def transform(form, table, real_part, imag_part, axis, direction_sign):
    result = jnp.einsum(form, jnp.stack([real_part, imag_part]), table, precision=HIGHEST_PREC)
    length = result.shape[axis] // 2
    with_cos = lax.slice_in_dim(result, 0, length, axis=axis)
    with_sin = lax.slice_in_dim(result, length, 2 * length, axis=axis)
    return (with_cos[0] - direction_sign * with_sin[1], with_cos[1] + direction_sign * with_sin[0])


def right_product(real_part, imag_part, wide_cols, direction_sign):
    return transform("smlck,kj->smlcj", wide_cols, real_part, imag_part, 4, direction_sign)


def forward_fields(
    part_real, part_imag, pupil_real, pupil_imag, offsets, wide_cols, wide_rows, length
):
    source_count = offsets.shape[0]
    groups = lax.axis_size("rows")
    crop_real = jnp.stack(
        [
            lax.dynamic_slice_in_dim(part_real, offsets[source_index, 1], length, 2)
            for source_index in range(source_count)
        ],
        axis=1,
    )
    crop_imag = jnp.stack(
        [
            lax.dynamic_slice_in_dim(part_imag, offsets[source_index, 1], length, 2)
            for source_index in range(source_count)
        ],
        axis=1,
    )
    got_real, got_imag = (
        lax.all_to_all(
            jnp.swapaxes(crop_real, 2, 3), "rows", split_axis=2, concat_axis=3, tiled=True
        ),
        lax.all_to_all(
            jnp.swapaxes(crop_imag, 2, 3), "rows", split_axis=2, concat_axis=3, tiled=True
        ),
    )
    win_real = jnp.stack(
        [
            lax.dynamic_slice_in_dim(got_real[:, source_index], offsets[source_index, 0], length, 2)
            for source_index in range(source_count)
        ],
        axis=1,
    )
    win_imag = jnp.stack(
        [
            lax.dynamic_slice_in_dim(got_imag[:, source_index], offsets[source_index, 0], length, 2)
            for source_index in range(source_count)
        ],
        axis=1,
    )
    lifted_real = pupil_real * win_real - pupil_imag * win_imag
    lifted_imag = pupil_real * win_imag + pupil_imag * win_real
    half_real, half_imag = transform("smlcr,yr->smlyc", wide_rows, lifted_real, lifted_imag, 3, 1.0)
    layout = half_real.shape
    blocked = (layout[0], layout[1], groups, layout[2] // groups, layout[3])
    back_real, back_imag = (
        lax.all_to_all(half_real.reshape(blocked), "rows", split_axis=2, concat_axis=4, tiled=True),
        lax.all_to_all(half_imag.reshape(blocked), "rows", split_axis=2, concat_axis=4, tiled=True),
    )
    flat = (layout[0], layout[1], layout[2] // groups, layout[3] * groups)
    return right_product(back_real.reshape(flat), back_imag.reshape(flat), wide_cols, 1.0)


def spectral_updates(diff_real, diff_imag, pupil_real, pupil_imag, offsets, wide_cols, size_k):
    source_count = offsets.shape[0]
    groups = lax.axis_size("rows")
    col_real, col_imag = right_product(diff_real, diff_imag, wide_cols, -1.0)
    layout = col_real.shape
    blocked = (layout[0], layout[1], layout[2], groups, layout[3] // groups)
    got_real, got_imag = (
        lax.all_to_all(col_real.reshape(blocked), "rows", split_axis=3, concat_axis=2, tiled=True),
        lax.all_to_all(col_imag.reshape(blocked), "rows", split_axis=3, concat_axis=2, tiled=True),
    )
    flat = (layout[0], layout[1], layout[2] * groups, layout[3] // groups)
    full_real = got_real.reshape(flat)
    full_imag = got_imag.reshape(flat)
    delta_real, delta_imag = transform("smlyc,yk->smlck", wide_cols, full_real, full_imag, 4, -1.0)
    upd_real = pupil_real * delta_real + pupil_imag * delta_imag
    upd_imag = pupil_real * delta_imag - pupil_imag * delta_real
    blank = jnp.zeros((layout[0], layout[3] // groups, size_k), jnp.float32)
    placed_real = jnp.stack(
        [
            lax.dynamic_update_slice_in_dim(
                blank, upd_real[:, source_index], offsets[source_index, 0], 2
            )
            for source_index in range(source_count)
        ],
        axis=1,
    )
    placed_imag = jnp.stack(
        [
            lax.dynamic_update_slice_in_dim(
                blank, upd_imag[:, source_index], offsets[source_index, 0], 2
            )
            for source_index in range(source_count)
        ],
        axis=1,
    )
    return (
        lax.all_to_all(placed_real, "rows", split_axis=3, concat_axis=2, tiled=True),
        lax.all_to_all(placed_imag, "rows", split_axis=3, concat_axis=2, tiled=True),
    )


def add_window(target, incoming, start_col, length):
    current = lax.dynamic_slice_in_dim(target, start_col, length, 2)
    return lax.dynamic_update_slice_in_dim(
        target, current + jnp.swapaxes(incoming, 1, 2), start_col, 2
    )


def body(object_real, object_imag, pupil_real, pupil_imag, measured, source_mask, offsets):
    length = pupil_real.shape[1]
    size_k = object_real.shape[2]
    source_count = offsets.shape[0]
    wide_cols, wide_rows = dft_tables(length)
    spec_real, spec_imag = (object_real, object_imag)
    weights = source_mask[0].astype(jnp.float32)
    field_real, field_imag = forward_fields(
        spec_real, spec_imag, pupil_real, pupil_imag, offsets, wide_cols, wide_rows, length
    )
    powers = jnp.sum(field_real * field_real + field_imag * field_imag, axis=0)
    partial_sum = jnp.tensordot(weights, powers, axes=1)
    share = lax.psum_scatter(partial_sum, "mode", scatter_dimension=0, tiled=True)
    share_rows = share.shape[0]
    measured_share = lax.dynamic_slice_in_dim(
        measured[0], lax.axis_index("mode") * share_rows, share_rows, 0
    )
    ratio_share = measured_share / jnp.sqrt(share + FLOOR_TERM)
    ratios = lax.all_gather(ratio_share, "mode", axis=0, tiled=True)
    factor = (ratios - 1.0)[None, None] * weights[None, :, None, None]
    diff_real = field_real * factor
    diff_imag = field_imag * factor
    ret_real, ret_imag = spectral_updates(
        diff_real, diff_imag, pupil_real, pupil_imag, offsets, wide_cols, size_k
    )
    for source_index in range(source_count):
        start_col = offsets[source_index, 1]
        spec_real = add_window(spec_real, ret_real[:, source_index], start_col, length)
        spec_imag = add_window(spec_imag, ret_imag[:, source_index], start_col, length)
    return (spec_real, spec_imag)


RADIX = 4
ROW_TILE = 16


def split_pair(table):
    high = table.astype(ml_dtypes.bfloat16)
    low = (table - high.astype(np.float64)).astype(ml_dtypes.bfloat16)
    return np.stack([high, low])


def radix_tables(length):
    part = length // RADIX
    t = np.arange(RADIX)[:, None, None]
    r = np.arange(part)[None, :, None]
    s = np.arange(part)[None, None, :]
    angles = (r * (t + RADIX * s) % length) * (2.0 * np.pi / length)
    cos_t = np.cos(angles) / np.sqrt(length)
    sin_t = np.sin(angles) / np.sqrt(length)
    swap = lambda x: np.swapaxes(x, 1, 2)
    width = part // RADIX
    pieces = lambda x: x.reshape(RADIX, part, RADIX, width)
    beside = lambda x, y: np.stack([pieces(x), pieces(y)], axis=3).reshape(RADIX, part, 2 * part)
    columns = np.concatenate([beside(cos_t, sin_t), beside(-sin_t, cos_t)], axis=1)
    rows = np.concatenate([swap(cos_t), swap(sin_t)], axis=1)
    rows_back = np.concatenate([cos_t, sin_t], axis=1)
    return tuple(split_pair(table) for table in (columns, rows, rows_back))


def halves(x):
    high = x.astype(jnp.bfloat16)
    low = (x - high.astype(jnp.float32)).astype(jnp.bfloat16)
    return high, low


def dot(a, b):
    return jnp.dot(a, b, preferred_element_type=jnp.float32)


def dot_right(pair_ref, table_ref, t, turned=False):
    def product(a, b):
        dims = (((1,), (1 if turned else 0,)), ((), ()))
        return lax.dot_general(a, b, dims, preferred_element_type=jnp.float32)

    high, low = pair_ref[0], pair_ref[1]
    return (
        product(high, table_ref[0, t])
        + product(low, table_ref[0, t])
        + product(high, table_ref[1, t])
    )


def dot_left(table_ref, t, high, low):
    return dot(table_ref[0, t], high) + dot(table_ref[0, t], low) + dot(table_ref[1, t], high)


def over_rows(rows, step):
    def one(i, _):
        step(pl.ds(pl.multiple_of(i * ROW_TILE, ROW_TILE), ROW_TILE))
        return 0

    lax.fori_loop(0, rows // ROW_TILE, one, 0, unroll=2)


def lanes_of(x, slots):
    width = x.shape[1] // slots
    return [x[:, n * width : (n + 1) * width] for n in range(slots)]


def times_i(x):
    half = x.shape[1] // 2
    turned = pltpu.roll(x, half, 1)
    return jnp.where(lax.broadcasted_iota(jnp.int32, x.shape, 1) < half, -turned, turned)


def lit_offsets(params_ref, leds, nth):
    row, col, seen = jnp.int32(0), jnp.int32(0), jnp.int32(0)
    for led in range(leds):
        lit = params_ref[led] != 0
        take = jnp.logical_and(lit, seen == nth)
        row = jnp.where(take, params_ref[leds + 2 * led], row)
        col = jnp.where(take, params_ref[leds + 2 * led + 1], col)
        seen = seen + lit.astype(jnp.int32)
    return row, col


def place_of(params_ref, leds, levels=False):
    return params_ref[3 * leds + (1 if levels else 0)]


def pupil_send_kernel(leds, params_ref, real_ref, imag_ref, out_ref):
    length = real_ref.shape[1]
    part = length // RADIX
    for nth in range(out_ref.shape[1]):
        row, _ = lit_offsets(params_ref, leds, nth)
        for index, ref in enumerate((real_ref, imag_ref)):
            rolled = pltpu.roll(ref[...], lax.rem(row, length), 1)
            for q in range(RADIX):
                block = rolled[:, q * part : (q + 1) * part].T
                out_ref[q, nth, index] = block
                out_ref[q + RADIX, nth, index] = block


def window_pupil(leds, params_ref, stage_ref, pupil_ref):
    here = place_of(params_ref, leds)
    blocks, count, _, rows, width = stage_ref.shape
    length = blocks * width
    upper, first = here // RADIX, lax.rem(here, RADIX) * rows
    for nth in range(count):
        row, col = lit_offsets(params_ref, leds, nth)

        def tile(at):
            position = first + at.start + lax.broadcasted_iota(jnp.int32, (ROW_TILE, length), 0)
            owned = (position < row).astype(jnp.int32) == upper
            for index in range(2):
                whole = [stage_ref[d, nth, index, at] for d in range(blocks)]
                whole = pltpu.roll(jnp.concatenate(whole, axis=1), lax.rem(col, length), 1)
                pupil_ref[nth, index, at] = jnp.where(owned, whole, 0.0)

        over_rows(rows, tile)


def columns_kernel(leds, chunk, params_ref, real_ref, imag_ref, table_ref, *refs):
    pair_ref = refs[-1]
    if chunk == 0:
        stage_ref, amplitude_ref, out_ref, pupil_ref = refs[:-1]

        @pl.when(pl.program_id(0) == 0)
        def _():
            window_pupil(leds, params_ref, stage_ref, pupil_ref)
    else:
        pupil_ref, out_ref = refs[0], refs[-2]
    rows, size_k = real_ref.shape[1:]
    length = size_k // 2
    for nth in range(out_ref.shape[1]):
        _, col = lit_offsets(params_ref, leds, nth)

        def tile(at):
            wrapped = lax.broadcasted_iota(jnp.int32, (ROW_TILE, length), 1) < col
            p_r, p_i = pupil_ref[nth, 0, at], pupil_ref[nth, 1, at]
            w_r = jnp.where(wrapped, real_ref[0, at, length:], real_ref[0, at, :length])
            w_i = jnp.where(wrapped, imag_ref[0, at, length:], imag_ref[0, at, :length])
            x_r = lanes_of(p_r * w_r - p_i * w_i, RADIX)
            x_i = lanes_of(p_r * w_i + p_i * w_r, RADIX)
            sum_r, sum_i = x_r[0] + x_r[2], x_i[0] + x_i[2]
            dif_r, dif_i = x_r[0] - x_r[2], x_i[0] - x_i[2]
            odd_r, odd_i = x_r[1] + x_r[3], x_i[1] + x_i[3]
            rot_r, rot_i = x_i[3] - x_i[1], x_r[1] - x_r[3]
            if chunk == 0:
                pairs = ((sum_r + odd_r, sum_i + odd_i), (dif_r + rot_r, dif_i + rot_i))
            else:
                pairs = ((sum_r - odd_r, sum_i - odd_i), (dif_r - rot_r, dif_i - rot_i))
            for t, pair in enumerate(pairs):
                pair_ref[t, 0, at], pair_ref[t, 1, at] = halves(jnp.concatenate(pair, axis=1))

        over_rows(rows, tile)
        for t in range(2):
            z = dot_right(pair_ref[t], table_ref, t)
            for u, piece in enumerate(lanes_of(z, RADIX)):
                out_ref[RADIX * t + u, nth, 0, :rows] = piece
    if chunk == 0:
        out_ref[:, :, 0, rows:] = amplitude_ref[:, :, 0]


def rows_kernel(leds, waits, params_ref, table_ref, got_ref, *refs):
    total_ref, pair_ref = refs[-2:]
    groups, count, modes, _, width = got_ref.shape
    levels = total_ref.shape[0]
    refs = refs[waits:-2]
    field_ref, total_refs = refs[0], refs[1 : 1 + levels]
    part = field_ref.shape[1]
    for amplitude_ref in refs[1 + levels :]:
        amplitude_ref[...] = got_ref[:, :, :, part:]
    slots = [(nth, mode) for nth in range(count) for mode in range(modes)]

    def tile(at):
        for n, (nth, mode) in enumerate(slots):
            x = [got_ref[q, nth, mode, at] + got_ref[q + RADIX, nth, mode, at] for q in range(RADIX)]
            even, odd = x[0] + x[2], x[1] + x[3]
            dif, rot = x[0] - x[2], times_i(x[1] - x[3])
            for t, value in enumerate((even + odd, dif + rot, even - odd, dif - rot)):
                lanes = slice(n * width, (n + 1) * width)
                pair_ref[t, 0, at, lanes], pair_ref[t, 1, at, lanes] = halves(value)

    over_rows(part, tile)
    powers = []
    for t in range(RADIX):
        both = dot_left(table_ref, t, pair_ref[t, 0], pair_ref[t, 1])
        power = None
        for n, (a, b) in enumerate(
            zip(lanes_of(both[:part], len(slots)), lanes_of(both[part:], len(slots)))
        ):
            z = a + times_i(b)
            field_ref[t, :, n * width : (n + 1) * width] = z
            power = z * z if power is None else power + z * z
        powers.append(power + pltpu.roll(power, width // 2, 1))
    rows = total_ref.shape[2] // 2
    low = lax.broadcasted_iota(jnp.int32, (part, width), 1) < width // 2
    for pair in range(2):
        packed = jnp.where(low, powers[2 * pair], powers[2 * pair + 1])
        for d in range(groups):
            for z in range(levels):
                first = (d * levels + z) * rows
                total_ref[z, d, pair * rows : (pair + 1) * rows] = packed[first : first + rows]
    level = place_of(params_ref, leds, True)
    for k, ref in enumerate(total_refs):
        ref[...] = total_ref[lax.rem(level + k, levels)]


def rows_back_kernel(leds, params_ref, table_ref, field_ref, *refs):
    out_ref, factor_ref, turn_ref = refs[-3:]
    groups, count, modes, part, width = out_ref.shape
    levels = factor_ref.shape[0]
    level = place_of(params_ref, leds, True)
    for k, ref in enumerate(refs[:levels]):
        factor_ref[lax.rem(level + levels - k, levels)] = ref[...]
    slots = [(nth, mode) for nth in range(count) for mode in range(modes)]
    rows = factor_ref.shape[2] // 2
    low = lax.broadcasted_iota(jnp.int32, (part, width), 1) < width // 2
    for t in range(RADIX):
        pair = t // 2
        packed = jnp.concatenate(
            [
                factor_ref[z, d, pair * rows : (pair + 1) * rows]
                for d in range(groups)
                for z in range(levels)
            ],
            axis=0,
        )
        turned = pltpu.roll(packed, width // 2, 1)
        factor = jnp.where(low, packed, turned) if t % 2 == 0 else jnp.where(low, turned, packed)
        diff = jnp.concatenate([x * factor for x in lanes_of(field_ref[t], len(slots))], axis=1)
        both = dot_left(table_ref, t, *halves(diff))
        for n, (a, b) in enumerate(
            zip(lanes_of(both[:part], len(slots)), lanes_of(both[part:], len(slots)))
        ):
            turn_ref[t, :, n * width : (n + 1) * width] = a - times_i(b)

    def tile(at):
        for n, (nth, mode) in enumerate(slots):
            v = [turn_ref[t, at, n * width : (n + 1) * width] for t in range(RADIX)]
            even, odd = v[0] + v[2], v[1] + v[3]
            dif, rot = v[0] - v[2], times_i(v[1] - v[3])
            for q, value in enumerate((even + odd, dif - rot, even - odd, dif + rot)):
                out_ref[q, nth, mode, at] = value
                out_ref[q + RADIX, nth, mode, at] = value

    over_rows(part, tile)


def columns_back_kernel(leds, chunk, params_ref, real_ref, imag_ref, table_ref, *refs):
    got_ref, pupil_ref, _, out_r, out_i, pair_ref, turn_ref = refs
    count = got_ref.shape[1]
    rows, size_k = real_ref.shape[1:]
    length = size_k // 2
    for nth in range(count):
        for t in range(2):

            def split(at):
                z = [got_ref[RADIX * t + n, nth, 0, at] for n in range(RADIX)]
                pair_ref[t, 0, at], pair_ref[t, 1, at] = halves(jnp.concatenate(z, axis=1))

            over_rows(rows, split)
            turn_ref[nth, t] = dot_right(pair_ref[t], table_ref, t, True)

    def tile(at):
        totals = [[ref[0, at, :length], ref[0, at, length:]] for ref in (real_ref, imag_ref)]
        for nth in range(count):
            _, col = lit_offsets(params_ref, leds, nth)
            wrapped = lax.broadcasted_iota(jnp.int32, (ROW_TILE, length), 1) < col
            p_r, p_i = pupil_ref[nth, 0, at], pupil_ref[nth, 1, at]
            (a_r, a_i), (b_r, b_i) = [lanes_of(turn_ref[nth, t, at], 2) for t in range(2)]
            if chunk == 0:
                x_r = [a_r + b_r, a_r + b_i, a_r - b_r, a_r - b_i]
                x_i = [a_i + b_i, a_i - b_r, a_i - b_i, a_i + b_r]
            else:
                x_r = [a_r + b_r, -a_r - b_i, a_r - b_r, b_i - a_r]
                x_i = [a_i + b_i, b_r - a_i, a_i - b_i, -a_i - b_r]
            x_r, x_i = jnp.concatenate(x_r, axis=1), jnp.concatenate(x_i, axis=1)
            for total, delta in zip(totals, (p_r * x_r + p_i * x_i, p_r * x_i - p_i * x_r)):
                total[0] = total[0] + jnp.where(wrapped, 0.0, delta)
                total[1] = total[1] + jnp.where(wrapped, delta, 0.0)
        for out, total in zip((out_r, out_i), totals):
            out[0, at, :length] = total[0]
            out[0, at, length:] = total[1]

    over_rows(rows, tile)


SMEM_SPEC = pl.BlockSpec(memory_space=pltpu.SMEM)
ANY_SPEC = pl.BlockSpec(memory_space=pltpu.HBM)


def room(count):
    return pltpu.CompilerParams(vmem_limit_bytes=(16 + 16 * count) * 1024 * 1024)


CHUNKS = 2


def fixed(shape):
    zeros = (0,) * len(shape)
    return pl.BlockSpec(shape, lambda *_: zeros)


def one_mode(shape):
    before = len(shape) - 3
    block = shape[:before] + (1,) + shape[before + 1 :]
    return pl.BlockSpec(block, lambda i: (0,) * before + (i, 0, 0))


def kept(shape):
    zeros = (0,) * len(shape)
    return pl.BlockSpec(shape, lambda *_: zeros, pipeline_mode=pl.Buffered(1))


def cost(macs, *arrays):
    moved = sum(math.prod(a.shape) * a.dtype.itemsize for a in arrays)
    return pl.CostEstimate(flops=2 * macs, bytes_accessed=moved, transcendentals=0)


def shaped(shape):
    return jax.ShapeDtypeStruct(shape, jnp.float32)


def in_hbm(shape):
    return pltpu.HBM(shape, jnp.float32)


def exchange(blocks):
    got = lax.all_to_all(blocks, "rows", split_axis=0, concat_axis=0, tiled=True)
    return pltpu.with_memory_space_constraint(got, pltpu.HBM)


def around(levels, value_of):
    ring = range(levels)
    return [value_of(0)] + [
        lax.ppermute(value_of(k), "mode", [(z, (z + k) % levels) for z in ring]) for k in ring[1:]
    ]


def amplitude_kernel(leds, params_ref, measured_ref, out_ref):
    groups, rows, lanes = out_ref.shape
    width, length = measured_ref.shape[1:]
    columns = lanes // 2
    depth = rows // RADIX
    first = place_of(params_ref, leds, True) * rows

    def pick(x, y, turned):
        total = None
        for _ in range(3):
            x_part = x.astype(jnp.bfloat16)
            x = x - x_part.astype(jnp.float32)
            piece = dot(y, x_part) if turned else dot(x_part, y)
            total = piece if total is None else total + piece
        return total

    def ones_where(condition):
        return jnp.where(condition, 1.0, 0.0).astype(jnp.bfloat16)

    order = lax.broadcasted_iota(jnp.int32, (rows, width), 0)
    source = RADIX * (order % depth) + 2 * ((order // depth) % 2) + order // (2 * depth)
    taken = lax.broadcasted_iota(jnp.int32, (rows, width), 1) == source + first
    mine = pick(measured_ref[0], ones_where(taken), True)
    part = length // RADIX
    from_col = lax.broadcasted_iota(jnp.int32, (length, part), 0)
    to_col = lax.broadcasted_iota(jnp.int32, (length, part), 1)
    half = rows // 2
    for t in range(RADIX):
        chunk, side = t // 2, t % 2
        found = pick(mine, ones_where(from_col == RADIX * to_col + t), False)
        for u, piece in enumerate(lanes_of(found, RADIX)):
            out_ref[RADIX * side + u, chunk * half : (chunk + 1) * half] = jnp.concatenate(
                [piece[:half], piece[half:]], axis=1
            )


def fast_body(object_real, object_imag, pupil_real, pupil_imag, measured, source_mask, offsets):
    width, length = pupil_real.shape
    modes, local_rows, size_k = object_real.shape
    groups, levels = lax.axis_size("rows"), lax.axis_size("mode")
    part = length // RADIX
    leds = offsets.shape[0]
    tables = [jnp.asarray(table) for table in radix_tables(length)]
    position = jnp.stack([lax.axis_index("rows"), lax.axis_index("mode")]).astype(jnp.int32)
    params = jnp.concatenate([source_mask.reshape(-1), offsets.reshape(-1), position])
    spectrum = pl.BlockSpec((1, local_rows, size_k), lambda i: (i, 0, 0))

    def update(count):
        slots = count * modes
        dft_macs = 3 * slots * 2 * 4 * part * part * local_rows
        pupil_shape = (groups, count, 2, local_rows, width)
        block_shape = (groups, count, modes, local_rows, width)
        half_table = (2, RADIX // CHUNKS) + tables[0].shape[2:]

        def columns(chunk, pupil, others):
            extra = others.shape[1] // slots if chunk == 0 else 0
            out = in_hbm(block_shape[:3] + (local_rows + extra, width))
            whole = shaped((count, 2, local_rows, length))
            specs = [
                SMEM_SPEC,
                spectrum,
                spectrum,
                pl.BlockSpec(half_table, lambda i: (0, chunk, 0, 0), pipeline_mode=pl.Buffered(1)),
            ]
            outs, out_specs = (out,), (one_mode(out.shape),)
            if chunk == 0:
                others = others.reshape(groups, count, modes, extra, width)
                specs += [kept(pupil_shape), one_mode(others.shape)]
                outs, out_specs = outs + (whole,), out_specs + (fixed(whole.shape),)
            else:
                specs += [kept(whole.shape), ANY_SPEC]
            sent, *kept_pupil = pl.pallas_call(
                functools.partial(columns_kernel, leds, chunk),
                out_shape=outs,
                grid=(modes,),
                in_specs=specs,
                out_specs=out_specs,
                scratch_shapes=[pltpu.VMEM((2, 2, local_rows, 2 * part), jnp.bfloat16)],
                compiler_params=room(count),
                cost_estimate=cost(dft_macs, out, out, object_real, object_imag),
                name="columns",
            )(params, object_real, object_imag, tables[0], pupil, others)
            return exchange(sent), kept_pupil, pltpu.with_memory_space_constraint(sent, pltpu.HBM)

        def rows(got, waits):
            field = shaped((RADIX, part, slots * width))
            total = shaped((groups, 2 * part // groups // levels, width))
            extra = got.shape[3] - local_rows
            outs = (field,) + (total,) * levels
            if extra > 0:
                outs += (shaped((groups, count, modes, extra, width)),)
            return pl.pallas_call(
                functools.partial(rows_kernel, leds, len(waits)),
                out_shape=outs,
                grid=(1,),
                in_specs=[SMEM_SPEC, fixed(tables[1].shape)]
                + [fixed(got.shape)]
                + [ANY_SPEC] * len(waits),
                out_specs=tuple(fixed(out.shape) for out in outs),
                scratch_shapes=[
                    pltpu.VMEM((levels,) + total.shape, jnp.float32),
                    pltpu.VMEM((RADIX, 2, part, slots * width), jnp.bfloat16),
                ],
                compiler_params=room(count),
                cost_estimate=cost(dft_macs, got, field),
                name="rows",
            )(params, tables[1], got, *waits)

        def rows_back(field, factor):
            out = in_hbm(block_shape)
            sent = pl.pallas_call(
                functools.partial(rows_back_kernel, leds),
                out_shape=out,
                grid=(1,),
                in_specs=[SMEM_SPEC, fixed(tables[2].shape), fixed(field.shape)]
                + [fixed(factor[0].shape)] * levels,
                out_specs=fixed(block_shape),
                scratch_shapes=[
                    pltpu.VMEM((levels,) + factor[0].shape, jnp.float32),
                    pltpu.VMEM(field.shape, jnp.float32),
                ],
                compiler_params=room(count),
                cost_estimate=cost(dft_macs, out, field),
                name="rows_back",
            )(params, tables[2], field, *factor)
            return exchange(sent), pltpu.with_memory_space_constraint(sent, pltpu.HBM)

        def columns_back(chunk, pupil, got, current, wait):
            out = shaped(object_real.shape)
            return pl.pallas_call(
                functools.partial(columns_back_kernel, leds, chunk),
                out_shape=(out, out),
                grid=(modes,),
                in_specs=[
                    SMEM_SPEC,
                    spectrum,
                    spectrum,
                    pl.BlockSpec(
                        half_table, lambda i: (0, chunk, 0, 0), pipeline_mode=pl.Buffered(1)
                    ),
                    one_mode(block_shape),
                    kept(pupil.shape),
                    ANY_SPEC,
                ],
                out_specs=(spectrum, spectrum),
                scratch_shapes=[
                    pltpu.VMEM((2, 2, local_rows, 2 * part), jnp.bfloat16),
                    pltpu.VMEM((count, 2, local_rows, 2 * part), jnp.float32),
                ],
                input_output_aliases={1: 0, 2: 1} if chunk > 0 else {},
                compiler_params=room(count),
                cost_estimate=cost(dft_macs, got, pupil, out, out, out, out),
                name="columns_back",
            )(params, *current, tables[0], got, pupil, wait)

        def run(*_):
            amplitude = shaped((groups, width // levels, width))
            amplitude = pl.pallas_call(
                functools.partial(amplitude_kernel, leds),
                out_shape=amplitude,
                grid=(1,),
                in_specs=[SMEM_SPEC, fixed(measured.shape)],
                out_specs=fixed(amplitude.shape),
                compiler_params=room(count),
                cost_estimate=cost(3 * length * length * RADIX * 8, amplitude, measured),
                name="amplitude",
            )(params, measured)
            out = in_hbm(pupil_shape)
            sent = pl.pallas_call(
                functools.partial(pupil_send_kernel, leds),
                out_shape=out,
                grid=(1,),
                in_specs=[SMEM_SPEC] + [fixed(pupil_real.shape)] * 2,
                out_specs=fixed(pupil_shape),
                compiler_params=room(count),
                cost_estimate=cost(0, out, pupil_real, pupil_imag),
                name="pupil_send",
            )(params, pupil_real, pupil_imag)
            got, (pupil,), wait = columns(0, exchange(sent), amplitude)
            more, _, wait = columns(1, pupil, wait)
            got = [got, more]
            back, waits = [], [wait]
            for chunk in range(CHUNKS):
                field, *totals = rows(got[chunk], waits)
                if chunk == 0:
                    mine = totals.pop().reshape(groups, width // levels, width)
                share = sum(around(levels, lambda k: totals[k]))
                deep = share.shape[1]
                ratio = mine[:, chunk * deep : (chunk + 1) * deep] / jnp.sqrt(share + FLOOR_TERM)
                factor = around(levels, lambda k: ratio - 1.0)
                blocks, wait = rows_back(field, factor)
                back.append(blocks)
                waits = [wait]
            current = (object_real, object_imag)
            for chunk in range(CHUNKS):
                current = columns_back(chunk, pupil, back[chunk], current, wait)
            return tuple(current)

        return run

    lit = jnp.sum((source_mask[0] != 0).astype(jnp.int32))
    most = max(leds - 1, 1)
    if most == 1:
        return update(1)()
    return lax.switch(jnp.clip(lit - 1, 0, most - 1), [update(n + 1) for n in range(most)])


def fits_fast(mesh, object_shape, pupil_shape, leds):
    groups, levels = mesh.shape["rows"], mesh.shape["mode"]
    length, size_k = pupil_shape[1], object_shape[2]
    modes, local_rows, width = object_shape[0] // levels, size_k // groups, length // groups
    amplitude_rows = width // levels
    return (
        size_k == 2 * length
        and groups == 2 * RADIX
        and levels == RADIX
        and local_rows % 256 == 0
        and width % 128 == 0
        and all(amplitude_rows % (8 * modes * n) == 0 for n in range(1, max(leds, 2)))
    )


def solution(mesh):
    in_specs = (
        P("mode", "rows", None),
        P("mode", "rows", None),
        P("rows", None),
        P("rows", None),
        P(None, "rows", None),
        P(),
        P(),
    )
    out_specs = (P("mode", "rows", None), P("mode", "rows", None))

    def chosen(object_real, object_imag, pupil_real, *others):
        fast = fits_fast(mesh, object_real.shape, pupil_real.shape, others[-1].shape[0])
        mapped = jax.shard_map(
            fast_body if fast else body,
            mesh=mesh,
            in_specs=in_specs,
            out_specs=out_specs,
            check_vma=False,
        )
        return mapped(object_real, object_imag, pupil_real, *others)

    return chosen
```

```python
import functools
import math

import jax
import jax.numpy as jnp
import ml_dtypes
import numpy as np
from jax import lax
from jax.experimental import pallas as pl
from jax.experimental.pallas import tpu as pltpu
from jax.sharding import PartitionSpec as P

FLOOR_TERM = 0.5
HIGHEST_PREC = lax.Precision.HIGHEST


def dft_tables(length):
    indices = jnp.arange(length, dtype=jnp.int32)
    phases = indices[:, None] * indices[None, :] % length
    angles = phases.astype(jnp.float32) * (2.0 * math.pi / length)
    scale_factor = 1.0 / math.sqrt(length)
    cos_table = jnp.cos(angles) * scale_factor
    sin_table = jnp.sin(angles) * scale_factor
    return (
        jnp.concatenate([cos_table, sin_table], axis=1),
        jnp.concatenate([cos_table, sin_table], axis=0),
    )


def transform(form, table, real_part, imag_part, axis, direction_sign):
    result = jnp.einsum(form, jnp.stack([real_part, imag_part]), table, precision=HIGHEST_PREC)
    length = result.shape[axis] // 2
    with_cos = lax.slice_in_dim(result, 0, length, axis=axis)
    with_sin = lax.slice_in_dim(result, length, 2 * length, axis=axis)
    return (with_cos[0] - direction_sign * with_sin[1], with_cos[1] + direction_sign * with_sin[0])


def right_product(real_part, imag_part, wide_cols, direction_sign):
    return transform("smlck,kj->smlcj", wide_cols, real_part, imag_part, 4, direction_sign)


def forward_fields(
    part_real, part_imag, pupil_real, pupil_imag, offsets, wide_cols, wide_rows, length
):
    source_count = offsets.shape[0]
    groups = lax.axis_size("rows")
    crop_real = jnp.stack(
        [
            lax.dynamic_slice_in_dim(part_real, offsets[source_index, 1], length, 2)
            for source_index in range(source_count)
        ],
        axis=1,
    )
    crop_imag = jnp.stack(
        [
            lax.dynamic_slice_in_dim(part_imag, offsets[source_index, 1], length, 2)
            for source_index in range(source_count)
        ],
        axis=1,
    )
    got_real, got_imag = (
        lax.all_to_all(
            jnp.swapaxes(crop_real, 2, 3), "rows", split_axis=2, concat_axis=3, tiled=True
        ),
        lax.all_to_all(
            jnp.swapaxes(crop_imag, 2, 3), "rows", split_axis=2, concat_axis=3, tiled=True
        ),
    )
    win_real = jnp.stack(
        [
            lax.dynamic_slice_in_dim(got_real[:, source_index], offsets[source_index, 0], length, 2)
            for source_index in range(source_count)
        ],
        axis=1,
    )
    win_imag = jnp.stack(
        [
            lax.dynamic_slice_in_dim(got_imag[:, source_index], offsets[source_index, 0], length, 2)
            for source_index in range(source_count)
        ],
        axis=1,
    )
    lifted_real = pupil_real * win_real - pupil_imag * win_imag
    lifted_imag = pupil_real * win_imag + pupil_imag * win_real
    half_real, half_imag = transform("smlcr,yr->smlyc", wide_rows, lifted_real, lifted_imag, 3, 1.0)
    layout = half_real.shape
    blocked = (layout[0], layout[1], groups, layout[2] // groups, layout[3])
    back_real, back_imag = (
        lax.all_to_all(half_real.reshape(blocked), "rows", split_axis=2, concat_axis=4, tiled=True),
        lax.all_to_all(half_imag.reshape(blocked), "rows", split_axis=2, concat_axis=4, tiled=True),
    )
    flat = (layout[0], layout[1], layout[2] // groups, layout[3] * groups)
    return right_product(back_real.reshape(flat), back_imag.reshape(flat), wide_cols, 1.0)


def spectral_updates(diff_real, diff_imag, pupil_real, pupil_imag, offsets, wide_cols, size_k):
    source_count = offsets.shape[0]
    groups = lax.axis_size("rows")
    col_real, col_imag = right_product(diff_real, diff_imag, wide_cols, -1.0)
    layout = col_real.shape
    blocked = (layout[0], layout[1], layout[2], groups, layout[3] // groups)
    got_real, got_imag = (
        lax.all_to_all(col_real.reshape(blocked), "rows", split_axis=3, concat_axis=2, tiled=True),
        lax.all_to_all(col_imag.reshape(blocked), "rows", split_axis=3, concat_axis=2, tiled=True),
    )
    flat = (layout[0], layout[1], layout[2] * groups, layout[3] // groups)
    full_real = got_real.reshape(flat)
    full_imag = got_imag.reshape(flat)
    delta_real, delta_imag = transform("smlyc,yk->smlck", wide_cols, full_real, full_imag, 4, -1.0)
    upd_real = pupil_real * delta_real + pupil_imag * delta_imag
    upd_imag = pupil_real * delta_imag - pupil_imag * delta_real
    blank = jnp.zeros((layout[0], layout[3] // groups, size_k), jnp.float32)
    placed_real = jnp.stack(
        [
            lax.dynamic_update_slice_in_dim(
                blank, upd_real[:, source_index], offsets[source_index, 0], 2
            )
            for source_index in range(source_count)
        ],
        axis=1,
    )
    placed_imag = jnp.stack(
        [
            lax.dynamic_update_slice_in_dim(
                blank, upd_imag[:, source_index], offsets[source_index, 0], 2
            )
            for source_index in range(source_count)
        ],
        axis=1,
    )
    return (
        lax.all_to_all(placed_real, "rows", split_axis=3, concat_axis=2, tiled=True),
        lax.all_to_all(placed_imag, "rows", split_axis=3, concat_axis=2, tiled=True),
    )


def add_window(target, incoming, start_col, length):
    current = lax.dynamic_slice_in_dim(target, start_col, length, 2)
    return lax.dynamic_update_slice_in_dim(
        target, current + jnp.swapaxes(incoming, 1, 2), start_col, 2
    )


def body(object_real, object_imag, pupil_real, pupil_imag, measured, source_mask, offsets):
    length = pupil_real.shape[1]
    size_k = object_real.shape[2]
    source_count = offsets.shape[0]
    wide_cols, wide_rows = dft_tables(length)
    spec_real, spec_imag = (object_real, object_imag)
    weights = source_mask[0].astype(jnp.float32)
    field_real, field_imag = forward_fields(
        spec_real, spec_imag, pupil_real, pupil_imag, offsets, wide_cols, wide_rows, length
    )
    powers = jnp.sum(field_real * field_real + field_imag * field_imag, axis=0)
    partial_sum = jnp.tensordot(weights, powers, axes=1)
    share = lax.psum_scatter(partial_sum, "mode", scatter_dimension=0, tiled=True)
    share_rows = share.shape[0]
    measured_share = lax.dynamic_slice_in_dim(
        measured[0], lax.axis_index("mode") * share_rows, share_rows, 0
    )
    ratio_share = measured_share / jnp.sqrt(share + FLOOR_TERM)
    ratios = lax.all_gather(ratio_share, "mode", axis=0, tiled=True)
    factor = (ratios - 1.0)[None, None] * weights[None, :, None, None]
    diff_real = field_real * factor
    diff_imag = field_imag * factor
    ret_real, ret_imag = spectral_updates(
        diff_real, diff_imag, pupil_real, pupil_imag, offsets, wide_cols, size_k
    )
    for source_index in range(source_count):
        start_col = offsets[source_index, 1]
        spec_real = add_window(spec_real, ret_real[:, source_index], start_col, length)
        spec_imag = add_window(spec_imag, ret_imag[:, source_index], start_col, length)
    return (spec_real, spec_imag)


RADIX = 4
ROW_TILE = 16


def split_pair(table):
    high = table.astype(ml_dtypes.bfloat16)
    low = (table - high.astype(np.float64)).astype(ml_dtypes.bfloat16)
    return np.stack([high, low])


def radix_tables(length):
    part = length // RADIX
    t = np.arange(RADIX)[:, None, None]
    r = np.arange(part)[None, :, None]
    s = np.arange(part)[None, None, :]
    angles = (r * (t + RADIX * s) % length) * (2.0 * np.pi / length)
    cos_t = np.cos(angles) / np.sqrt(length)
    sin_t = np.sin(angles) / np.sqrt(length)
    swap = lambda x: np.swapaxes(x, 1, 2)
    width = part // RADIX
    pieces = lambda x: x.reshape(RADIX, part, RADIX, width)
    beside = lambda x, y: np.stack([pieces(x), pieces(y)], axis=3).reshape(RADIX, part, 2 * part)
    columns = np.concatenate([beside(cos_t, sin_t), beside(-sin_t, cos_t)], axis=1)
    rows = np.concatenate([swap(cos_t), swap(sin_t)], axis=1)
    rows_back = np.concatenate([cos_t, sin_t], axis=1)
    return tuple(split_pair(table) for table in (columns, rows, rows_back))


def halves(x):
    high = x.astype(jnp.bfloat16)
    low = (x - high.astype(jnp.float32)).astype(jnp.bfloat16)
    return high, low


def dot(a, b):
    return jnp.dot(a, b, preferred_element_type=jnp.float32)


def dot_right(pair_ref, table_ref, t, turned=False):
    def product(a, b):
        dims = (((1,), (1 if turned else 0,)), ((), ()))
        return lax.dot_general(a, b, dims, preferred_element_type=jnp.float32)

    high, low = pair_ref[0], pair_ref[1]
    return (
        product(high, table_ref[0, t])
        + product(low, table_ref[0, t])
        + product(high, table_ref[1, t])
    )


def dot_left(table_ref, t, high, low):
    return dot(table_ref[0, t], high) + dot(table_ref[0, t], low) + dot(table_ref[1, t], high)


def over_rows(rows, step):
    def one(i, _):
        step(pl.ds(pl.multiple_of(i * ROW_TILE, ROW_TILE), ROW_TILE))
        return 0

    lax.fori_loop(0, rows // ROW_TILE, one, 0, unroll=2)


def lanes_of(x, slots):
    width = x.shape[1] // slots
    return [x[:, n * width : (n + 1) * width] for n in range(slots)]


def times_i(x):
    half = x.shape[1] // 2
    turned = pltpu.roll(x, half, 1)
    return jnp.where(lax.broadcasted_iota(jnp.int32, x.shape, 1) < half, -turned, turned)


def lit_offsets(params_ref, leds, nth):
    row, col, seen = jnp.int32(0), jnp.int32(0), jnp.int32(0)
    for led in range(leds):
        lit = params_ref[led] != 0
        take = jnp.logical_and(lit, seen == nth)
        row = jnp.where(take, params_ref[leds + 2 * led], row)
        col = jnp.where(take, params_ref[leds + 2 * led + 1], col)
        seen = seen + lit.astype(jnp.int32)
    return row, col


def place_of(params_ref, leds, levels=False):
    return params_ref[3 * leds + (1 if levels else 0)]


def pupil_send_kernel(leds, params_ref, real_ref, imag_ref, out_ref):
    length = real_ref.shape[1]
    part = length // RADIX
    for nth in range(out_ref.shape[1]):
        row, _ = lit_offsets(params_ref, leds, nth)
        for index, ref in enumerate((real_ref, imag_ref)):
            rolled = pltpu.roll(ref[...], lax.rem(row, length), 1)
            for q in range(RADIX):
                block = rolled[:, q * part : (q + 1) * part].T
                out_ref[q, nth, index] = block
                out_ref[q + RADIX, nth, index] = block


def window_pupil(leds, params_ref, stage_ref, pupil_ref):
    here = place_of(params_ref, leds)
    blocks, count, _, rows, width = stage_ref.shape
    length = blocks * width
    upper, first = here // RADIX, lax.rem(here, RADIX) * rows
    for nth in range(count):
        row, col = lit_offsets(params_ref, leds, nth)

        def tile(at):
            position = first + at.start + lax.broadcasted_iota(jnp.int32, (ROW_TILE, length), 0)
            owned = (position < row).astype(jnp.int32) == upper
            for index in range(2):
                whole = [stage_ref[d, nth, index, at] for d in range(blocks)]
                whole = pltpu.roll(jnp.concatenate(whole, axis=1), lax.rem(col, length), 1)
                pupil_ref[nth, index, at] = jnp.where(owned, whole, 0.0)

        over_rows(rows, tile)


def columns_kernel(leds, chunk, params_ref, real_ref, imag_ref, table_ref, *refs):
    pair_ref = refs[-1]
    if chunk == 0:
        stage_ref, amplitude_ref, out_ref, pupil_ref = refs[:-1]

        @pl.when(pl.program_id(0) == 0)
        def _():
            window_pupil(leds, params_ref, stage_ref, pupil_ref)
    else:
        pupil_ref, out_ref = refs[0], refs[-2]
    rows, size_k = real_ref.shape[1:]
    length = size_k // 2
    for nth in range(out_ref.shape[1]):
        _, col = lit_offsets(params_ref, leds, nth)

        def tile(at):
            wrapped = lax.broadcasted_iota(jnp.int32, (ROW_TILE, length), 1) < col
            p_r, p_i = pupil_ref[nth, 0, at], pupil_ref[nth, 1, at]
            w_r = jnp.where(wrapped, real_ref[0, at, length:], real_ref[0, at, :length])
            w_i = jnp.where(wrapped, imag_ref[0, at, length:], imag_ref[0, at, :length])
            x_r = lanes_of(p_r * w_r - p_i * w_i, RADIX)
            x_i = lanes_of(p_r * w_i + p_i * w_r, RADIX)
            sum_r, sum_i = x_r[0] + x_r[2], x_i[0] + x_i[2]
            dif_r, dif_i = x_r[0] - x_r[2], x_i[0] - x_i[2]
            odd_r, odd_i = x_r[1] + x_r[3], x_i[1] + x_i[3]
            rot_r, rot_i = x_i[3] - x_i[1], x_r[1] - x_r[3]
            if chunk == 0:
                pairs = ((sum_r + odd_r, sum_i + odd_i), (dif_r + rot_r, dif_i + rot_i))
            else:
                pairs = ((sum_r - odd_r, sum_i - odd_i), (dif_r - rot_r, dif_i - rot_i))
            for t, pair in enumerate(pairs):
                pair_ref[t, 0, at], pair_ref[t, 1, at] = halves(jnp.concatenate(pair, axis=1))

        over_rows(rows, tile)
        for t in range(2):
            z = dot_right(pair_ref[t], table_ref, t)
            for u, piece in enumerate(lanes_of(z, RADIX)):
                out_ref[RADIX * t + u, nth, 0, :rows] = piece
    if chunk == 0:
        out_ref[:, :, 0, rows:] = amplitude_ref[:, :, 0]


def rows_kernel(leds, waits, params_ref, table_ref, got_ref, *refs):
    total_ref, pair_ref = refs[-2:]
    groups, count, modes, _, width = got_ref.shape
    levels = total_ref.shape[0]
    refs = refs[waits:-2]
    field_ref, total_refs = refs[0], refs[1 : 1 + levels]
    part = field_ref.shape[1]
    for amplitude_ref in refs[1 + levels :]:
        amplitude_ref[...] = got_ref[:, :, :, part:]
    slots = [(nth, mode) for nth in range(count) for mode in range(modes)]

    def tile(at):
        for n, (nth, mode) in enumerate(slots):
            x = [got_ref[q, nth, mode, at] + got_ref[q + RADIX, nth, mode, at] for q in range(RADIX)]
            even, odd = x[0] + x[2], x[1] + x[3]
            dif, rot = x[0] - x[2], times_i(x[1] - x[3])
            for t, value in enumerate((even + odd, dif + rot, even - odd, dif - rot)):
                lanes = slice(n * width, (n + 1) * width)
                pair_ref[t, 0, at, lanes], pair_ref[t, 1, at, lanes] = halves(value)

    over_rows(part, tile)
    powers = []
    for t in range(RADIX):
        both = dot_left(table_ref, t, pair_ref[t, 0], pair_ref[t, 1])
        power = None
        for n, (a, b) in enumerate(
            zip(lanes_of(both[:part], len(slots)), lanes_of(both[part:], len(slots)))
        ):
            z = a + times_i(b)
            field_ref[t, :, n * width : (n + 1) * width] = z
            power = z * z if power is None else power + z * z
        powers.append(power + pltpu.roll(power, width // 2, 1))
    rows = total_ref.shape[2] // 2
    low = lax.broadcasted_iota(jnp.int32, (part, width), 1) < width // 2
    for pair in range(2):
        packed = jnp.where(low, powers[2 * pair], powers[2 * pair + 1])
        for d in range(groups):
            for z in range(levels):
                first = (d * levels + z) * rows
                total_ref[z, d, pair * rows : (pair + 1) * rows] = packed[first : first + rows]
    level = place_of(params_ref, leds, True)
    for k, ref in enumerate(total_refs):
        ref[...] = total_ref[lax.rem(level + k, levels)]


def rows_back_kernel(leds, params_ref, table_ref, field_ref, *refs):
    out_ref, factor_ref, turn_ref = refs[-3:]
    groups, count, modes, part, width = out_ref.shape
    levels = factor_ref.shape[0]
    level = place_of(params_ref, leds, True)
    for k, ref in enumerate(refs[:levels]):
        factor_ref[lax.rem(level + levels - k, levels)] = ref[...]
    slots = [(nth, mode) for nth in range(count) for mode in range(modes)]
    rows = factor_ref.shape[2] // 2
    low = lax.broadcasted_iota(jnp.int32, (part, width), 1) < width // 2
    for t in range(RADIX):
        pair = t // 2
        packed = jnp.concatenate(
            [
                factor_ref[z, d, pair * rows : (pair + 1) * rows]
                for d in range(groups)
                for z in range(levels)
            ],
            axis=0,
        )
        turned = pltpu.roll(packed, width // 2, 1)
        factor = jnp.where(low, packed, turned) if t % 2 == 0 else jnp.where(low, turned, packed)
        diff = jnp.concatenate([x * factor for x in lanes_of(field_ref[t], len(slots))], axis=1)
        both = dot_left(table_ref, t, *halves(diff))
        for n, (a, b) in enumerate(
            zip(lanes_of(both[:part], len(slots)), lanes_of(both[part:], len(slots)))
        ):
            turn_ref[t, :, n * width : (n + 1) * width] = a - times_i(b)

    def tile(at):
        for n, (nth, mode) in enumerate(slots):
            v = [turn_ref[t, at, n * width : (n + 1) * width] for t in range(RADIX)]
            even, odd = v[0] + v[2], v[1] + v[3]
            dif, rot = v[0] - v[2], times_i(v[1] - v[3])
            for q, value in enumerate((even + odd, dif - rot, even - odd, dif + rot)):
                out_ref[q, nth, mode, at] = value
                out_ref[q + RADIX, nth, mode, at] = value

    over_rows(part, tile)


def columns_back_kernel(leds, chunk, params_ref, real_ref, imag_ref, table_ref, *refs):
    got_ref, pupil_ref, _, out_r, out_i, pair_ref, turn_ref = refs
    count = got_ref.shape[1]
    rows, size_k = real_ref.shape[1:]
    length = size_k // 2
    for nth in range(count):
        for t in range(2):

            def split(at):
                z = [got_ref[RADIX * t + n, nth, 0, at] for n in range(RADIX)]
                pair_ref[t, 0, at], pair_ref[t, 1, at] = halves(jnp.concatenate(z, axis=1))

            over_rows(rows, split)
            turn_ref[nth, t] = dot_right(pair_ref[t], table_ref, t, True)

    def tile(at):
        totals = [[ref[0, at, :length], ref[0, at, length:]] for ref in (real_ref, imag_ref)]
        for nth in range(count):
            _, col = lit_offsets(params_ref, leds, nth)
            wrapped = lax.broadcasted_iota(jnp.int32, (ROW_TILE, length), 1) < col
            p_r, p_i = pupil_ref[nth, 0, at], pupil_ref[nth, 1, at]
            (a_r, a_i), (b_r, b_i) = [lanes_of(turn_ref[nth, t, at], 2) for t in range(2)]
            if chunk == 0:
                x_r = [a_r + b_r, a_r + b_i, a_r - b_r, a_r - b_i]
                x_i = [a_i + b_i, a_i - b_r, a_i - b_i, a_i + b_r]
            else:
                x_r = [a_r + b_r, -a_r - b_i, a_r - b_r, b_i - a_r]
                x_i = [a_i + b_i, b_r - a_i, a_i - b_i, -a_i - b_r]
            x_r, x_i = jnp.concatenate(x_r, axis=1), jnp.concatenate(x_i, axis=1)
            for total, delta in zip(totals, (p_r * x_r + p_i * x_i, p_r * x_i - p_i * x_r)):
                total[0] = total[0] + jnp.where(wrapped, 0.0, delta)
                total[1] = total[1] + jnp.where(wrapped, delta, 0.0)
        for out, total in zip((out_r, out_i), totals):
            out[0, at, :length] = total[0]
            out[0, at, length:] = total[1]

    over_rows(rows, tile)


SMEM_SPEC = pl.BlockSpec(memory_space=pltpu.SMEM)
ANY_SPEC = pl.BlockSpec(memory_space=pltpu.HBM)


def room(count):
    return pltpu.CompilerParams(vmem_limit_bytes=(16 + 16 * count) * 1024 * 1024)


CHUNKS = 2


def fixed(shape):
    zeros = (0,) * len(shape)
    return pl.BlockSpec(shape, lambda *_: zeros)


def one_mode(shape):
    before = len(shape) - 3
    block = shape[:before] + (1,) + shape[before + 1 :]
    return pl.BlockSpec(block, lambda i: (0,) * before + (i, 0, 0))


def kept(shape):
    zeros = (0,) * len(shape)
    return pl.BlockSpec(shape, lambda *_: zeros, pipeline_mode=pl.Buffered(1))


def cost(macs, *arrays):
    moved = sum(math.prod(a.shape) * a.dtype.itemsize for a in arrays)
    return pl.CostEstimate(flops=2 * macs, bytes_accessed=moved, transcendentals=0)


def shaped(shape):
    return jax.ShapeDtypeStruct(shape, jnp.float32)


def in_hbm(shape):
    return pltpu.HBM(shape, jnp.float32)


def exchange(blocks):
    return lax.all_to_all(blocks, "rows", split_axis=0, concat_axis=0, tiled=True)


def in_place(x):
    return pltpu.with_memory_space_constraint(x, pltpu.HBM)


def around(levels, value_of):
    ring = range(levels)
    return [value_of(0)] + [
        lax.ppermute(value_of(k), "mode", [(z, (z + k) % levels) for z in ring]) for k in ring[1:]
    ]


def amplitude_kernel(leds, params_ref, measured_ref, out_ref):
    groups, rows, lanes = out_ref.shape
    width, length = measured_ref.shape[1:]
    columns = lanes // 2
    depth = rows // RADIX
    first = place_of(params_ref, leds, True) * rows

    def pick(x, y, turned):
        total = None
        for _ in range(3):
            x_part = x.astype(jnp.bfloat16)
            x = x - x_part.astype(jnp.float32)
            piece = dot(y, x_part) if turned else dot(x_part, y)
            total = piece if total is None else total + piece
        return total

    def ones_where(condition):
        return jnp.where(condition, 1.0, 0.0).astype(jnp.bfloat16)

    order = lax.broadcasted_iota(jnp.int32, (rows, width), 0)
    source = RADIX * (order % depth) + 2 * ((order // depth) % 2) + order // (2 * depth)
    taken = lax.broadcasted_iota(jnp.int32, (rows, width), 1) == source + first
    mine = pick(measured_ref[0], ones_where(taken), True)
    part = length // RADIX
    from_col = lax.broadcasted_iota(jnp.int32, (length, part), 0)
    to_col = lax.broadcasted_iota(jnp.int32, (length, part), 1)
    half = rows // 2
    for t in range(RADIX):
        chunk, side = t // 2, t % 2
        found = pick(mine, ones_where(from_col == RADIX * to_col + t), False)
        for u, piece in enumerate(lanes_of(found, RADIX)):
            out_ref[RADIX * side + u, chunk * half : (chunk + 1) * half] = jnp.concatenate(
                [piece[:half], piece[half:]], axis=1
            )


def fast_body(object_real, object_imag, pupil_real, pupil_imag, measured, source_mask, offsets):
    width, length = pupil_real.shape
    modes, local_rows, size_k = object_real.shape
    groups, levels = lax.axis_size("rows"), lax.axis_size("mode")
    part = length // RADIX
    leds = offsets.shape[0]
    tables = [in_place(jnp.asarray(table)) for table in radix_tables(length)]
    position = jnp.stack([lax.axis_index("rows"), lax.axis_index("mode")]).astype(jnp.int32)
    params = jnp.concatenate([source_mask.reshape(-1), offsets.reshape(-1), position])
    spectrum = pl.BlockSpec((1, local_rows, size_k), lambda i: (i, 0, 0))

    def update(count):
        slots = count * modes
        dft_macs = 3 * slots * 2 * 4 * part * part * local_rows
        pupil_shape = (groups, count, 2, local_rows, width)
        block_shape = (groups, count, modes, local_rows, width)
        half_table = (2, RADIX // CHUNKS) + tables[0].shape[2:]

        def columns(chunk, pupil, others):
            extra = others.shape[1] // slots if chunk == 0 else 0
            out = in_hbm(block_shape[:3] + (local_rows + extra, width))
            whole = shaped((count, 2, local_rows, length))
            specs = [
                SMEM_SPEC,
                spectrum,
                spectrum,
                pl.BlockSpec(half_table, lambda i: (0, chunk, 0, 0), pipeline_mode=pl.Buffered(1)),
            ]
            outs, out_specs = (out,), (one_mode(out.shape),)
            if chunk == 0:
                others = others.reshape(groups, count, modes, extra, width)
                specs += [kept(pupil_shape), one_mode(others.shape)]
                outs, out_specs = outs + (whole,), out_specs + (fixed(whole.shape),)
            else:
                specs += [kept(whole.shape), ANY_SPEC]
            sent, *kept_pupil = pl.pallas_call(
                functools.partial(columns_kernel, leds, chunk),
                out_shape=outs,
                grid=(modes,),
                in_specs=specs,
                out_specs=out_specs,
                scratch_shapes=[pltpu.VMEM((2, 2, local_rows, 2 * part), jnp.bfloat16)],
                compiler_params=room(count),
                cost_estimate=cost(dft_macs, out, out, object_real, object_imag),
                name="columns",
            )(params, object_real, object_imag, tables[0], pupil, others)
            return in_place(exchange(sent)), kept_pupil, in_place(sent)

        def rows(got, waits):
            field = shaped((RADIX, part, slots * width))
            total = shaped((groups, 2 * part // groups // levels, width))
            extra = got.shape[3] - local_rows
            outs = (field,) + (total,) * levels
            if extra > 0:
                outs += (shaped((groups, count, modes, extra, width)),)
            return pl.pallas_call(
                functools.partial(rows_kernel, leds, len(waits)),
                out_shape=outs,
                grid=(1,),
                in_specs=[SMEM_SPEC, fixed(tables[1].shape)]
                + [fixed(got.shape)]
                + [ANY_SPEC] * len(waits),
                out_specs=tuple(fixed(out.shape) for out in outs),
                scratch_shapes=[
                    pltpu.VMEM((levels,) + total.shape, jnp.float32),
                    pltpu.VMEM((RADIX, 2, part, slots * width), jnp.bfloat16),
                ],
                compiler_params=room(count),
                cost_estimate=cost(dft_macs, got, field),
                name="rows",
            )(params, tables[1], got, *waits)

        def rows_back(field, factor):
            out = in_hbm(block_shape)
            sent = pl.pallas_call(
                functools.partial(rows_back_kernel, leds),
                out_shape=out,
                grid=(1,),
                in_specs=[SMEM_SPEC, fixed(tables[2].shape), fixed(field.shape)]
                + [fixed(factor[0].shape)] * levels,
                out_specs=fixed(block_shape),
                scratch_shapes=[
                    pltpu.VMEM((levels,) + factor[0].shape, jnp.float32),
                    pltpu.VMEM(field.shape, jnp.float32),
                ],
                compiler_params=room(count),
                cost_estimate=cost(dft_macs, out, field),
                name="rows_back",
            )(params, tables[2], field, *factor)
            return in_place(exchange(sent)), in_place(sent)

        def columns_back(chunk, pupil, got, current, wait):
            out = shaped(object_real.shape)
            return pl.pallas_call(
                functools.partial(columns_back_kernel, leds, chunk),
                out_shape=(out, out),
                grid=(modes,),
                in_specs=[
                    SMEM_SPEC,
                    spectrum,
                    spectrum,
                    pl.BlockSpec(
                        half_table, lambda i: (0, chunk, 0, 0), pipeline_mode=pl.Buffered(1)
                    ),
                    one_mode(block_shape),
                    kept(pupil.shape),
                    ANY_SPEC,
                ],
                out_specs=(spectrum, spectrum),
                scratch_shapes=[
                    pltpu.VMEM((2, 2, local_rows, 2 * part), jnp.bfloat16),
                    pltpu.VMEM((count, 2, local_rows, 2 * part), jnp.float32),
                ],
                input_output_aliases={1: 0, 2: 1} if chunk > 0 else {},
                compiler_params=room(count),
                cost_estimate=cost(dft_macs, got, pupil, out, out, out, out),
                name="columns_back",
            )(params, *current, tables[0], got, pupil, wait)

        def run(*_):
            amplitude = shaped((groups, width // levels, width))
            amplitude = pl.pallas_call(
                functools.partial(amplitude_kernel, leds),
                out_shape=amplitude,
                grid=(1,),
                in_specs=[SMEM_SPEC, fixed(measured.shape)],
                out_specs=fixed(amplitude.shape),
                compiler_params=room(count),
                cost_estimate=cost(3 * length * length * RADIX * 8, amplitude, measured),
                name="amplitude",
            )(params, measured)
            out = in_hbm(pupil_shape)
            sent = pl.pallas_call(
                functools.partial(pupil_send_kernel, leds),
                out_shape=out,
                grid=(1,),
                in_specs=[SMEM_SPEC] + [fixed(pupil_real.shape)] * 2,
                out_specs=fixed(pupil_shape),
                compiler_params=room(count),
                cost_estimate=cost(0, out, pupil_real, pupil_imag),
                name="pupil_send",
            )(params, pupil_real, pupil_imag)
            got, (pupil,), wait = columns(0, exchange(sent), amplitude)
            more, _, wait = columns(1, pupil, wait)
            got = [got, more]
            back, waits = [], [wait]
            for chunk in range(CHUNKS):
                field, *totals = rows(got[chunk], waits)
                if chunk == 0:
                    mine = totals.pop().reshape(groups, width // levels, width)
                share = sum(around(levels, lambda k: totals[k]))
                deep = share.shape[1]
                ratio = mine[:, chunk * deep : (chunk + 1) * deep] / jnp.sqrt(share + FLOOR_TERM)
                factor = around(levels, lambda k: ratio - 1.0)
                blocks, wait = rows_back(field, factor)
                back.append(blocks)
                waits = [wait]
            current = (object_real, object_imag)
            for chunk in range(CHUNKS):
                current = columns_back(chunk, pupil, back[chunk], current, wait)
            return tuple(current)

        return run

    lit = jnp.sum((source_mask[0] != 0).astype(jnp.int32))
    most = max(leds - 1, 1)
    if most == 1:
        return update(1)()
    return lax.switch(jnp.clip(lit - 1, 0, most - 1), [update(n + 1) for n in range(most)])


def fits_fast(mesh, object_shape, pupil_shape, leds):
    groups, levels = mesh.shape["rows"], mesh.shape["mode"]
    length, size_k = pupil_shape[1], object_shape[2]
    modes, local_rows, width = object_shape[0] // levels, size_k // groups, length // groups
    amplitude_rows = width // levels
    return (
        size_k == 2 * length
        and groups == 2 * RADIX
        and levels == RADIX
        and local_rows % 256 == 0
        and width % 128 == 0
        and all(amplitude_rows % (8 * modes * n) == 0 for n in range(1, max(leds, 2)))
    )


def solution(mesh):
    in_specs = (
        P("mode", "rows", None),
        P("mode", "rows", None),
        P("rows", None),
        P("rows", None),
        P(None, "rows", None),
        P(),
        P(),
    )
    out_specs = (P("mode", "rows", None), P("mode", "rows", None))

    def chosen(object_real, object_imag, pupil_real, *others):
        fast = fits_fast(mesh, object_real.shape, pupil_real.shape, others[-1].shape[0])
        mapped = jax.shard_map(
            fast_body if fast else body,
            mesh=mesh,
            in_specs=in_specs,
            out_specs=out_specs,
            check_vma=False,
        )
        return mapped(object_real, object_imag, pupil_real, *others)

    return chosen
```
